256 devices in a mesh: pool: 8 (over z), ctx: 4 (over x), head: 8 (over y, core).
Axes of the slice: x: 4, y: 4, z: 8, core: 2. Of those that a mesh axis runs over, the one named last changes fastest.
Arguments:
- query_nope: bfloat16 [5120, 4096], P(('pool', 'ctx'), 'head'), may hold values from -6 to 6
- query_rope: bfloat16 [5120, 2048], P(('pool', 'ctx'), 'head'), may hold values from -100 to 100
- new_latent: bfloat16 [2560, 1152], P(('pool', 'ctx')), may hold values from -6 to 6
- cache_pool: bfloat16 [512, 73728], P(('pool', 'ctx')), may hold values from -6 to 6
- hit_holder: int32 [8, 64], replicated, may hold values from 0 to 31, as said below
- hit_block: int32 [8, 64], replicated, may hold values from 0 to 15
- prior_blocks: int32 [8, 2], replicated, may hold values from 1 to 63, as said below
- new_counts: int32 [8, 2], replicated, may hold values from 1 to 480, 640 in all within a row
- key_absorb: bfloat16 [32, 128, 512], P('head'), may hold values from -0.5 to 0.5
- value_absorb: bfloat16 [32, 512, 128], P('head'), may hold values from -1 to 1
- out_weight: bfloat16 [4096, 7168], P('head'), may hold values from -0.375 to 0.375
Outputs:
- layer_output: bfloat16 [5120, 7168], P(('pool', 'ctx'), 'head')
The draws below stay inside these ranges and needn't reach their ends.
Inputs may be any that keep to these rules, and one draw needn't show every extreme that they name: `hit_holder`: row g lists group g's cached blocks, request 0's first; among the listed blocks of a group each holder appears at most 2 times, and in some group every holder appears exactly 2 times; entries past a group's blocks are ignored. `prior_blocks`: A group's blocks, the sum of its row, number at most 64, and exactly that in some group.
All inputs are finite; a program needn't handle non-finite values.
Results may differ from the reference program's by a relative error of at most 0.0086.
Values may be sent and summed in bfloat16 or wider, within the bound.
No kernel may reach another device: no remote copies, remote signals or barrier semaphores. Data moves between devices by JAX's collectives and lax.ppermute only.
A program may use at most 128 MiB of HBM per device.

```python
import math
import jax
import jax.numpy as jnp
import numpy as np
from jax import lax

D = 7168
KV_RANK = 512
ROPE = 64
QK_NOPE = 128
VD = 128
H = 32
BLK = 128
CAP = 2
REQ = 2
HOLD = 16
TOK_DEV = 160
WIDE = 576
GROUPS = 8
HOLDERS = 32
MAXB = 64
NEWG = 640
TOKENS = 5120
N_CTX = 4


def draw_new_latent(key, part):
    key = jax.random.fold_in(key, 7)
    base = jnp.clip(jax.random.normal(key, (TOKENS, WIDE), jnp.float32), -6.0, 6.0)
    return base.reshape(TOKENS // 2, 2 * WIDE).astype(jnp.bfloat16)


def draw_query_rope(key, part):
    key = jax.random.fold_in(key, 9)
    base = jnp.clip(jax.random.normal(key, (TOKENS, H, ROPE), jnp.float32), -6.0, 6.0)
    return base.reshape(TOKENS, H * ROPE).astype(jnp.bfloat16)


def shuffle_row(row_key):
    base = jnp.arange(HOLDERS * CAP, dtype=jnp.int32) // CAP
    return jax.random.permutation(row_key, base)


def draw_hit_holder(key, part):
    key = jax.random.fold_in(key, 11)
    row_keys = jax.random.split(key, GROUPS)
    return jax.vmap(shuffle_row)(row_keys)


def draw_prior_blocks(key, part):
    key = jax.random.fold_in(key, 13)
    block_total = jax.random.randint(jax.random.fold_in(key, 1), (GROUPS,), 2, MAXB + 1)
    fullest = jax.random.randint(jax.random.fold_in(key, 2), (), 0, GROUPS)
    group_ids = jnp.arange(GROUPS, dtype=jnp.int32)
    block_total = jnp.where(group_ids == fullest, MAXB, block_total)
    first_share = jax.random.randint(jax.random.fold_in(key, 3), (GROUPS,), 1, block_total)
    first_share = jnp.where(group_ids == fullest, MAXB - 1, first_share)
    return jnp.stack([first_share, block_total - first_share], axis=1).astype(jnp.int32)


def with_ends(result, rng, least, high):
    longest = result.shape.index(max(result.shape))
    spots = []
    for shift in (0, 1):
        where = [jax.random.randint(jax.random.fold_in(rng, axis), (), 0, length) for axis, length in enumerate(result.shape)]
        where[longest] = (where[longest] + shift) % result.shape[longest]
        spots.append(tuple(where))
    return result.at[spots[0]].set(least).at[spots[1]].set(high)


def steps_of(stream_key, extent, cuts, smallest, high):
    gain = 1.0
    for dim, parts in cuts:
        draws = jax.random.uniform(jax.random.fold_in(jax.random.fold_in(stream_key, 6), dim), (parts,), jnp.float32, smallest / len(cuts), high / len(cuts))
        gain = gain * jnp.repeat(jnp.exp(draws), extent[dim] // parts).reshape((-1,) + (1,) * (len(extent) - 1 - dim))
    return gain


def split_up(number_of, total, most, slope):
    loads = [(1 << 20) // math.isqrt(grade ** slope) + 1 for grade in range(2, number_of + 1)]
    surplus, holding = total - most - (number_of - 1), [1] * (number_of - 1)
    while surplus > 0:
        movable = [i for i in range(number_of - 1) if holding[i] < most]
        whole, budget = sum([loads[i] for i in movable]), surplus
        for i in movable:
            more = min(most - holding[i], max(1, budget * loads[i] // whole), surplus)
            holding[i] = holding[i] + more
            surplus = surplus - more
    return np.array([most] + holding)


def uneven(rng, amount, total, limit, lean):
    if amount == 2:
        one = jax.random.randint(rng, (), max(1, total - limit), min(limit, total - 1) + 1)
        return jnp.stack([one, total - one])
    lengths = jnp.asarray(split_up(amount, total, limit, lean), jnp.int32)
    pairs = (amount - 1) // 2
    donor, taker = lengths[1:1 + 2 * pairs:2], lengths[2:2 + 2 * pairs:2]
    margin = jnp.minimum(donor - 1, limit - taker)
    moved = jax.random.randint(jax.random.fold_in(rng, 1), (pairs,), 0, 1 << 20) % (margin + 1)
    lengths = lengths.at[1:1 + 2 * pairs:2].set(donor - moved).at[2:2 + 2 * pairs:2].set(taker + moved)
    return lengths[jax.random.permutation(jax.random.fold_in(rng, 2), amount)]


def noise(rng, shape, scale, limit, pieces=(), kind=jnp.bfloat16):
    values = scale * jax.random.normal(rng, shape, jnp.float32)
    if pieces:
        values = values * steps_of(rng, shape, pieces, -0.22, 0.18)
    return jnp.clip(values, -limit, limit).astype(kind)


def setup_inputs(seed: int = 0) -> dict:
    seeds = jax.random.split(jax.random.key(seed), 12)
    return {
        "query_nope": noise(seeds[0], (TOKENS, H * QK_NOPE), 1.0, 6.0, ((0, 32), (1, 8))),
        "query_rope": draw_query_rope(jax.random.fold_in(seeds[11], 71), 0),
        "new_latent": draw_new_latent(jax.random.fold_in(seeds[11], 71), 0),
        "cache_pool": noise(seeds[3], (HOLDERS * HOLD, BLK * WIDE), 1.0, 6.0, ((0, 32),)),
        "hit_holder": draw_hit_holder(jax.random.fold_in(seeds[11], 71), 0),
        "hit_block": with_ends(jax.random.randint(seeds[5], (GROUPS, MAXB), 0, HOLD), jax.random.fold_in(seeds[5], 1), 0, HOLD - 1).astype(jnp.int32),
        "prior_blocks": draw_prior_blocks(jax.random.fold_in(seeds[11], 71), 0),
        "new_counts": jax.vmap(lambda own: uneven(own, REQ, TOK_DEV * N_CTX, TOK_DEV * N_CTX * 3 // 4, 0))(jax.random.split(seeds[7], GROUPS)).reshape((GROUPS, REQ)).astype(jnp.int32),
        "key_absorb": noise(seeds[8], (H, QK_NOPE, KV_RANK), QK_NOPE ** -0.5, 0.5, ((0, 8),)),
        "value_absorb": noise(seeds[9], (H, KV_RANK, VD), (KV_RANK // 16) ** -0.5, 1.0, ((0, 8),)),
        "out_weight": noise(seeds[10], (H * VD, D), (H * VD // 16) ** -0.5, 0.375, ((0, 8),)),
    }


def request_of(position, counts):
    bounds = jnp.cumsum(counts)
    return jnp.sum((position[:, None] >= bounds[None, :-1]).astype(jnp.int32), axis=1)


def reference(query_nope, query_rope, new_latent, cache_pool, hit_holder, hit_block, prior_blocks, new_counts, key_absorb, value_absorb, out_weight):
    score_scale = (QK_NOPE + ROPE) ** -0.5
    nope_rows = query_nope.reshape(TOKENS, H, QK_NOPE).astype(jnp.float32)
    latent_query = jnp.einsum("thn,hnr->thr", nope_rows, key_absorb.astype(jnp.float32)).astype(jnp.bfloat16)
    queries = jnp.concatenate([latent_query, query_rope.reshape(TOKENS, H, ROPE)], axis=2)
    new_rows = new_latent.reshape(TOKENS, WIDE)
    blocks = cache_pool.reshape(HOLDERS * HOLD, BLK, WIDE)
    group_outputs = []
    for group in range(GROUPS):
        entries = jnp.arange(MAXB, dtype=jnp.int32)
        bounds = jnp.cumsum(prior_blocks[group])
        live_entry = entries < bounds[-1]
        entry_req = request_of(entries, prior_blocks[group])
        rows_index = (hit_holder[group] * HOLD + hit_block[group]).astype(jnp.int32)
        cached = blocks[rows_index].reshape(MAXB * BLK, WIDE)
        new_keys = new_rows[group * NEWG:(group + 1) * NEWG]
        all_keys = jnp.concatenate([cached, new_keys], axis=0)
        positions = jnp.arange(NEWG, dtype=jnp.int32)
        tok_req = request_of(positions, new_counts[group])
        cached_vis = (entry_req[None, :, None] == tok_req[:, None, None]) & live_entry[None, :, None]
        cached_vis = jnp.broadcast_to(cached_vis, (NEWG, MAXB, BLK)).reshape(NEWG, MAXB * BLK)
        new_vis = (tok_req[None, :] == tok_req[:, None]) & (positions[None, :] <= positions[:, None])
        visible = jnp.concatenate([cached_vis, new_vis], axis=1)
        group_queries = queries[group * NEWG:(group + 1) * NEWG].transpose(1, 0, 2)

        def one_head(pair):
            head_query, head_value = pair
            scores = jnp.dot(head_query, all_keys.T, preferred_element_type=jnp.float32) * score_scale
            scores = jnp.where(visible, scores, -jnp.inf)
            largest = jnp.max(scores, axis=1, keepdims=True)
            exp_scores = jnp.exp(scores - largest)
            weights = (exp_scores / jnp.sum(exp_scores, axis=1, keepdims=True)).astype(jnp.bfloat16)
            latent_out = jnp.dot(weights, all_keys[:, :KV_RANK], preferred_element_type=jnp.float32).astype(jnp.bfloat16)
            return jnp.dot(latent_out, head_value, preferred_element_type=jnp.float32).astype(jnp.bfloat16)

        head_outputs = lax.map(one_head, (group_queries, value_absorb))
        merged = head_outputs.transpose(1, 0, 2).reshape(NEWG, H * VD)
        group_outputs.append(jnp.dot(merged, out_weight, preferred_element_type=jnp.float32).astype(jnp.bfloat16))
    return jnp.concatenate(group_outputs, axis=0)
```

```python
from functools import partial

import jax
import jax.numpy as jnp
from jax import lax
from jax.experimental import pallas as pl
from jax.experimental.pallas import tpu as pltpu
from jax.sharding import PartitionSpec as P

KV_RANK = 512
ROPE = 64
QK_NOPE = 128
VD = 128
BLK = 128
PAIRS = BLK // 2
WIDE2 = 2 * (KV_RANK + ROPE)
HEADS = 4
TOK = 160
TQ = 80
CK = 512
SLOTS = 16
KEYS = SLOTS * BLK
KW = 768
BIG = 2.0**100
SCALE = (QK_NOPE + ROPE) ** (-0.5)
LOG2E = 1.4426950408889634
BF = jnp.bfloat16
F32 = jnp.float32
STAT = 16


def iota(shape, dim):
    return lax.broadcasted_iota(jnp.int32, shape, dim)


def pick_kernel(ids, cache_ref, holder_ref, block_ref, prior_ref, out_ref):
    me = ids[0] * 4 + ids[1]
    core = ids[2] % 2
    lane = iota((8, 64), 1)
    count = prior_ref[:, 0:1] + prior_ref[:, 1:2]
    match = (holder_ref[...] == me) & (lane < count)
    first = jnp.min(jnp.where(match, lane, 1000), axis=1, keepdims=True)
    last = jnp.max(jnp.where(match, lane, -1), axis=1, keepdims=True)
    wanted = jnp.where(core == 0, first, jnp.where(last > first, last, -2))
    chosen = match & (lane == wanted)
    index = jnp.sum(jnp.where(chosen, block_ref[...] + 1, 0), axis=1, keepdims=True) - 1
    spread = (iota((128, 8), 0) // 16 == iota((128, 8), 1)).astype(BF)
    rows_index = jnp.dot(
        spread,
        jnp.broadcast_to(index.astype(F32), (8, 256)).astype(BF),
        preferred_element_type=F32,
    )
    row = iota((128, 256), 0)
    col = iota((128, 256), 1)
    onehot = ((col // 16 == row % 16) & ((col % 16).astype(F32) == rows_index)).astype(BF)
    stacked = jnp.concatenate(
        [cache_ref[:, p * WIDE2 : (p + 1) * WIDE2] for p in range(16)], axis=0
    )
    out = jnp.dot(onehot, stacked, preferred_element_type=F32).astype(BF)
    for g in range(8):
        out_ref[g] = out[g * 16 : (g + 1) * 16]


def align(rows):
    n = rows.shape[0]
    low = iota((n, 128), 1) < 64
    tile = [rows[:, j * 128 : (j + 1) * 128] for j in range(9)]
    flip = {
        j: jnp.concatenate([tile[j][:, 64:], tile[j][:, :64]], axis=1) for j in range(4, 9)
    }
    even = tile[:4] + [jnp.where(low, tile[4], flip[4])]
    odd = [jnp.where(low, flip[4 + j], flip[5 + j]) for j in range(4)]
    odd = odd + [jnp.where(low, flip[8], tile[8])]
    return even, odd


def attend_kernel(
    ids, holder, prior, counts,
    q_ref, ka_ref, va_ref, nl_ref,
    a0, am, ap, ax, ay, b0, bm, bp, bx, by,
    out_ref,
    kc, kb, kn, qb, acc, mx, sm, pos, seen, meta, sem,
):
    step = pl.program_id(0)
    group = ids[0]
    ctx = ids[1]
    core = ids[2] % 2
    n0 = counts[group, 0]

    @pl.when(step == 0)
    def _():
        for i in range(SLOTS):
            pos[i] = -1
        for i in range(8):
            seen[i] = 0
        own = prior[group, 0]
        total = own + prior[group, 1]

        def entry(e, carry):
            filled, mine = carry
            where = holder[group, e]
            hit = where % 4 == ctx
            p = where // 4

            @pl.when(hit)
            def _():
                s = seen[p]
                seen[p] = s + 1
                pos[p * 2 + s] = filled

            add = hit.astype(jnp.int32)
            return filled + add, mine + jnp.where(e < own, add, 0)

        filled, mine = lax.fori_loop(0, total, entry, (jnp.int32(0), jnp.int32(0)))
        meta[0] = mine * BLK
        meta[1] = filled * BLK
        for i in range(SLOTS):
            dead = pos[i] < 0

            @pl.when(dead)
            def _():
                pos[i] = filled

            filled = filled + dead.astype(jnp.int32)
        for p in range(8):
            for same, pieces in ((True, (a0, am, ap, ax, ay)), (False, (b0, bm, bp, bx, by))):
                slot = core if same else 1 - core
                to = pos[p * 2 + slot]
                sources = [pieces[0].at[p], pieces[1].at[p], pieces[2].at[p]]
                sources.append(pieces[3].at[p] if p < 4 else pieces[4].at[p - 4])
                for i, source in enumerate(sources):
                    pltpu.make_async_copy(source, kc.at[to, i], sem).start()

        def mark(base, n, keys0, keys1):
            row = iota((n, 128), 0) + base
            lane = iota((n, 128), 1)
            miss0 = (lane == 0) & jnp.logical_not(keys0(row))
            miss1 = (lane == 1) & jnp.logical_not(keys1(row))
            return jnp.where(miss0 | miss1, -BIG, 0.0).astype(BF)

        def place(ref, at, n, rows_):
            for j, value in enumerate(rows_):
                ref[pl.ds(at, n), j * 128 : (j + 1) * 128] = value

        even, odd = align(nl_ref[...])
        kn[...] = jnp.zeros(kn.shape, BF)
        place(kn, 0, 80, even)
        place(kn, 128, 80, odd)

        def new_position(row):
            return ctx * TOK + 2 * (row % 128) + row // 128

        kn[:, 640:768] = mark(
            0, 256, lambda r: new_position(r) < n0, lambda r: new_position(r) >= n0
        )
        kb[KEYS:, :] = jnp.zeros((CK, KW), BF)
        for i in range(SLOTS + CK // BLK):
            kb[i * BLK : (i + 1) * BLK, 640:768] = mark(
                i * BLK, BLK,
                lambda r: r < meta[0],
                lambda r: (r >= meta[0]) & (r < meta[1]),
            )
        pltpu.make_async_copy(kc, kc, sem).wait()

        def shape_up(i, _):
            for piece in range(4):
                even, odd = align(kc[i, piece])
                at = i * BLK + piece * 32
                place(kb, pl.multiple_of(at, 32), 16, even)
                place(kb, pl.multiple_of(at + 16, 16), 16, odd)
            return 0

        lax.fori_loop(0, SLOTS, shape_up, 0)

    turn = jnp.where(step == 0, 0, jnp.where(step == 1, 3, jnp.where(step == 2, 1, 2)))
    owner = (ctx + turn) % 4
    lane16 = iota((16, 128), 1)
    stats = jnp.zeros((16, 128), F32)
    rows = HEADS * TQ
    for half in range(TOK // TQ):
        t0 = owner * TOK + half * TQ
        part = q_ref[0, half * TQ : (half + 1) * TQ, :]
        lane = iota((TQ, 128), 1)
        token = iota((TQ, 128), 0) + t0
        flags = jnp.where(
            ((lane == 0) & (token < n0)) | ((lane == 1) & (token >= n0)), 1.0, 0.0
        ).astype(BF)
        for j in range(HEADS):
            at = slice(j * TQ, (j + 1) * TQ)
            qb[at, 0:512] = jnp.dot(
                part[:, j * 128 : (j + 1) * 128], ka_ref[j], preferred_element_type=F32
            ).astype(BF)
            rope = part[:, 512 + (j // 2) * 128 : 640 + (j // 2) * 128]
            keep = lane < 64 if j % 2 == 0 else lane >= 64
            qb[at, 512:640] = jnp.where(keep, rope, jnp.zeros_like(rope))
            qb[at, 640:768] = flags
        mx[...] = jnp.full(mx.shape, -BIG, F32)
        sm[...] = jnp.zeros(sm.shape, F32)
        acc[...] = jnp.zeros(acc.shape, F32)

        def fold(scores, at, values):
            before = mx[at, :]
            top = jnp.maximum(before, jnp.max(scores, axis=1, keepdims=True))
            keep = jnp.exp2((before - top) * (SCALE * LOG2E))
            weight = jnp.exp2((scores - top[:, 0:1]) * (SCALE * LOG2E))
            sm[at, :] = sm[at, :] * keep + jnp.sum(weight, axis=1, keepdims=True)
            mx[at, :] = top
            acc[at, :] = acc[at, :] * keep[:, 0:1] + jnp.dot(
                weight.astype(BF), values, preferred_element_type=F32
            )

        def product(at, keys):
            return lax.dot_general(
                qb[at, :], keys, (((1,), (1,)), ((), ())), preferred_element_type=F32
            )

        parts = [slice(i * rows // 2, (i + 1) * rows // 2) for i in range(2)]

        @pl.when(t0 + TQ > ctx * TOK)
        def _():
            for at in parts:
                n = at.stop - at.start
                key = iota((n, 256), 1)
                position = ctx * TOK + 2 * (key % 128) + key // 128
                here = t0 + (iota((n, 256), 0) % TQ)
                seen_keys = (position <= here) & (key % 128 < 80)
                scores = jnp.where(seen_keys, product(at, kn[...]), -BIG)
                fold(scores, at, kn[:, 0:512])

        low = jnp.where(t0 < n0, 0, meta[0])
        high = jnp.where(t0 + TQ > n0, meta[1], meta[0])

        def chunk(i, _):
            at_key = pl.multiple_of(low + i * CK, BLK)
            keys = kb[pl.ds(at_key, CK), :]
            for at in parts:
                fold(product(at, keys), at, kb[pl.ds(at_key, CK), 0:512])
            return 0

        lax.fori_loop(0, (high - low + CK - 1) // CK, chunk, 0)

        for j in range(HEADS):
            at = slice(j * TQ, (j + 1) * TQ)
            mass = sm[at, :]
            none = mass == 0.0
            safe = jnp.where(none, 1.0, mass)
            lse = jnp.where(none, -BIG, mx[at, :] * SCALE + jnp.log(safe))
            latent = (acc[at, :] / safe[:, 0:1]).astype(BF)
            head = jnp.dot(latent, va_ref[j], preferred_element_type=F32).astype(BF)
            out_ref[0, half * TQ : (half + 1) * TQ, j * 128 : (j + 1) * 128] = head
            one = lse.astype(BF).astype(F32)
            two = (lse - one).astype(BF).astype(F32)
            three = lse - one - two
            for k in range(TQ // 16):
                base = 12 * (half * (TQ // 16) + k) + 3 * j
                cut = slice(k * 16, (k + 1) * 16)
                for i, value in enumerate((one, two, three)):
                    stats = jnp.where(lane16 == base + i, value[cut], stats)
    out_ref[0, TOK : TOK + STAT, 0:128] = stats.astype(BF)
    out_ref[0, TOK : TOK + STAT, 128:512] = jnp.zeros((STAT, 384), BF)


def merge(got_ref):
    lane_in = iota((128, 512), 0)
    lane_head = iota((128, 512), 1) // 128
    outs = []
    stats = jnp.concatenate([got_ref[c, TOK : TOK + STAT, 0:128] for c in range(4)], axis=0)
    for k in range(TOK // 16):
        pickup = ((lane_in >= 12 * k + 3 * lane_head) & (lane_in < 12 * k + 3 * lane_head + 3))
        lse = jnp.dot(stats, pickup.astype(BF), preferred_element_type=F32)
        lse = [lse[c * 16 : (c + 1) * 16] for c in range(4)]
        top = jnp.maximum(jnp.maximum(lse[0], lse[1]), jnp.maximum(lse[2], lse[3]))
        weight = [jnp.exp(v - top) for v in lse]
        total = weight[0] + weight[1] + weight[2] + weight[3]
        mixed = sum(
            weight[c] * got_ref[c, k * 16 : (k + 1) * 16, :].astype(F32) for c in range(4)
        )
        outs.append((mixed / total).astype(BF))
    return outs


def away_kernel(ids, got_ref, w_ref, head_ref, out_ref, held):
    @pl.when(pl.program_id(0) == 0)
    def _():
        for k, value in enumerate(merge(got_ref)):
            held[k * 16 : (k + 1) * 16, :] = value
        head_ref[...] = held[...]

    out_ref[0] = jnp.dot(held[...], w_ref[...], preferred_element_type=F32).astype(BF)


def home_kernel(ids, head_ref, w_ref, out_ref):
    out_ref[0] = jnp.dot(head_ref[...], w_ref[...], preferred_element_type=F32).astype(BF)


def shift(value, axis, by, size):
    return lax.ppermute(value, axis, [(i, (i + by) % size) for i in range(size)])


def swap_core(value):
    return lax.ppermute(value, "head", [(i, i ^ 1) for i in range(8)])


def local(
    query_nope, query_rope, new_latent, cache_pool, hit_holder, hit_block,
    prior_blocks, new_counts, key_absorb, value_absorb, out_weight,
):
    ids = jnp.stack(
        [lax.axis_index("pool"), lax.axis_index("ctx"), lax.axis_index("head")]
    ).astype(jnp.int32)

    quarter = 16 * WIDE2
    picked = pl.pallas_call(
        pick_kernel,
        grid_spec=pltpu.PrefetchScalarGridSpec(
            num_scalar_prefetch=1,
            grid=(1,),
            in_specs=[
                pl.BlockSpec((16, quarter), lambda i, ids: (0, ids[2] // 2)),
                pl.BlockSpec((8, 64), lambda i, ids: (0, 0)),
                pl.BlockSpec((8, 64), lambda i, ids: (0, 0)),
                pl.BlockSpec((8, 2), lambda i, ids: (0, 0)),
            ],
            out_specs=pl.BlockSpec((8, 16, WIDE2), lambda i, ids: (0, 0, 0)),
        ),
        out_shape=jax.ShapeDtypeStruct((8, 16, WIDE2), BF),
        name="pick_blocks",
    )(ids, cache_pool, hit_holder, hit_block, prior_blocks)

    a0 = lax.all_to_all(picked, "pool", split_axis=0, concat_axis=0, tiled=True)

    queries = jnp.concatenate([query_nope, query_rope], axis=1)
    qm = shift(queries, "ctx", 1, 4)
    qp = shift(queries, "ctx", -1, 4)
    qx = shift(qm[:80], "ctx", 1, 4)
    qy = shift(qp[80:], "ctx", -1, 4)
    all_q = jnp.concatenate([queries, qm, qp, qx, qy], axis=0).reshape(4, TOK, 768)

    am = shift(a0, "head", 2, 8)
    ap = shift(a0, "head", -2, 8)
    b0 = swap_core(a0)
    ax = shift(am[:4], "head", 2, 8)
    ay = shift(ap[4:], "head", -2, 8)
    bm = swap_core(am)
    bp = swap_core(ap)
    bx = swap_core(ax)
    by = swap_core(ay)

    def turn_of(i, ids):
        turn = jnp.where(i == 0, 0, jnp.where(i == 1, 3, jnp.where(i == 2, 1, 2)))
        return (lax.rem(ids[1] + turn, 4), 0, 0)

    whole = lambda *shape: pl.BlockSpec(shape, lambda i, *_: (0,) * len(shape))
    partial_out = pl.pallas_call(
        attend_kernel,
        grid_spec=pltpu.PrefetchScalarGridSpec(
            num_scalar_prefetch=4,
            grid=(4,),
            in_specs=[
                pl.BlockSpec((1, TOK, 768), lambda i, *_: (i, 0, 0)),
                whole(HEADS, 128, 512),
                whole(HEADS, 512, 128),
                whole(80, WIDE2),
            ]
            + [pl.BlockSpec(memory_space=pl.ANY)] * 10,
            out_specs=pl.BlockSpec((1, TOK + STAT, 512), lambda i, ids, *_: turn_of(i, ids)),
            scratch_shapes=[
                pltpu.VMEM((SLOTS, 4, 16, WIDE2), BF),
                pltpu.VMEM((KEYS + CK, KW), BF),
                pltpu.VMEM((256, KW), BF),
                pltpu.VMEM((HEADS * TQ, KW), BF),
                pltpu.VMEM((HEADS * TQ, 512), F32),
                pltpu.VMEM((HEADS * TQ, 128), F32),
                pltpu.VMEM((HEADS * TQ, 128), F32),
                pltpu.SMEM((SLOTS,), jnp.int32),
                pltpu.SMEM((8,), jnp.int32),
                pltpu.SMEM((2,), jnp.int32),
                pltpu.SemaphoreType.DMA,
            ],
        ),
        out_shape=jax.ShapeDtypeStruct((4, TOK + STAT, 512), BF),
        compiler_params=pltpu.CompilerParams(vmem_limit_bytes=48 * 2**20),
        name="attend",
    )(
        ids, hit_holder, prior_blocks, new_counts,
        all_q, key_absorb, value_absorb, new_latent,
        a0, am, ap, ax, ay, b0, bm, bp, bx, by,
    )

    got = lax.all_to_all(partial_out, "ctx", split_axis=0, concat_axis=0, tiled=True)

    heads, away = pl.pallas_call(
        away_kernel,
        grid_spec=pltpu.PrefetchScalarGridSpec(
            num_scalar_prefetch=1,
            grid=(4,),
            in_specs=[
                whole(4, TOK + STAT, 512),
                pl.BlockSpec((512, 896), lambda i, ids: (0, 2 * i + 1 - ids[2] % 2)),
            ],
            out_specs=[whole(TOK, 512), pl.BlockSpec((1, TOK, 896), lambda i, ids: (i, 0, 0))],
            scratch_shapes=[pltpu.VMEM((TOK, 512), BF)],
        ),
        out_shape=[
            jax.ShapeDtypeStruct((TOK, 512), BF),
            jax.ShapeDtypeStruct((4, TOK, 896), BF),
        ],
        name="project_away",
    )(ids, got, out_weight)
    arrived = swap_core(away)
    home = pl.pallas_call(
        home_kernel,
        grid_spec=pltpu.PrefetchScalarGridSpec(
            num_scalar_prefetch=1,
            grid=(4,),
            in_specs=[
                whole(TOK, 512),
                pl.BlockSpec((512, 896), lambda i, ids: (0, 2 * i + ids[2] % 2)),
            ],
            out_specs=pl.BlockSpec((1, TOK, 896), lambda i, ids: (i, 0, 0)),
        ),
        out_shape=jax.ShapeDtypeStruct((4, TOK, 896), BF),
        name="project_home",
    )(ids, heads, out_weight)
    summed = (home.astype(F32) + arrived.astype(F32)).astype(BF)
    shares = lax.all_to_all(
        summed, "head", split_axis=0, concat_axis=0, tiled=True,
        axis_index_groups=[[0, 2, 4, 6], [1, 3, 5, 7]],
    )
    return jnp.sum(shares.astype(F32), axis=0).astype(BF)


def solution(mesh):
    return jax.shard_map(
        local,
        mesh=mesh,
        in_specs=(
            P(("pool", "ctx"), "head"),
            P(("pool", "ctx"), "head"),
            P(("pool", "ctx"), None),
            P(("pool", "ctx"), None),
            P(),
            P(),
            P(),
            P(),
            P("head", None, None),
            P("head", None, None),
            P("head", None),
        ),
        out_specs=P(("pool", "ctx"), "head"),
        check_vma=False,
    )
```

```python
from functools import partial

import jax
import jax.numpy as jnp
from jax import lax
from jax.experimental import pallas as pl
from jax.experimental.pallas import tpu as pltpu
from jax.sharding import PartitionSpec as P

KV_RANK = 512
ROPE = 64
QK_NOPE = 128
VD = 128
BLK = 128
PAIRS = BLK // 2
WIDE2 = 2 * (KV_RANK + ROPE)
HEADS = 4
TOK = 160
CK = 1024
SLOTS = 16
KEYS = SLOTS * BLK
KW = 768
BIG = 2.0**100
SCALE = (QK_NOPE + ROPE) ** (-0.5)
LOG2E = 1.4426950408889634
BF = jnp.bfloat16
F32 = jnp.float32
STAT = 16


def iota(shape, dim):
    return lax.broadcasted_iota(jnp.int32, shape, dim)


def pick_kernel(ids, cache_ref, holder_ref, block_ref, prior_ref, out_ref):
    me = ids[0] * 4 + ids[1]
    core = ids[2] % 2
    lane = iota((8, 64), 1)
    count = prior_ref[:, 0:1] + prior_ref[:, 1:2]
    match = (holder_ref[...] == me) & (lane < count)
    first = jnp.min(jnp.where(match, lane, 1000), axis=1, keepdims=True)
    last = jnp.max(jnp.where(match, lane, -1), axis=1, keepdims=True)
    wanted = jnp.where(core == 0, first, jnp.where(last > first, last, -2))
    chosen = match & (lane == wanted)
    index = jnp.sum(jnp.where(chosen, block_ref[...] + 1, 0), axis=1, keepdims=True) - 1
    spread = (iota((128, 8), 0) // 16 == iota((128, 8), 1)).astype(BF)
    rows_index = jnp.dot(
        spread,
        jnp.broadcast_to(index.astype(F32), (8, 256)).astype(BF),
        preferred_element_type=F32,
    )
    row = iota((128, 256), 0)
    col = iota((128, 256), 1)
    onehot = ((col // 16 == row % 16) & ((col % 16).astype(F32) == rows_index)).astype(BF)
    stacked = jnp.concatenate(
        [cache_ref[:, p * WIDE2 : (p + 1) * WIDE2] for p in range(16)], axis=0
    )
    out = jnp.dot(onehot, stacked, preferred_element_type=F32).astype(BF)
    even, odd, rope = align(out)
    for g in range(8):
        at = slice(g * 16, (g + 1) * 16)
        for j in range(4):
            out_ref[g, :, j * 128 : (j + 1) * 128] = even[j][at]
            out_ref[g, :, 512 + j * 128 : 640 + j * 128] = odd[j][at]
        out_ref[g, :, 1024:1152] = rope[at]


def align(rows):
    low = iota((rows.shape[0], 128), 1) < 64
    tile = [rows[:, j * 128 : (j + 1) * 128] for j in range(9)]
    flip = {j: pltpu.roll(tile[j].astype(F32), 64, 1).astype(BF) for j in range(5, 9)}
    flip[4] = pltpu.roll(tile[4].astype(F32), 64, 1).astype(BF)
    odd = [jnp.where(low, flip[4 + j], flip[5 + j]) for j in range(4)]
    return tile[:4], odd, jnp.where(low, tile[4], tile[8])


def both_ropes(tile):
    low = iota(tile.shape, 1) < 64
    flip = pltpu.roll(tile.astype(F32), 64, 1).astype(BF)
    return jnp.where(low, tile, flip), jnp.where(low, flip, tile)


def attend_kernel(
    ids, holder, prior, counts,
    q_ref, ka_ref, va_ref, nl_ref,
    a0, am, ap, ax, ay, b0, bm, bp, bx, by,
    out_ref,
    kc, kb, kn, qb, acc, mx, sm, pos, seen, meta, sem,
):
    step = pl.program_id(0)
    group = ids[0]
    ctx = ids[1]
    core = ids[2] & 1
    n0 = counts[group, 0]

    @pl.when(step == 0)
    def _():
        for i in range(SLOTS):
            pos[i] = -1
        for i in range(8):
            seen[i] = 0
        own = prior[group, 0]
        total = own + prior[group, 1]

        def entry(e, carry):
            filled, mine = carry
            where = holder[group, e]
            hit = (where & 3) == ctx
            p = where >> 2

            @pl.when(hit)
            def _():
                s = seen[p]
                seen[p] = s + 1
                pos[p * 2 + s] = filled

            add = hit.astype(jnp.int32)
            return filled + add, mine + jnp.where(e < own, add, 0)

        filled, mine = lax.fori_loop(0, total, entry, (jnp.int32(0), jnp.int32(0)))
        meta[0] = mine * BLK
        meta[1] = filled * BLK
        for i in range(SLOTS):
            dead = pos[i] < 0

            @pl.when(dead)
            def _():
                pos[i] = filled

            filled = filled + dead.astype(jnp.int32)
        for p in range(8):
            for same, pieces in ((True, (a0, am, ap, ax, ay)), (False, (b0, bm, bp, bx, by))):
                slot = core if same else 1 - core
                to = pos[p * 2 + slot]
                sources = [pieces[0].at[p], pieces[1].at[p], pieces[2].at[p]]
                sources.append(pieces[3].at[p] if p < 4 else pieces[4].at[p - 4])
                for i, source in enumerate(sources):
                    pltpu.make_async_copy(source, kc.at[to, i], sem).start()

        def mark(n, base, keys0, keys1):
            row = iota((n, 128), 0) + base
            lane = iota((n, 128), 1)
            miss0 = (lane == 0) & jnp.logical_not(keys0(row))
            miss1 = (lane == 1) & jnp.logical_not(keys1(row))
            return jnp.where(miss0 | miss1, -BIG, 0.0).astype(BF)

        even, odd, rope = align(nl_ref[...])
        rope = both_ropes(rope)
        kn[...] = jnp.zeros(kn.shape, BF)
        for parity, latent in enumerate((even, odd)):
            at = slice(parity * 128, parity * 128 + 80)
            for j in range(4):
                kn[at, j * 128 : (j + 1) * 128] = latent[j]
            kn[at, 512:640] = rope[parity]

        def new_position(row):
            return ctx * TOK + 2 * (row & 127) + (row >> 7)

        kn[:, 640:768] = mark(
            256, 0, lambda r: new_position(r) < n0, lambda r: new_position(r) >= n0
        )
        kb[KEYS:, :] = jnp.zeros((CK, KW), BF)

        def marks(i, _):
            at = pl.multiple_of(i * BLK, BLK)
            kb[pl.ds(at, BLK), 640:768] = mark(
                BLK, at, lambda r: r < meta[0], lambda r: (r >= meta[0]) & (r < meta[1])
            )
            return 0

        lax.fori_loop(0, SLOTS + CK // BLK, marks, 0)
        pltpu.make_async_copy(kc, kc, sem).wait()

        def shape_up(i, _):
            at = pl.multiple_of(i * BLK, BLK)
            block = kc[i].reshape(64, WIDE2)
            ropes = both_ropes(block[:, 1024:1152])
            for parity in range(2):
                to = pl.ds(pl.multiple_of(at + parity * 64, 64), 64)
                kb[to, 0:512] = block[:, parity * 512 : parity * 512 + 512]
                kb[to, 512:640] = ropes[parity]
            return 0

        lax.fori_loop(0, SLOTS, shape_up, 0)

    turn = jnp.where(step == 0, 0, jnp.where(step == 1, 3, jnp.where(step == 2, 1, 2)))
    owner = (ctx + turn) & 3
    rows = HEADS * TOK
    t0 = owner * TOK
    part = q_ref[0]
    lane = iota((TOK, 128), 1)
    token = iota((TOK, 128), 0) + t0
    flags = jnp.where(
        ((lane == 0) & (token < n0)) | ((lane == 1) & (token >= n0)), 1.0, 0.0
    ).astype(BF)
    for j in range(HEADS):
        at = slice(j * TOK, (j + 1) * TOK)
        qb[at, 0:512] = jnp.dot(
            part[:, j * 128 : (j + 1) * 128], ka_ref[j], preferred_element_type=F32
        ).astype(BF)
        rope = part[:, 512 + (j // 2) * 128 : 640 + (j // 2) * 128]
        keep = lane < 64 if j % 2 == 0 else lane >= 64
        qb[at, 512:640] = jnp.where(keep, rope, jnp.zeros_like(rope))
        qb[at, 640:768] = flags
    mx[...] = jnp.full(mx.shape, -BIG, F32)
    sm[...] = jnp.zeros(sm.shape, F32)
    acc[...] = jnp.zeros(acc.shape, F32)

    def wide(value, n):
        return jnp.concatenate([value] * (n // 128), axis=1)

    def fold(scores, values):
        before = mx[...]
        top = jnp.maximum(before, jnp.max(scores, axis=1, keepdims=True))
        keep = jnp.exp2((before - top) * (SCALE * LOG2E))
        weight = jnp.exp2((scores - wide(top, scores.shape[1])) * (SCALE * LOG2E))
        sm[...] = sm[...] * keep + jnp.sum(weight, axis=1, keepdims=True)
        mx[...] = top
        acc[...] = acc[...] * wide(keep, 512) + jnp.dot(
            weight.astype(BF), values, preferred_element_type=F32
        )

    def product(keys):
        return lax.dot_general(
            qb[...], keys, (((1,), (1,)), ((), ())), preferred_element_type=F32
        )

    @pl.when(t0 + TOK > ctx * TOK)
    def _():
        key = iota((rows, 256), 1)
        position = ctx * TOK + 2 * (key & 127) + (key >> 7)
        here = jnp.concatenate([iota((TOK, 256), 0)] * HEADS, axis=0) + t0
        seen_keys = (position <= here) & ((key & 127) < 80)
        fold(jnp.where(seen_keys, product(kn[...]), -BIG), kn[:, 0:512])

    low = jnp.where(t0 < n0, 0, meta[0])
    high = jnp.where(t0 + TOK > n0, meta[1], meta[0])

    def chunk(start, size):
        at = pl.ds(pl.multiple_of(start, BLK), size)
        fold(product(kb[at, :]), kb[at, 0:512])

    full = (high - low + CK // 2 - 1) // CK

    def many(i, _):
        chunk(low + i * CK, CK)
        return 0

    lax.fori_loop(0, full, many, 0)

    @pl.when(low + full * CK < high)
    def _():
        chunk(low + full * CK, CK // 2)

    lane16 = iota((16, 128), 1)
    stats = jnp.zeros((16, 128), F32)
    for j in range(HEADS):
        at = slice(j * TOK, (j + 1) * TOK)
        mass = sm[at, :]
        none = mass == 0.0
        safe = jnp.where(none, 1.0, mass)
        lse = jnp.where(none, -BIG, mx[at, :] * SCALE + jnp.log(safe))
        latent = (acc[at, :] * wide(1.0 / safe, 512)).astype(BF)
        head = jnp.dot(latent, va_ref[j], preferred_element_type=F32).astype(BF)
        out_ref[0, 0:TOK, j * 128 : (j + 1) * 128] = head
        one = lse.astype(BF).astype(F32)
        two = (lse - one).astype(BF).astype(F32)
        three = lse - one - two
        for k in range(TOK // 16):
            base = 12 * k + 3 * j
            cut = slice(k * 16, (k + 1) * 16)
            for i, value in enumerate((one, two, three)):
                stats = jnp.where(lane16 == base + i, value[cut], stats)
    out_ref[0, TOK : TOK + STAT, 0:128] = stats.astype(BF)
    out_ref[0, TOK : TOK + STAT, 128:512] = jnp.zeros((STAT, 384), BF)


def merge(got_ref):
    lane_in = iota((128, 512), 0)
    lane_head = iota((128, 512), 1) // 128
    outs = []
    stats = jnp.concatenate([got_ref[c, TOK : TOK + STAT, 0:128] for c in range(4)], axis=0)
    for k in range(TOK // 16):
        pickup = ((lane_in >= 12 * k + 3 * lane_head) & (lane_in < 12 * k + 3 * lane_head + 3))
        lse = jnp.dot(stats, pickup.astype(BF), preferred_element_type=F32)
        lse = [lse[c * 16 : (c + 1) * 16] for c in range(4)]
        top = jnp.maximum(jnp.maximum(lse[0], lse[1]), jnp.maximum(lse[2], lse[3]))
        weight = [jnp.exp(v - top) for v in lse]
        total = weight[0] + weight[1] + weight[2] + weight[3]
        mixed = sum(
            weight[c] * got_ref[c, k * 16 : (k + 1) * 16, :].astype(F32) for c in range(4)
        )
        outs.append((mixed / total).astype(BF))
    return outs


def away_kernel(ids, got_ref, w_ref, head_ref, out_ref, held):
    @pl.when(pl.program_id(0) == 0)
    def _():
        for k, value in enumerate(merge(got_ref)):
            held[k * 16 : (k + 1) * 16, :] = value
        head_ref[...] = held[...]

    out_ref[0] = jnp.dot(held[...], w_ref[...], preferred_element_type=F32).astype(BF)


def home_kernel(ids, head_ref, w_ref, out_ref):
    out_ref[0] = jnp.dot(head_ref[...], w_ref[...], preferred_element_type=F32).astype(BF)


def shift(value, axis, by, size):
    return lax.ppermute(value, axis, [(i, (i + by) % size) for i in range(size)])


def swap_core(value):
    return lax.ppermute(value, "head", [(i, i ^ 1) for i in range(8)])


def whole(*shape):
    return pl.BlockSpec(shape, lambda i, *_: (0,) * len(shape))


def attend(ids, hit_holder, prior_blocks, new_counts, all_q, key_absorb, value_absorb, new_latent, pieces):
    def turn_of(i, ids):
        turn = jnp.where(i == 0, 0, jnp.where(i == 1, 3, jnp.where(i == 2, 1, 2)))
        return (lax.rem(ids[1] + turn, 4), 0, 0)

    return pl.pallas_call(
        attend_kernel,
        grid_spec=pltpu.PrefetchScalarGridSpec(
            num_scalar_prefetch=4,
            grid=(4,),
            in_specs=[
                pl.BlockSpec((1, TOK, 768), lambda i, *_: (i, 0, 0)),
                whole(HEADS, 128, 512),
                whole(HEADS, 512, 128),
                whole(80, WIDE2),
            ]
            + [pl.BlockSpec(memory_space=pl.ANY)] * 10,
            out_specs=pl.BlockSpec((1, TOK + STAT, 512), lambda i, ids, *_: turn_of(i, ids)),
            scratch_shapes=[
                pltpu.VMEM((SLOTS, 4, 16, WIDE2), BF),
                pltpu.VMEM((KEYS + CK, KW), BF),
                pltpu.VMEM((256, KW), BF),
                pltpu.VMEM((HEADS * TOK, KW), BF),
                pltpu.VMEM((HEADS * TOK, 512), F32),
                pltpu.VMEM((HEADS * TOK, 128), F32),
                pltpu.VMEM((HEADS * TOK, 128), F32),
                pltpu.SMEM((SLOTS,), jnp.int32),
                pltpu.SMEM((8,), jnp.int32),
                pltpu.SMEM((2,), jnp.int32),
                pltpu.SemaphoreType.DMA,
            ],
        ),
        out_shape=jax.ShapeDtypeStruct((4, TOK + STAT, 512), BF),
        compiler_params=pltpu.CompilerParams(vmem_limit_bytes=48 * 2**20),
        name="attend",
    )(
        ids, hit_holder, prior_blocks, new_counts,
        all_q, key_absorb, value_absorb, new_latent,
        *pieces,
    )


def local(
    query_nope, query_rope, new_latent, cache_pool, hit_holder, hit_block,
    prior_blocks, new_counts, key_absorb, value_absorb, out_weight,
):
    ids = jnp.stack(
        [lax.axis_index("pool"), lax.axis_index("ctx"), lax.axis_index("head")]
    ).astype(jnp.int32)

    quarter = 16 * WIDE2
    picked = pl.pallas_call(
        pick_kernel,
        grid_spec=pltpu.PrefetchScalarGridSpec(
            num_scalar_prefetch=1,
            grid=(1,),
            in_specs=[
                pl.BlockSpec((16, quarter), lambda i, ids: (0, ids[2] // 2)),
                pl.BlockSpec((8, 64), lambda i, ids: (0, 0)),
                pl.BlockSpec((8, 64), lambda i, ids: (0, 0)),
                pl.BlockSpec((8, 2), lambda i, ids: (0, 0)),
            ],
            out_specs=pl.BlockSpec((8, 16, WIDE2), lambda i, ids: (0, 0, 0)),
        ),
        out_shape=jax.ShapeDtypeStruct((8, 16, WIDE2), BF),
        name="pick_blocks",
    )(ids, cache_pool, hit_holder, hit_block, prior_blocks)

    a0 = lax.all_to_all(picked, "pool", split_axis=0, concat_axis=0, tiled=True)

    queries = jnp.concatenate([query_nope, query_rope], axis=1)
    qm = shift(queries, "ctx", 1, 4)
    qp = shift(queries, "ctx", -1, 4)
    qx = shift(qm[:80], "ctx", 1, 4)
    qy = shift(qp[80:], "ctx", -1, 4)
    all_q = jnp.concatenate([queries, qm, qp, qx, qy], axis=0).reshape(4, TOK, 768)

    am = shift(a0, "head", 2, 8)
    ap = shift(a0, "head", -2, 8)
    b0 = swap_core(a0)
    ax = shift(am[:4], "head", 2, 8)
    ay = shift(ap[4:], "head", -2, 8)
    bm = swap_core(am)
    bp = swap_core(ap)
    bx = swap_core(ax)
    by = swap_core(ay)

    partial_out = attend(
        ids, hit_holder, prior_blocks, new_counts, all_q, key_absorb, value_absorb, new_latent,
        (a0, am, ap, ax, ay, b0, bm, bp, bx, by),
    )

    got = lax.all_to_all(partial_out, "ctx", split_axis=0, concat_axis=0, tiled=True)

    heads, away = pl.pallas_call(
        away_kernel,
        grid_spec=pltpu.PrefetchScalarGridSpec(
            num_scalar_prefetch=1,
            grid=(4,),
            in_specs=[
                whole(4, TOK + STAT, 512),
                pl.BlockSpec((512, 896), lambda i, ids: (0, 2 * i + 1 - ids[2] % 2)),
            ],
            out_specs=[whole(TOK, 512), pl.BlockSpec((1, TOK, 896), lambda i, ids: (i, 0, 0))],
            scratch_shapes=[pltpu.VMEM((TOK, 512), BF)],
        ),
        out_shape=[
            jax.ShapeDtypeStruct((TOK, 512), BF),
            jax.ShapeDtypeStruct((4, TOK, 896), BF),
        ],
        name="project_away",
    )(ids, got, out_weight)
    arrived = swap_core(away)
    home = pl.pallas_call(
        home_kernel,
        grid_spec=pltpu.PrefetchScalarGridSpec(
            num_scalar_prefetch=1,
            grid=(4,),
            in_specs=[
                whole(TOK, 512),
                pl.BlockSpec((512, 896), lambda i, ids: (0, 2 * i + ids[2] % 2)),
            ],
            out_specs=pl.BlockSpec((1, TOK, 896), lambda i, ids: (i, 0, 0)),
        ),
        out_shape=jax.ShapeDtypeStruct((4, TOK, 896), BF),
        name="project_home",
    )(ids, heads, out_weight)
    summed = (home.astype(F32) + arrived.astype(F32)).astype(BF)
    shares = lax.all_to_all(
        summed, "head", split_axis=0, concat_axis=0, tiled=True,
        axis_index_groups=[[0, 2, 4, 6], [1, 3, 5, 7]],
    )
    return jnp.sum(shares.astype(F32), axis=0).astype(BF)


def solution(mesh):
    return jax.shard_map(
        local,
        mesh=mesh,
        in_specs=(
            P(("pool", "ctx"), "head"),
            P(("pool", "ctx"), "head"),
            P(("pool", "ctx"), None),
            P(("pool", "ctx"), None),
            P(),
            P(),
            P(),
            P(),
            P("head", None, None),
            P("head", None, None),
            P("head", None),
        ),
        out_specs=P(("pool", "ctx"), "head"),
        check_vma=False,
    )
```

```python
from functools import partial

import jax
import jax.numpy as jnp
from jax import lax
from jax.experimental import pallas as pl
from jax.experimental.pallas import tpu as pltpu
from jax.sharding import PartitionSpec as P

KV_RANK = 512
ROPE = 64
QK_NOPE = 128
VD = 128
BLK = 128
PAIRS = BLK // 2
WIDE2 = 2 * (KV_RANK + ROPE)
HEADS = 4
TOK = 160
CK = 1024
SLOTS = 16
KEYS = SLOTS * BLK
KW = 768
BIG = 2.0**100
SCALE = (QK_NOPE + ROPE) ** (-0.5)
LOG2E = 1.4426950408889634
BF = jnp.bfloat16
F32 = jnp.float32
STAT = 16


def iota(shape, dim):
    return lax.broadcasted_iota(jnp.int32, shape, dim)


def pick_kernel(
    ids, cache_ref, holder_ref, block_ref, prior_ref, nope_ref, rope_ref, out_ref, query_ref
):
    query_ref[:, 0:512] = nope_ref[...]
    query_ref[:, 512:768] = rope_ref[...]
    me = ids[0] * 4 + ids[1]
    core = ids[2] % 2
    lane = iota((8, 64), 1)
    count = prior_ref[:, 0:1] + prior_ref[:, 1:2]
    match = (holder_ref[...] == me) & (lane < count)
    first = jnp.min(jnp.where(match, lane, 1000), axis=1, keepdims=True)
    last = jnp.max(jnp.where(match, lane, -1), axis=1, keepdims=True)
    wanted = jnp.where(core == 0, first, jnp.where(last > first, last, -2))
    chosen = match & (lane == wanted)
    index = jnp.sum(jnp.where(chosen, block_ref[...] + 1, 0), axis=1, keepdims=True) - 1
    spread = (iota((128, 8), 0) // 16 == iota((128, 8), 1)).astype(BF)
    rows_index = jnp.dot(
        spread,
        jnp.broadcast_to(index.astype(F32), (8, 256)).astype(BF),
        preferred_element_type=F32,
    )
    row = iota((128, 256), 0)
    col = iota((128, 256), 1)
    onehot = ((col // 16 == row % 16) & ((col % 16).astype(F32) == rows_index)).astype(BF)
    stacked = jnp.concatenate(
        [cache_ref[:, p * WIDE2 : (p + 1) * WIDE2] for p in range(16)], axis=0
    )
    out = jnp.dot(onehot, stacked, preferred_element_type=F32).astype(BF)
    even, odd, rope = align(out)
    for g in range(8):
        at = slice(g * 16, (g + 1) * 16)
        for j in range(4):
            out_ref[g, :, j * 128 : (j + 1) * 128] = even[j][at]
            out_ref[g, :, 512 + j * 128 : 640 + j * 128] = odd[j][at]
        out_ref[g, :, 1024:1152] = rope[at]


def align(rows):
    low = iota((rows.shape[0], 128), 1) < 64
    tile = [rows[:, j * 128 : (j + 1) * 128] for j in range(9)]
    flip = {j: pltpu.roll(tile[j].astype(F32), 64, 1).astype(BF) for j in range(5, 9)}
    flip[4] = pltpu.roll(tile[4].astype(F32), 64, 1).astype(BF)
    odd = [jnp.where(low, flip[4 + j], flip[5 + j]) for j in range(4)]
    return tile[:4], odd, jnp.where(low, tile[4], tile[8])


def both_ropes(tile):
    low = iota(tile.shape, 1) < 64
    flip = pltpu.roll(tile.astype(F32), 64, 1).astype(BF)
    return jnp.where(low, tile, flip), jnp.where(low, flip, tile)


def wide(value, n):
    return jnp.concatenate([value] * (n // 128), axis=1)


def turn_of(step):
    return jnp.where(step == 0, 0, jnp.where(step == 1, 3, jnp.where(step == 2, 1, 2)))


def product(queries, keys):
    return lax.dot_general(
        queries, keys, (((1,), (1,)), ((), ())), preferred_element_type=F32
    )


def ready_kernel(
    ids, holder, prior, counts,
    q0, qm, qp, qx, qy, ka_ref, nl_ref,
    q_out, acc_out, mx_out, sm_out, mark_out, table,
    part, kn, seen,
):
    step = pl.program_id(0)
    group = ids[0]
    ctx = ids[1]
    n0 = counts[group, 0]

    def mark(n, base, keys0, keys1):
        row = iota((n, 128), 0) + base
        lane = iota((n, 128), 1)
        miss0 = (lane == 0) & jnp.logical_not(keys0(row))
        miss1 = (lane == 1) & jnp.logical_not(keys1(row))
        return jnp.where(miss0 | miss1, -BIG, 0.0).astype(BF)

    @pl.when(step == 0)
    def _():
        for i in range(SLOTS):
            table[i] = -1
        for i in range(8):
            seen[i] = 0
        own = prior[group, 0]
        total = own + prior[group, 1]

        def entry(e, carry):
            filled, mine = carry
            where = holder[group, e]
            hit = (where & 3) == ctx
            p = where >> 2

            @pl.when(hit)
            def _():
                s = seen[p]
                seen[p] = s + 1
                table[p * 2 + s] = filled

            add = hit.astype(jnp.int32)
            return filled + add, mine + jnp.where(e < own, add, 0)

        filled, mine = lax.fori_loop(0, total, entry, (jnp.int32(0), jnp.int32(0)))
        end0 = mine * BLK
        end1 = filled * BLK
        table[SLOTS] = end0
        table[SLOTS + 1] = end1
        table[SLOTS + 2] = n0
        for i in range(SLOTS + 3, 32):
            table[i] = 0
        for i in range(SLOTS):
            dead = table[i] < 0

            @pl.when(dead)
            def _():
                table[i] = filled

            filled = filled + dead.astype(jnp.int32)

        def marks(i, _):
            at = pl.multiple_of(i * BLK, BLK)
            mark_out[pl.ds(at, BLK), :] = mark(
                BLK, at, lambda r: r < end0, lambda r: (r >= end0) & (r < end1)
            )
            return 0

        lax.fori_loop(0, SLOTS + CK // BLK, marks, 0)

        even, odd, rope = align(nl_ref[...])
        rope = both_ropes(rope)
        kn[...] = jnp.zeros(kn.shape, BF)
        for parity, latent in enumerate((even, odd)):
            at = slice(parity * 128, parity * 128 + 80)
            for j in range(4):
                kn[at, j * 128 : (j + 1) * 128] = latent[j]
            kn[at, 512:640] = rope[parity]

        def new_position(row):
            return ctx * TOK + 2 * (row & 127) + (row >> 7)

        kn[:, 640:768] = mark(
            256, 0, lambda r: new_position(r) < n0, lambda r: new_position(r) >= n0
        )
        part[...] = q0[...]

    @pl.when(step == 1)
    def _():
        part[...] = qm[...]

    @pl.when(step == 2)
    def _():
        part[...] = qp[...]

    @pl.when(step == 3)
    def _():
        part[0:80] = qx[...]
        part[80:160] = qy[...]

    rows = HEADS * TOK
    t0 = ((ctx + turn_of(step)) & 3) * TOK
    lane = iota((TOK, 128), 1)
    token = iota((TOK, 128), 0) + t0
    flags = jnp.where(
        ((lane == 0) & (token < n0)) | ((lane == 1) & (token >= n0)), 1.0, 0.0
    ).astype(BF)
    for j in range(HEADS):
        at = slice(j * TOK, (j + 1) * TOK)
        q_out[0, at, 0:512] = jnp.dot(
            part[:, j * 128 : (j + 1) * 128], ka_ref[j], preferred_element_type=F32
        ).astype(BF)
        rope = part[:, 512 + (j // 2) * 128 : 640 + (j // 2) * 128]
        keep = lane < 64 if j % 2 == 0 else lane >= 64
        q_out[0, at, 512:640] = jnp.where(keep, rope, jnp.zeros_like(rope))
        q_out[0, at, 640:768] = flags

    visible = t0 + TOK > ctx * TOK

    @pl.when(visible)
    def _():
        key = iota((rows, 256), 1)
        position = ctx * TOK + 2 * (key & 127) + (key >> 7)
        here = jnp.concatenate([iota((TOK, 256), 0)] * HEADS, axis=0) + t0
        seen_keys = (position <= here) & ((key & 127) < 80)
        scores = jnp.where(seen_keys, product(q_out[0], kn[...]), -BIG)
        top = jnp.maximum(
            jnp.full((rows, 128), -BIG, F32), jnp.max(scores, axis=1, keepdims=True)
        )
        weight = jnp.exp2((scores - wide(top, 256)) * (SCALE * LOG2E))
        mx_out[0] = top
        sm_out[0] = jnp.zeros((rows, 128), F32) + jnp.sum(weight, axis=1, keepdims=True)
        acc_out[0] = jnp.dot(weight.astype(BF), kn[:, 0:512], preferred_element_type=F32)

    @pl.when(jnp.logical_not(visible))
    def _():
        mx_out[0] = jnp.full((rows, 128), -BIG, F32)
        sm_out[0] = jnp.zeros((rows, 128), F32)
        acc_out[0] = jnp.zeros((rows, 512), F32)


def attend_kernel(
    ids, table,
    q_ref, acc0, mx0, sm0, va_ref, mark_ref,
    a0, am, ap, ax, ay, b0, bm, bp, bx, by,
    out_ref,
    kc, kb, acc, mx, sm, sem,
):
    step = pl.program_id(0)
    core = ids[2] & 1
    end0 = table[SLOTS]
    end1 = table[SLOTS + 1]
    n0 = table[SLOTS + 2]

    @pl.when(step == 0)
    def _():
        for w, pieces in enumerate(((a0, am, ap, ax, ay), (b0, bm, bp, bx, by))):
            for i in range(3):
                pltpu.make_async_copy(pieces[i], kc.at[w, i], sem.at[w]).start()
            pltpu.make_async_copy(pieces[3], kc.at[w, 3, pl.ds(0, 4)], sem.at[w]).start()
            pltpu.make_async_copy(pieces[4], kc.at[w, 3, pl.ds(4, 4)], sem.at[w]).start()
        marks = pltpu.make_async_copy(mark_ref, kb.at[:, pl.ds(640, 128)], sem.at[2])
        marks.start()
        kb[KEYS:, 0:640] = jnp.zeros((CK, 640), BF)
        for w in range(2):
            pltpu.make_async_copy(kc.at[w], kc.at[w], sem.at[w]).wait()
            slot = core if w == 0 else 1 - core

            def shape_up(p, _):
                at = table[p * 2 + slot] * BLK
                for i in range(4):
                    block = kc[w, i, p]
                    ropes = both_ropes(block[:, 1024:1152])
                    for parity in range(2):
                        to = pl.ds(pl.multiple_of(at + parity * 64 + i * 16, 16), 16)
                        kb[to, 0:512] = block[:, parity * 512 : parity * 512 + 512]
                        kb[to, 512:640] = ropes[parity]
                return 0

            lax.fori_loop(0, 8, shape_up, 0)
        marks.wait()

    t0 = ((ids[1] + turn_of(step)) & 3) * TOK
    mx[...] = mx0[0]
    sm[...] = sm0[0]
    acc[...] = acc0[0]

    def chunk(start, size):
        at = pl.ds(pl.multiple_of(start, BLK), size)
        scores = product(q_ref[0], kb[at, :])
        before = mx[...]
        top = jnp.maximum(before, jnp.max(scores, axis=1, keepdims=True))
        keep = jnp.exp2((before - top) * (SCALE * LOG2E))
        weight = jnp.exp2((scores - wide(top, size)) * (SCALE * LOG2E))
        sm[...] = sm[...] * keep + jnp.sum(weight, axis=1, keepdims=True)
        mx[...] = top
        acc[...] = acc[...] * wide(keep, 512) + jnp.dot(
            weight.astype(BF), kb[at, 0:512], preferred_element_type=F32
        )

    low = jnp.where(t0 < n0, 0, end0)
    high = jnp.where(t0 + TOK > n0, end1, end0)
    full = (high - low + CK // 2 - 1) // CK

    def many(i, _):
        chunk(low + i * CK, CK)
        return 0

    lax.fori_loop(0, full, many, 0)

    @pl.when(low + full * CK < high)
    def _():
        chunk(low + full * CK, CK // 2)

    lane16 = iota((16, 128), 1)
    stats = jnp.zeros((16, 128), F32)
    for j in range(HEADS):
        at = slice(j * TOK, (j + 1) * TOK)
        mass = sm[at, :]
        none = mass == 0.0
        safe = jnp.where(none, 1.0, mass)
        lse = jnp.where(none, -BIG, mx[at, :] * SCALE + jnp.log(safe))
        latent = (acc[at, :] * wide(1.0 / safe, 512)).astype(BF)
        head = jnp.dot(latent, va_ref[j], preferred_element_type=F32).astype(BF)
        out_ref[0, 0:TOK, j * 128 : (j + 1) * 128] = head
        one = lse.astype(BF).astype(F32)
        two = (lse - one).astype(BF).astype(F32)
        three = lse - one - two
        for k in range(TOK // 16):
            base = 12 * k + 3 * j
            cut = slice(k * 16, (k + 1) * 16)
            for i, value in enumerate((one, two, three)):
                stats = jnp.where(lane16 == base + i, value[cut], stats)
    out_ref[0, TOK : TOK + STAT, 0:128] = stats.astype(BF)
    out_ref[0, TOK : TOK + STAT, 128:512] = jnp.zeros((STAT, 384), BF)


def merge(got_ref):
    lane_in = iota((128, 512), 0)
    lane_head = iota((128, 512), 1) // 128
    outs = []
    stats = jnp.concatenate([got_ref[c, TOK : TOK + STAT, 0:128] for c in range(4)], axis=0)
    for k in range(TOK // 16):
        pickup = ((lane_in >= 12 * k + 3 * lane_head) & (lane_in < 12 * k + 3 * lane_head + 3))
        lse = jnp.dot(stats, pickup.astype(BF), preferred_element_type=F32)
        lse = [lse[c * 16 : (c + 1) * 16] for c in range(4)]
        top = jnp.maximum(jnp.maximum(lse[0], lse[1]), jnp.maximum(lse[2], lse[3]))
        weight = [jnp.exp(v - top) for v in lse]
        total = weight[0] + weight[1] + weight[2] + weight[3]
        mixed = sum(
            weight[c] * got_ref[c, k * 16 : (k + 1) * 16, :].astype(F32) for c in range(4)
        )
        outs.append((mixed / total).astype(BF))
    return outs


def fetch(ids, w_ref, held, sem, picks):
    copies = []
    for i, (turn, other) in enumerate(picks):
        y = ((ids[2] >> 1) + turn) & 3
        column = (y * 2 + ((ids[2] & 1) ^ other)) * 896
        copies.append(
            pltpu.make_async_copy(
                w_ref.at[:, pl.ds(pl.multiple_of(column, 128), 896)], held.at[i], sem.at[i]
            )
        )
        copies[-1].start()
    return copies


def first_kernel(ids, got_ref, w_ref, head_ref, away_ref, home_ref, held, sem):
    copies = fetch(ids, w_ref, held, sem, ((2, 1), (2, 0)))
    for k, value in enumerate(merge(got_ref)):
        head_ref[k * 16 : (k + 1) * 16, :] = value
    for i, out in enumerate((away_ref, home_ref)):
        copies[i].wait()
        out[...] = jnp.dot(head_ref[...], held[i], preferred_element_type=F32).astype(BF)


def rest_kernel(other, ids, head_ref, w_ref, out_ref, held, sem):
    copies = fetch(ids, w_ref, held, sem, ((1, other), (3, other), (0, other)))
    for i in range(3):
        copies[i].wait()
        out_ref[i] = jnp.dot(head_ref[...], held[i], preferred_element_type=F32).astype(BF)


def shift(value, axis, by, size):
    return lax.ppermute(value, axis, [(i, (i + by) % size) for i in range(size)])


def swap_core(value):
    return lax.ppermute(value, "head", [(i, i ^ 1) for i in range(8)])


def whole(*shape):
    return pl.BlockSpec(shape, lambda i, *_: (0,) * len(shape))


def prepare(ids, hit_holder, prior_blocks, new_counts, queries, key_absorb, new_latent):
    rows = HEADS * TOK
    tile = lambda n: pl.BlockSpec((1, rows, n), lambda i, *_: (i, 0, 0))
    return pl.pallas_call(
        ready_kernel,
        grid_spec=pltpu.PrefetchScalarGridSpec(
            num_scalar_prefetch=4,
            grid=(4,),
            in_specs=[
                whole(TOK, 768), whole(TOK, 768), whole(TOK, 768), whole(80, 768), whole(80, 768),
                whole(HEADS, 128, 512),
                whole(80, WIDE2),
            ],
            out_specs=[
                tile(KW), tile(512), tile(128), tile(128),
                whole(KEYS + CK, 128),
                pl.BlockSpec(memory_space=pltpu.SMEM),
            ],
            scratch_shapes=[
                pltpu.VMEM((TOK, 768), BF),
                pltpu.VMEM((256, KW), BF),
                pltpu.SMEM((8,), jnp.int32),
            ],
        ),
        out_shape=[
            jax.ShapeDtypeStruct((4, rows, KW), BF),
            jax.ShapeDtypeStruct((4, rows, 512), F32),
            jax.ShapeDtypeStruct((4, rows, 128), F32),
            jax.ShapeDtypeStruct((4, rows, 128), F32),
            jax.ShapeDtypeStruct((KEYS + CK, 128), BF),
            jax.ShapeDtypeStruct((32,), jnp.int32),
        ],
        compiler_params=pltpu.CompilerParams(vmem_limit_bytes=28 * 2**20),
        cost_estimate=pl.CostEstimate(
            flops=3 * 10**9, bytes_accessed=14 * 10**6, transcendentals=10**6
        ),
        name="prepare",
    )(ids, hit_holder, prior_blocks, new_counts, *queries, key_absorb, new_latent)


def attend(ids, ready, value_absorb, pieces):
    q_all, acc0, mx0, sm0, marks, table = ready
    rows = HEADS * TOK
    tile = lambda n: pl.BlockSpec((1, rows, n), lambda i, *_: (i, 0, 0))
    hbm = pl.BlockSpec(memory_space=pl.ANY)
    return pl.pallas_call(
        attend_kernel,
        grid_spec=pltpu.PrefetchScalarGridSpec(
            num_scalar_prefetch=2,
            grid=(4,),
            in_specs=[tile(KW), tile(512), tile(128), tile(128), whole(HEADS, 512, 128)]
            + [hbm] * 11,
            out_specs=pl.BlockSpec(
                (1, TOK + STAT, 512),
                lambda i, ids, table: ((ids[1] + turn_of(i)) & 3, 0, 0),
            ),
            scratch_shapes=[
                pltpu.VMEM((2, 4, 8, 16, WIDE2), BF),
                pltpu.VMEM((KEYS + CK, KW), BF),
                pltpu.VMEM((rows, 512), F32),
                pltpu.VMEM((rows, 128), F32),
                pltpu.VMEM((rows, 128), F32),
                pltpu.SemaphoreType.DMA((3,)),
            ],
        ),
        out_shape=jax.ShapeDtypeStruct((4, TOK + STAT, 512), BF),
        compiler_params=pltpu.CompilerParams(vmem_limit_bytes=36 * 2**20),
        cost_estimate=pl.CostEstimate(
            flops=15 * 10**9, bytes_accessed=16 * 10**6, transcendentals=5 * 10**6
        ),
        name="attend",
    )(ids, table, q_all, acc0, mx0, sm0, value_absorb, marks, *pieces)


def rest(other, ids, heads, out_weight):
    return pl.pallas_call(
        partial(rest_kernel, other),
        grid_spec=pltpu.PrefetchScalarGridSpec(
            num_scalar_prefetch=1,
            grid=(1,),
            in_specs=[whole(TOK, 512), pl.BlockSpec(memory_space=pl.ANY)],
            out_specs=whole(3, TOK, 896),
            scratch_shapes=[pltpu.VMEM((3, 512, 896), BF), pltpu.SemaphoreType.DMA((3,))],
        ),
        out_shape=jax.ShapeDtypeStruct((3, TOK, 896), BF),
        compiler_params=pltpu.CompilerParams(vmem_limit_bytes=12 * 2**20),
        cost_estimate=pl.CostEstimate(
            flops=1 * 10**9, bytes_accessed=4 * 10**6, transcendentals=0
        ),
        name="project_home" if other == 0 else "project_away",
    )(ids, heads, out_weight)


def local(
    query_nope, query_rope, new_latent, cache_pool, hit_holder, hit_block,
    prior_blocks, new_counts, key_absorb, value_absorb, out_weight,
):
    ids = jnp.stack(
        [lax.axis_index("pool"), lax.axis_index("ctx"), lax.axis_index("head")]
    ).astype(jnp.int32)

    quarter = 16 * WIDE2
    picked, queries = pl.pallas_call(
        pick_kernel,
        grid_spec=pltpu.PrefetchScalarGridSpec(
            num_scalar_prefetch=1,
            grid=(1,),
            in_specs=[
                pl.BlockSpec((16, quarter), lambda i, ids: (0, ids[2] // 2)),
                whole(8, 64),
                whole(8, 64),
                whole(8, 2),
                whole(TOK, 512),
                whole(TOK, 256),
            ],
            out_specs=[whole(8, 16, WIDE2), whole(TOK, 768)],
        ),
        out_shape=[
            jax.ShapeDtypeStruct((8, 16, WIDE2), BF),
            jax.ShapeDtypeStruct((TOK, 768), BF),
        ],
        name="pick_blocks",
    )(ids, cache_pool, hit_holder, hit_block, prior_blocks, query_nope, query_rope)

    a0 = lax.all_to_all(picked, "pool", split_axis=0, concat_axis=0, tiled=True)

    qm = shift(queries, "ctx", 1, 4)
    qp = shift(queries, "ctx", -1, 4)
    qx = shift(qm[:80], "ctx", 1, 4)
    qy = shift(qp[80:], "ctx", -1, 4)

    a0, qx, qy = lax.optimization_barrier((a0, qx, qy))
    am = shift(a0, "head", 2, 8)
    ap = shift(a0, "head", -2, 8)
    b0 = swap_core(a0)
    ready = prepare(
        ids, hit_holder, prior_blocks, new_counts, (queries, qm, qp, qx, qy),
        key_absorb, new_latent,
    )
    ax = shift(am[:4], "head", 2, 8)
    ay = shift(ap[4:], "head", -2, 8)
    bm = swap_core(am)
    bp = swap_core(ap)
    bx = swap_core(ax)
    by = swap_core(ay)
    partial_out = attend(ids, ready, value_absorb, (a0, am, ap, ax, ay, b0, bm, bp, bx, by))

    got = lax.all_to_all(partial_out, "ctx", split_axis=0, concat_axis=0, tiled=True)

    heads, away2, home2 = pl.pallas_call(
        first_kernel,
        grid_spec=pltpu.PrefetchScalarGridSpec(
            num_scalar_prefetch=1,
            grid=(1,),
            in_specs=[whole(4, TOK + STAT, 512), pl.BlockSpec(memory_space=pl.ANY)],
            out_specs=[whole(TOK, 512), whole(TOK, 896), whole(TOK, 896)],
            scratch_shapes=[pltpu.VMEM((2, 512, 896), BF), pltpu.SemaphoreType.DMA((2,))],
        ),
        out_shape=[
            jax.ShapeDtypeStruct((TOK, 512), BF),
            jax.ShapeDtypeStruct((TOK, 896), BF),
            jax.ShapeDtypeStruct((TOK, 896), BF),
        ],
        compiler_params=pltpu.CompilerParams(vmem_limit_bytes=12 * 2**20),
        name="merge_project",
    )(ids, got, out_weight)
    across = swap_core(away2)
    away = rest(1, ids, heads, out_weight)
    arrived = swap_core(away)
    opposite = (home2.astype(F32) + across.astype(F32)).astype(BF)
    from_low = shift(opposite[:80], "head", 2, 8)
    from_high = shift(opposite[80:], "head", -2, 8)
    home = rest(0, ids, heads, out_weight)
    both = home.astype(F32) + arrived.astype(F32)
    up = jnp.concatenate([both[0, :80] + from_low.astype(F32), both[0, 80:]], axis=0).astype(BF)
    down = jnp.concatenate([both[1, :80], both[1, 80:] + from_high.astype(F32)], axis=0).astype(BF)
    got_up = shift(up, "head", 2, 8)
    got_down = shift(down, "head", -2, 8)
    return (both[2] + got_up.astype(F32) + got_down.astype(F32)).astype(BF)


def solution(mesh):
    return jax.shard_map(
        local,
        mesh=mesh,
        in_specs=(
            P(("pool", "ctx"), "head"),
            P(("pool", "ctx"), "head"),
            P(("pool", "ctx"), None),
            P(("pool", "ctx"), None),
            P(),
            P(),
            P(),
            P(),
            P("head", None, None),
            P("head", None, None),
            P("head", None),
        ),
        out_specs=P(("pool", "ctx"), "head"),
        check_vma=False,
    )
```

```python
from functools import partial

import jax
import jax.numpy as jnp
from jax import lax
from jax.experimental import pallas as pl
from jax.experimental.pallas import tpu as pltpu
from jax.sharding import PartitionSpec as P

KV_RANK = 512
ROPE = 64
QK_NOPE = 128
VD = 128
BLK = 128
PAIRS = BLK // 2
WIDE2 = 2 * (KV_RANK + ROPE)
HEADS = 4
TOK = 160
SLOTS = 16
HALF = BLK // 2
KEYS = SLOTS * HALF
KW = 768
BIG = 2.0**100
SCALE = (QK_NOPE + ROPE) ** (-0.5)
LOG2E = 1.4426950408889634
BF = jnp.bfloat16
F32 = jnp.float32
STAT = 16


def iota(shape, dim):
    return lax.broadcasted_iota(jnp.int32, shape, dim)


def pick_kernel(
    ids, prior, cache_ref, holder_ref, block_ref, nope_ref, rope_ref, out_ref, query_ref
):
    query_ref[:, 0:512] = nope_ref[...]
    query_ref[:, 512:768] = rope_ref[...]
    me = ids[0] * 4 + ids[1]
    core = ids[2] & 1
    lane = iota((8, 64), 1)
    group = iota((8, 64), 0)
    count = jnp.zeros((8, 64), jnp.int32)
    for g in range(8):
        count = jnp.where(group == g, prior[0, g] + prior[1, g], count)
    match = (holder_ref[...] == me) & (lane < count)
    first = jnp.min(jnp.where(match, lane, 1000), axis=1, keepdims=True)
    last = jnp.max(jnp.where(match, lane, -1), axis=1, keepdims=True)
    wanted = jnp.where(core == 0, first, jnp.where(last > first, last, -2))
    chosen = match & (lane == wanted)
    index = jnp.sum(jnp.where(chosen, block_ref[...] + 1, 0), axis=1, keepdims=True) - 1
    spread = (iota((128, 8), 0) // 16 == iota((128, 8), 1)).astype(BF)
    rows_index = jnp.dot(
        spread,
        jnp.broadcast_to(index.astype(F32), (8, 256)).astype(BF),
        preferred_element_type=F32,
    )
    row = iota((128, 256), 0)
    col = iota((128, 256), 1)
    onehot = ((col // 16 == row % 16) & ((col % 16).astype(F32) == rows_index)).astype(BF)
    for part in range(2):
        stacked = jnp.concatenate(
            [
                cache_ref[:, p * WIDE2 : (p + 1) * WIDE2]
                for p in range(part * 16, part * 16 + 16)
            ],
            axis=0,
        )
        out = jnp.dot(onehot, stacked, preferred_element_type=F32).astype(BF)
        even, odd, rope = align(out)
        to = slice(part * 16, part * 16 + 16)
        for g in range(8):
            at = slice(g * 16, (g + 1) * 16)
            for j in range(4):
                out_ref[g, to, j * 128 : (j + 1) * 128] = even[j][at]
                out_ref[g, to, 512 + j * 128 : 640 + j * 128] = odd[j][at]
            out_ref[g, to, 1024:1152] = rope[at]


def align(rows):
    low = iota((rows.shape[0], 128), 1) < 64
    tile = [rows[:, j * 128 : (j + 1) * 128] for j in range(9)]
    flip = {j: pltpu.roll(tile[j].astype(F32), 64, 1).astype(BF) for j in range(5, 9)}
    flip[4] = pltpu.roll(tile[4].astype(F32), 64, 1).astype(BF)
    odd = [jnp.where(low, flip[4 + j], flip[5 + j]) for j in range(4)]
    return tile[:4], odd, jnp.where(low, tile[4], tile[8])


def both_ropes(tile):
    low = iota(tile.shape, 1) < 64
    flip = pltpu.roll(tile.astype(F32), 64, 1).astype(BF)
    return jnp.where(low, tile, flip), jnp.where(low, flip, tile)


def wide(value, n):
    return jnp.concatenate([value] * (n // 128), axis=1)


def turn_of(step):
    return jnp.where(step == 0, 0, jnp.where(step == 1, 3, jnp.where(step == 2, 1, 2)))


def product(queries, keys):
    return lax.dot_general(
        queries, keys, (((1,), (1,)), ((), ())), preferred_element_type=F32
    )


def ready_kernel(
    ids, holder, prior, counts,
    q0, qm, qp, qx, qy, ka_ref, nl_ref,
    q_out, acc_out, mx_out, sm_out, mark_out, table,
    part, kn, seen,
):
    step = pl.program_id(0)
    group = ids[0]
    ctx = ids[1]
    n0 = counts[0, group]

    def mark(n, base, keys0, keys1):
        row = iota((n, 128), 0) + base
        lane = iota((n, 128), 1)
        miss0 = (lane == 0) & jnp.logical_not(keys0(row))
        miss1 = (lane == 1) & jnp.logical_not(keys1(row))
        return jnp.where(miss0 | miss1, -BIG, 0.0).astype(BF)

    @pl.when(step == 0)
    def _():
        for i in range(SLOTS):
            table[i] = -1
        for i in range(8):
            seen[i] = 0
        own = prior[0, group]
        total = own + prior[1, group]

        def entry(e, carry):
            filled, mine = carry
            where = holder[group, e]
            hit = (where & 3) == ctx
            p = where >> 2

            @pl.when(hit)
            def _():
                s = seen[p]
                seen[p] = s + 1
                table[p * 2 + s] = filled

            add = hit.astype(jnp.int32)
            return filled + add, mine + jnp.where(e < own, add, 0)

        filled, mine = lax.fori_loop(0, total, entry, (jnp.int32(0), jnp.int32(0)))
        end0 = mine * HALF
        end1 = filled * HALF
        table[SLOTS] = end0
        table[SLOTS + 1] = end1
        table[SLOTS + 2] = n0
        for i in range(SLOTS + 3, 32):
            table[i] = 0
        for i in range(SLOTS):
            dead = table[i] < 0

            @pl.when(dead)
            def _():
                table[i] = filled

            filled = filled + dead.astype(jnp.int32)

        def marks(i, _):
            at = pl.multiple_of(i * BLK, BLK)
            mark_out[pl.ds(at, BLK), :] = mark(
                BLK, at, lambda r: r < end0, lambda r: (r >= end0) & (r < end1)
            )
            return 0

        lax.fori_loop(0, 2 * KEYS // BLK, marks, 0)

        even, odd, rope = align(nl_ref[...])
        rope = both_ropes(rope)
        kn[...] = jnp.zeros(kn.shape, BF)
        for parity, latent in enumerate((even, odd)):
            at = slice(parity * 128, parity * 128 + 80)
            for j in range(4):
                kn[at, j * 128 : (j + 1) * 128] = latent[j]
            kn[at, 512:640] = rope[parity]

        def new_position(row):
            return ctx * TOK + 2 * (row & 127) + (row >> 7)

        kn[:, 640:768] = mark(
            256, 0, lambda r: new_position(r) < n0, lambda r: new_position(r) >= n0
        )
        part[...] = q0[...]

    @pl.when(step == 1)
    def _():
        part[...] = qm[...]

    @pl.when(step == 2)
    def _():
        part[...] = qp[...]

    @pl.when(step == 3)
    def _():
        part[0:80] = qx[...]
        part[80:160] = qy[...]

    rows = HEADS * TOK
    t0 = ((ctx + turn_of(step)) & 3) * TOK
    lane = iota((TOK, 128), 1)
    token = iota((TOK, 128), 0) + t0
    flags = jnp.where(
        ((lane == 0) & (token < n0)) | ((lane == 1) & (token >= n0)), 1.0, 0.0
    ).astype(BF)
    for j in range(HEADS):
        at = slice(j * TOK, (j + 1) * TOK)
        q_out[0, at, 0:512] = jnp.dot(
            part[:, j * 128 : (j + 1) * 128], ka_ref[j], preferred_element_type=F32
        ).astype(BF)
        rope = part[:, 512 + (j // 2) * 128 : 640 + (j // 2) * 128]
        keep = lane < 64 if j % 2 == 0 else lane >= 64
        q_out[0, at, 512:640] = jnp.where(keep, rope, jnp.zeros_like(rope))
        q_out[0, at, 640:768] = flags

    visible = t0 + TOK > ctx * TOK

    @pl.when(visible)
    def _():
        key = iota((rows, 256), 1)
        position = ctx * TOK + 2 * (key & 127) + (key >> 7)
        here = jnp.concatenate([iota((TOK, 256), 0)] * HEADS, axis=0) + t0
        seen_keys = (position <= here) & ((key & 127) < 80)
        scores = jnp.where(seen_keys, product(q_out[0], kn[...]), -BIG)
        top = jnp.maximum(
            jnp.full((rows, 128), -BIG, F32), jnp.max(scores, axis=1, keepdims=True)
        )
        weight = jnp.exp2((scores - wide(top, 256)) * (SCALE * LOG2E))
        mx_out[0] = top
        sm_out[0] = jnp.zeros((rows, 128), F32) + jnp.sum(weight, axis=1, keepdims=True)
        acc_out[0] = jnp.dot(weight.astype(BF), kn[:, 0:512], preferred_element_type=F32)

    @pl.when(jnp.logical_not(visible))
    def _():
        mx_out[0] = jnp.full((rows, 128), -BIG, F32)
        sm_out[0] = jnp.zeros((rows, 128), F32)
        acc_out[0] = jnp.zeros((rows, 512), F32)


def attend_kernel(turns, loads, last, ids, table, q_ref, acc0, mx0, sm0, *refs):
    refs = list(refs)
    if last:
        va_ref = refs.pop(0)
    mark_ref = refs.pop(0)
    pieces = [refs.pop(0) for _ in loads]
    if last:
        outs = [refs.pop(0) for _ in turns]
        acc, mx, sm = [refs.pop() for _ in range(3)]
    else:
        acc_out, mx_out, sm_out = [refs.pop(0) for _ in range(3)]
    kc, kb, sem = refs
    step = pl.program_id(0)
    core = ids[2] & 1
    end0 = table[SLOTS]
    end1 = table[SLOTS + 1]
    n0 = table[SLOTS + 2]

    @pl.when(step == 0)
    def _():
        for piece, (w, p0, n) in zip(pieces, loads):
            pltpu.make_async_copy(piece, kc.at[w, pl.ds(p0, n)], sem.at[w]).start()
        marks = pltpu.make_async_copy(mark_ref, kb.at[:, pl.ds(640, 128)], sem.at[2])
        marks.start()
        kb[KEYS:, 0:640] = jnp.zeros((KEYS, 640), BF)
        for w in range(2):
            pltpu.make_async_copy(kc.at[w], kc.at[w], sem.at[w]).wait()
            slot = core if w == 0 else 1 - core

            def shape_up(p, _):
                at = table[p * 2 + slot] * HALF
                block = kc[w, p]
                ropes = both_ropes(block[:, 1024:1152])
                for parity in range(2):
                    to = pl.ds(pl.multiple_of(at + parity * 32, 32), 32)
                    kb[to, 0:512] = block[:, parity * 512 : parity * 512 + 512]
                    kb[to, 512:640] = ropes[parity]
                return 0

            lax.fori_loop(0, 8, shape_up, 0)
        marks.wait()

    turn = turns[-1]
    for i in range(len(turns) - 2, -1, -1):
        turn = jnp.where(step == i, turns[i], turn)
    t0 = ((ids[1] + turn) & 3) * TOK
    low = jnp.where(t0 < n0, 0, end0)
    high = jnp.where(t0 + TOK > n0, end1, end0)
    size = high - low

    def chunk(size):
        at = pl.ds(pl.multiple_of(low, HALF), size)
        scores = product(q_ref[0], kb[at, :])
        before = mx0[0]
        top = jnp.maximum(before, jnp.max(scores, axis=1, keepdims=True))
        keep = jnp.exp2((before - top) * (SCALE * LOG2E))
        weight = jnp.exp2((scores - wide(top, size)) * (SCALE * LOG2E))
        put(
            acc0[0] * wide(keep, 512)
            + jnp.dot(weight.astype(BF), kb[at, 0:512], preferred_element_type=F32),
            top,
            sm0[0] * keep + jnp.sum(weight, axis=1, keepdims=True),
        )

    def put(total, top, mass):
        if last:
            acc[...], mx[...], sm[...] = total, top, mass
        else:
            acc_out[0], mx_out[0], sm_out[0] = total, top, mass

    @pl.when(size > 512)
    def _():
        chunk(1024)

    @pl.when((size > 128) & (size <= 512))
    def _():
        chunk(512)

    @pl.when((size > 0) & (size <= 128))
    def _():
        chunk(128)

    @pl.when(size <= 0)
    def _():
        put(acc0[0], mx0[0], sm0[0])

    if not last:
        return
    lane16 = iota((16, 128), 1)
    stats = jnp.zeros((16, 128), F32)
    heads = []
    for j in range(HEADS):
        at = slice(j * TOK, (j + 1) * TOK)
        mass = sm[at, :]
        none = mass == 0.0
        safe = jnp.where(none, 1.0, mass)
        lse = jnp.where(none, -BIG, mx[at, :] * SCALE + jnp.log(safe))
        latent = (acc[at, :] * wide(1.0 / safe, 512)).astype(BF)
        heads.append(jnp.dot(latent, va_ref[j], preferred_element_type=F32).astype(BF))
        one = lse.astype(BF).astype(F32)
        two = (lse - one).astype(BF).astype(F32)
        three = lse - one - two
        for k in range(TOK // 16):
            base = 12 * k + 3 * j
            cut = slice(k * 16, (k + 1) * 16)
            for i, value in enumerate((one, two, three)):
                stats = jnp.where(lane16 == base + i, value[cut], stats)

    for i, out_ref in enumerate(outs):

        @pl.when(step == i)
        def _():
            for j in range(HEADS):
                out_ref[0:TOK, j * 128 : (j + 1) * 128] = heads[j]
            out_ref[TOK : TOK + STAT, 0:128] = stats.astype(BF)
            out_ref[TOK : TOK + STAT, 128:512] = jnp.zeros((STAT, 384), BF)


def merge(got):
    lane_in = iota((128, 512), 0)
    lane_head = iota((128, 512), 1) // 128
    outs = []
    stats = jnp.concatenate([got[c][TOK : TOK + STAT, 0:128] for c in range(4)], axis=0)
    for k in range(TOK // 16):
        pickup = ((lane_in >= 12 * k + 3 * lane_head) & (lane_in < 12 * k + 3 * lane_head + 3))
        lse = jnp.dot(stats, pickup.astype(BF), preferred_element_type=F32)
        lse = [lse[c * 16 : (c + 1) * 16] for c in range(4)]
        top = jnp.maximum(jnp.maximum(lse[0], lse[1]), jnp.maximum(lse[2], lse[3]))
        weight = [jnp.exp(v - top) for v in lse]
        total = weight[0] + weight[1] + weight[2] + weight[3]
        mixed = sum(
            weight[c] * got[c][k * 16 : (k + 1) * 16, :].astype(F32) for c in range(4)
        )
        outs.append((mixed / total).astype(BF))
    return outs


def fetch(ids, w_ref, held, sem, picks):
    copies = []
    for i, (turn, other) in enumerate(picks):
        y = ((ids[2] >> 1) + turn) & 3
        column = (y * 2 + ((ids[2] & 1) ^ other)) * 896
        copies.append(
            pltpu.make_async_copy(
                w_ref.at[:, pl.ds(pl.multiple_of(column, 128), 896)], held.at[i], sem.at[i]
            )
        )
        copies[-1].start()
    return copies


def first_kernel(ids, g0, g1, g2, g3, w_ref, head_ref, away_ref, home_ref, held, sem):
    copies = fetch(ids, w_ref, held, sem, ((2, 1), (2, 0)))
    for k, value in enumerate(merge((g0, g1, g2, g3))):
        head_ref[k * 16 : (k + 1) * 16, :] = value
    for i, out in enumerate((away_ref, home_ref)):
        copies[i].wait()
        out[...] = jnp.dot(head_ref[...], held[i], preferred_element_type=F32).astype(BF)


def rest_kernel(other, ids, head_ref, w_ref, out_ref, held, sem):
    copies = fetch(ids, w_ref, held, sem, ((1, other), (3, other), (0, other)))
    for i in range(3):
        copies[i].wait()
        out_ref[i] = jnp.dot(head_ref[...], held[i], preferred_element_type=F32).astype(BF)


def shift(value, axis, by, size):
    return lax.ppermute(value, axis, [(i, (i + by) % size) for i in range(size)])


def swap_core(value):
    return lax.ppermute(value, "head", [(i, i ^ 1) for i in range(8)])


def whole(*shape):
    return pl.BlockSpec(shape, lambda i, *_: (0,) * len(shape))


def prepare(ids, hit_holder, prior_blocks, new_counts, queries, key_absorb, new_latent):
    rows = HEADS * TOK
    tile = lambda n: pl.BlockSpec((1, rows, n), lambda i, *_: (i, 0, 0))
    return pl.pallas_call(
        ready_kernel,
        grid_spec=pltpu.PrefetchScalarGridSpec(
            num_scalar_prefetch=4,
            grid=(4,),
            in_specs=[
                whole(TOK, 768), whole(TOK, 768), whole(TOK, 768), whole(80, 768), whole(80, 768),
                whole(HEADS, 128, 512),
                whole(80, WIDE2),
            ],
            out_specs=[
                tile(KW), tile(512), tile(128), tile(128),
                whole(2 * KEYS, 128),
                pl.BlockSpec(memory_space=pltpu.SMEM),
            ],
            scratch_shapes=[
                pltpu.VMEM((TOK, 768), BF),
                pltpu.VMEM((256, KW), BF),
                pltpu.SMEM((8,), jnp.int32),
            ],
        ),
        out_shape=[
            pltpu.HBM((4, rows, KW), BF),
            pltpu.HBM((4, rows, 512), F32),
            pltpu.HBM((4, rows, 128), F32),
            pltpu.HBM((4, rows, 128), F32),
            pltpu.HBM((2 * KEYS, 128), BF),
            jax.ShapeDtypeStruct((32,), jnp.int32),
        ],
        compiler_params=pltpu.CompilerParams(vmem_limit_bytes=28 * 2**20),
        cost_estimate=pl.CostEstimate(
            flops=3 * 10**9, bytes_accessed=14 * 10**6, transcendentals=10**6
        ),
        name="prepare",
    )(ids, hit_holder, prior_blocks, new_counts, *queries, key_absorb, new_latent)


ORDER = (0, 3, 1, 2)


def attend(ids, ready, turns, loads, pieces, value_absorb=None):
    q_all, acc0, mx0, sm0, marks = [
        pltpu.with_memory_space_constraint(value, pltpu.HBM) for value in ready[:5]
    ]
    table = ready[5]
    rows = HEADS * TOK
    last = value_absorb is not None
    places = [ORDER.index(turn) for turn in turns]

    def at(i, *_):
        place = places[-1]
        for k in range(len(places) - 2, -1, -1):
            place = jnp.where(i == k, places[k], place)
        return (place, 0, 0)

    tile = lambda n: pl.BlockSpec((1, rows, n), at)
    hbm = pl.BlockSpec(memory_space=pl.ANY)
    if last:
        out_specs = [whole(TOK + STAT, 512)] * len(turns)
        out_shape = [jax.ShapeDtypeStruct((TOK + STAT, 512), BF)] * len(turns)
    else:
        out_specs = [tile(512), tile(128), tile(128)]
        out_shape = [pltpu.HBM((4, rows, n), F32) for n in (512, 128, 128)]
    return pl.pallas_call(
        partial(attend_kernel, turns, loads, last),
        grid_spec=pltpu.PrefetchScalarGridSpec(
            num_scalar_prefetch=2,
            grid=(len(turns),),
            in_specs=[tile(KW), tile(512), tile(128), tile(128)]
            + [whole(HEADS, 512, 128)] * last
            + [hbm] * (1 + len(pieces)),
            out_specs=out_specs,
            scratch_shapes=[
                pltpu.VMEM((2, 8, 32, WIDE2), BF),
                pltpu.VMEM((2 * KEYS, KW), BF),
                pltpu.SemaphoreType.DMA((3,)),
            ]
            + [pltpu.VMEM((rows, n), F32) for n in (128, 128, 512)] * last,
        ),
        out_shape=out_shape,
        compiler_params=pltpu.CompilerParams(vmem_limit_bytes=32 * 2**20),
        cost_estimate=pl.CostEstimate(
            flops=2 * 10**9 * len(turns),
            bytes_accessed=5 * 10**6 * len(turns),
            transcendentals=10**6,
        ),
        name="attend_last" if last else "attend_first",
    )(
        ids, table, q_all, acc0, mx0, sm0, *([value_absorb] * last), marks, *pieces
    )


def rest(other, ids, heads, out_weight):
    return pl.pallas_call(
        partial(rest_kernel, other),
        grid_spec=pltpu.PrefetchScalarGridSpec(
            num_scalar_prefetch=1,
            grid=(1,),
            in_specs=[whole(TOK, 512), pl.BlockSpec(memory_space=pl.ANY)],
            out_specs=whole(3, TOK, 896),
            scratch_shapes=[pltpu.VMEM((3, 512, 896), BF), pltpu.SemaphoreType.DMA((3,))],
        ),
        out_shape=jax.ShapeDtypeStruct((3, TOK, 896), BF),
        compiler_params=pltpu.CompilerParams(vmem_limit_bytes=12 * 2**20),
        cost_estimate=pl.CostEstimate(
            flops=1 * 10**9, bytes_accessed=4 * 10**6, transcendentals=0
        ),
        name="project_home" if other == 0 else "project_away",
    )(ids, heads, out_weight)


def local(
    query_nope, query_rope, new_latent, cache_pool, hit_holder, hit_block,
    prior_blocks, new_counts, key_absorb, value_absorb, out_weight,
):
    ids = jnp.stack(
        [lax.axis_index("pool"), lax.axis_index("ctx"), lax.axis_index("head")]
    ).astype(jnp.int32)

    half = 32 * WIDE2
    prior = prior_blocks.T
    counts = new_counts.T
    picked, queries = pl.pallas_call(
        pick_kernel,
        grid_spec=pltpu.PrefetchScalarGridSpec(
            num_scalar_prefetch=2,
            grid=(1,),
            in_specs=[
                pl.BlockSpec((16, half), lambda i, ids, _: (0, (ids[2] >> 1) & 1)),
                whole(8, 64),
                whole(8, 64),
                whole(TOK, 512),
                whole(TOK, 256),
            ],
            out_specs=[whole(8, 32, WIDE2), whole(TOK, 768)],
        ),
        out_shape=[
            jax.ShapeDtypeStruct((8, 32, WIDE2), BF),
            jax.ShapeDtypeStruct((TOK, 768), BF),
        ],
        name="pick_blocks",
    )(ids, prior, cache_pool, hit_holder, hit_block, query_nope, query_rope)

    qm = shift(queries, "ctx", 1, 4)
    qp = shift(queries, "ctx", -1, 4)
    qx = shift(qm[:80], "ctx", 1, 4)
    qy = shift(qp[80:], "ctx", -1, 4)

    a0 = lax.all_to_all(picked, "pool", split_axis=0, concat_axis=0, tiled=True)

    ready = prepare(
        ids, hit_holder, prior, counts, (queries, qm, qp, qx, qy), key_absorb, new_latent
    )
    table, a0 = lax.optimization_barrier((ready[5], a0))
    ready = (*ready[:5], table)
    am = shift(a0[:4], "head", 2, 8)
    ap = shift(a0[4:], "head", -2, 8)
    b0 = swap_core(a0)
    state = attend(ids, ready, ORDER, ((0, 0, 8), (1, 0, 8)), (a0, b0))
    acc, am, ap = lax.optimization_barrier((state[1], am, ap))
    state = (state[0], acc, state[2])
    ready = (ready[0], *state, ready[4], table)
    bm = swap_core(am)
    bp = swap_core(ap)
    loads = ((0, 0, 4), (0, 4, 4), (1, 0, 4), (1, 4, 4))
    pieces = (am, ap, bm, bp)
    to_far, to_low = attend(ids, ready, (2, 3), loads, pieces, value_absorb)
    from_far = shift(to_far, "ctx", 2, 4)
    from_high_ctx = shift(to_low, "ctx", -1, 4)
    to_high, kept = attend(ids, ready, (1, 0), loads, pieces, value_absorb)
    from_low_ctx = shift(to_high, "ctx", 1, 4)

    heads, away2, home2 = pl.pallas_call(
        first_kernel,
        grid_spec=pltpu.PrefetchScalarGridSpec(
            num_scalar_prefetch=1,
            grid=(1,),
            in_specs=[whole(TOK + STAT, 512)] * 4 + [pl.BlockSpec(memory_space=pl.ANY)],
            out_specs=[whole(TOK, 512), whole(TOK, 896), whole(TOK, 896)],
            scratch_shapes=[pltpu.VMEM((2, 512, 896), BF), pltpu.SemaphoreType.DMA((2,))],
        ),
        out_shape=[
            jax.ShapeDtypeStruct((TOK, 512), BF),
            jax.ShapeDtypeStruct((TOK, 896), BF),
            jax.ShapeDtypeStruct((TOK, 896), BF),
        ],
        compiler_params=pltpu.CompilerParams(vmem_limit_bytes=12 * 2**20),
        name="merge_project",
    )(ids, kept, from_low_ctx, from_high_ctx, from_far, out_weight)
    across = swap_core(away2)
    away = rest(1, ids, heads, out_weight)
    arrived = swap_core(away)
    opposite = (home2.astype(F32) + across.astype(F32)).astype(BF)
    from_low = shift(opposite[:80], "head", 2, 8)
    from_high = shift(opposite[80:], "head", -2, 8)
    home = rest(0, ids, heads, out_weight)
    both = home.astype(F32) + arrived.astype(F32)
    up = jnp.concatenate([both[0, :80] + from_low.astype(F32), both[0, 80:]], axis=0).astype(BF)
    down = jnp.concatenate([both[1, :80], both[1, 80:] + from_high.astype(F32)], axis=0).astype(BF)
    got_up = shift(up, "head", 2, 8)
    got_down = shift(down, "head", -2, 8)
    return (both[2] + got_up.astype(F32) + got_down.astype(F32)).astype(BF)


def solution(mesh):
    return jax.shard_map(
        local,
        mesh=mesh,
        in_specs=(
            P(("pool", "ctx"), "head"),
            P(("pool", "ctx"), "head"),
            P(("pool", "ctx"), None),
            P(("pool", "ctx"), None),
            P(),
            P(),
            P(),
            P(),
            P("head", None, None),
            P("head", None, None),
            P("head", None),
        ),
        out_specs=P(("pool", "ctx"), "head"),
        check_vma=False,
    )
```

```python
from functools import partial

import jax
import jax.numpy as jnp
from jax import lax
from jax.experimental import pallas as pl
from jax.experimental.pallas import tpu as pltpu
from jax.sharding import PartitionSpec as P

KV_RANK = 512
ROPE = 64
QK_NOPE = 128
VD = 128
BLK = 128
PAIRS = BLK // 2
WIDE2 = 2 * (KV_RANK + ROPE)
HEADS = 4
TOK = 160
SLOTS = 16
KEYS = SLOTS * BLK
CUT = 96
KW = 768
BIG = 2.0**100
SCALE = (QK_NOPE + ROPE) ** (-0.5)
LOG2E = 1.4426950408889634
BF = jnp.bfloat16
F32 = jnp.float32
STAT = 16
ORDER = (0, 3, 1, 2)


def iota(shape, dim):
    return lax.broadcasted_iota(jnp.int32, shape, dim)


def pick_kernel(
    ids, prior, cache_ref, holder_ref, block_ref, nope_ref, rope_ref, out_ref, query_ref
):
    query_ref[:, 0:512] = nope_ref[...]
    query_ref[:, 512:768] = rope_ref[...]
    me = ids[0] * 4 + ids[1]
    core = ids[2] & 1
    lane = iota((8, 64), 1)
    group = iota((8, 64), 0)
    count = jnp.zeros((8, 64), jnp.int32)
    for g in range(8):
        count = jnp.where(group == g, prior[0, g] + prior[1, g], count)
    match = (holder_ref[...] == me) & (lane < count)
    first = jnp.min(jnp.where(match, lane, 1000), axis=1, keepdims=True)
    last = jnp.max(jnp.where(match, lane, -1), axis=1, keepdims=True)
    wanted = jnp.where(core == 0, first, jnp.where(last > first, last, -2))
    chosen = match & (lane == wanted)
    index = jnp.sum(jnp.where(chosen, block_ref[...] + 1, 0), axis=1, keepdims=True) - 1
    spread = (iota((128, 8), 0) // 16 == iota((128, 8), 1)).astype(BF)
    rows_index = jnp.dot(
        spread,
        jnp.broadcast_to(index.astype(F32), (8, 256)).astype(BF),
        preferred_element_type=F32,
    )
    row = iota((128, 256), 0)
    col = iota((128, 256), 1)
    onehot = ((col // 16 == row % 16) & ((col % 16).astype(F32) == rows_index)).astype(BF)
    for part in range(2):
        stacked = jnp.concatenate(
            [
                cache_ref[:, p * WIDE2 : (p + 1) * WIDE2]
                for p in range(part * 16, part * 16 + 16)
            ],
            axis=0,
        )
        out = jnp.dot(onehot, stacked, preferred_element_type=F32).astype(BF)
        even, odd, rope = align(out)
        to = slice(part * 16, part * 16 + 16)
        for g in range(8):
            at = slice(g * 16, (g + 1) * 16)
            for j in range(4):
                out_ref[g, to, j * 128 : (j + 1) * 128] = even[j][at]
                out_ref[g, to, 512 + j * 128 : 640 + j * 128] = odd[j][at]
            out_ref[g, to, 1024:1152] = rope[at]


def align(rows):
    low = iota((rows.shape[0], 128), 1) < 64
    tile = [rows[:, j * 128 : (j + 1) * 128] for j in range(9)]
    flip = {j: pltpu.roll(tile[j].astype(F32), 64, 1).astype(BF) for j in range(5, 9)}
    flip[4] = pltpu.roll(tile[4].astype(F32), 64, 1).astype(BF)
    odd = [jnp.where(low, flip[4 + j], flip[5 + j]) for j in range(4)]
    return tile[:4], odd, jnp.where(low, tile[4], tile[8])


def both_ropes(tile):
    low = iota(tile.shape, 1) < 64
    flip = pltpu.roll(tile.astype(F32), 64, 1).astype(BF)
    return jnp.where(low, tile, flip), jnp.where(low, flip, tile)


def wide(value, n):
    return jnp.concatenate([value] * (n // 128), axis=1)


def turn_of(step):
    return jnp.where(step == 0, 0, jnp.where(step == 1, 3, jnp.where(step == 2, 1, 2)))


def product(queries, keys):
    return lax.dot_general(
        queries, keys, (((1,), (1,)), ((), ())), preferred_element_type=F32
    )


def ready_kernel(
    ids, holder, prior, counts,
    q0, qm, qp, qx, qy, ka_ref, nl_ref,
    q_out, acc_out, mx_out, sm_out, mark_out, table,
    part, kn, seen,
):
    step = pl.program_id(0)
    group = ids[0]
    ctx = ids[1]
    n0 = counts[0, group]

    def mark(n, base, keys0, keys1):
        row = iota((n, 128), 0) + base
        lane = iota((n, 128), 1)
        miss0 = (lane == 0) & jnp.logical_not(keys0(row))
        miss1 = (lane == 1) & jnp.logical_not(keys1(row))
        return jnp.where(miss0 | miss1, -BIG, 0.0).astype(BF)

    @pl.when(step == 0)
    def _():
        for i in range(SLOTS):
            table[i] = -1
        for i in range(8):
            seen[i] = 0
        own = prior[0, group]
        total = own + prior[1, group]

        def entry(e, carry):
            filled, mine = carry
            where = holder[group, e]
            hit = (where & 3) == ctx
            p = where >> 2

            @pl.when(hit)
            def _():
                s = seen[p]
                seen[p] = s + 1
                table[p * 2 + s] = filled

            add = hit.astype(jnp.int32)
            return filled + add, mine + jnp.where(e < own, add, 0)

        filled, mine = lax.fori_loop(0, total, entry, (jnp.int32(0), jnp.int32(0)))
        end0 = mine * BLK
        end1 = filled * BLK
        table[SLOTS] = end0
        table[SLOTS + 1] = end1
        table[SLOTS + 2] = n0
        for i in range(SLOTS + 3, 32):
            table[i] = 0
        for i in range(SLOTS):
            dead = table[i] < 0

            @pl.when(dead)
            def _():
                table[i] = filled

            filled = filled + dead.astype(jnp.int32)

        def marks(i, _):
            at = pl.multiple_of(i * BLK, BLK)
            mark_out[pl.ds(at, BLK), :] = mark(
                BLK, at, lambda r: r < end0, lambda r: (r >= end0) & (r < end1)
            )
            return 0

        lax.fori_loop(0, SLOTS, marks, 0)

        even, odd, rope = align(nl_ref[...])
        rope = both_ropes(rope)
        kn[...] = jnp.zeros(kn.shape, BF)
        for parity, latent in enumerate((even, odd)):
            at = slice(parity * 128, parity * 128 + 80)
            for j in range(4):
                kn[at, j * 128 : (j + 1) * 128] = latent[j]
            kn[at, 512:640] = rope[parity]

        def new_position(row):
            return ctx * TOK + 2 * (row & 127) + (row >> 7)

        kn[:, 640:768] = mark(
            256, 0, lambda r: new_position(r) < n0, lambda r: new_position(r) >= n0
        )
        part[...] = q0[...]

    @pl.when(step == 1)
    def _():
        part[...] = qm[...]

    @pl.when(step == 2)
    def _():
        part[...] = qp[...]

    @pl.when(step == 3)
    def _():
        part[0:80] = qx[...]
        part[80:160] = qy[...]

    rows = HEADS * TOK
    t0 = ((ctx + turn_of(step)) & 3) * TOK
    lane = iota((TOK, 128), 1)
    token = iota((TOK, 128), 0) + t0
    flags = jnp.where(
        ((lane == 0) & (token < n0)) | ((lane == 1) & (token >= n0)), 1.0, 0.0
    ).astype(BF)
    for j in range(HEADS):
        at = slice(j * TOK, (j + 1) * TOK)
        q_out[0, at, 0:512] = jnp.dot(
            part[:, j * 128 : (j + 1) * 128], ka_ref[j], preferred_element_type=F32
        ).astype(BF)
        rope = part[:, 512 + (j // 2) * 128 : 640 + (j // 2) * 128]
        keep = lane < 64 if j % 2 == 0 else lane >= 64
        q_out[0, at, 512:640] = jnp.where(keep, rope, jnp.zeros_like(rope))
        q_out[0, at, 640:768] = flags

    visible = t0 + TOK > ctx * TOK

    @pl.when(visible)
    def _():
        key = iota((rows, 256), 1)
        position = ctx * TOK + 2 * (key & 127) + (key >> 7)
        here = jnp.concatenate([iota((TOK, 256), 0)] * HEADS, axis=0) + t0
        seen_keys = (position <= here) & ((key & 127) < 80)
        scores = jnp.where(seen_keys, product(q_out[0], kn[...]), -BIG)
        top = jnp.maximum(
            jnp.full((rows, 128), -BIG, F32), jnp.max(scores, axis=1, keepdims=True)
        )
        weight = jnp.exp2((scores - wide(top, 256)) * (SCALE * LOG2E))
        mx_out[0] = top
        sm_out[0] = jnp.zeros((rows, 128), F32) + jnp.sum(weight, axis=1, keepdims=True)
        acc_out[0] = jnp.dot(weight.astype(BF), kn[:, 0:512], preferred_element_type=F32)

    @pl.when(jnp.logical_not(visible))
    def _():
        mx_out[0] = jnp.full((rows, 128), -BIG, F32)
        sm_out[0] = jnp.zeros((rows, 128), F32)
        acc_out[0] = jnp.zeros((rows, 512), F32)


def attend_kernel(
    ids, table,
    q_ref, acc0, mx0, sm0, va_ref, mark_ref, a0, am, ap, b0, bm, bp,
    far_a, far_b, low_ref, high_ref, kept_ref,
    kc, kb, acc, mx, sm, sem,
):
    step = pl.program_id(0)
    core = ids[2] & 1
    end0 = table[SLOTS]
    end1 = table[SLOTS + 1]
    n0 = table[SLOTS + 2]

    @pl.when(step == 0)
    def _():
        marks = pltpu.make_async_copy(mark_ref, kb.at[:, pl.ds(640, 128)], sem.at[2])
        marks.start()
        for w, (own, first, second) in enumerate(((a0, am, ap), (b0, bm, bp))):
            pltpu.make_async_copy(own, kc.at[w, 0], sem.at[w]).start()
            pltpu.make_async_copy(first, kc.at[w, 1, pl.ds(0, 4)], sem.at[w]).start()
            pltpu.make_async_copy(second, kc.at[w, 1, pl.ds(4, 4)], sem.at[w]).start()
        for w in range(2):
            pltpu.make_async_copy(kc.at[w], kc.at[w], sem.at[w]).wait()
            slot = core if w == 0 else 1 - core

            def shape_up(p, _):
                at = table[p * 2 + slot] * BLK
                for half in range(2):
                    block = kc[w, half, p]
                    ropes = both_ropes(block[:, 1024:1152])
                    for parity in range(2):
                        to = pl.ds(pl.multiple_of(at + half * 64 + parity * 32, 32), 32)
                        kb[to, 0:512] = block[:, parity * 512 : parity * 512 + 512]
                        kb[to, 512:640] = ropes[parity]
                return 0

            lax.fori_loop(0, 8, shape_up, 0)
        marks.wait()

    t0 = ((ids[1] + turn_of(step)) & 3) * TOK
    low = jnp.where(t0 < n0, 0, end0)
    high = jnp.where(t0 + TOK > n0, end1, end0)
    extent = high - low

    def chunk(size):
        at = pl.ds(pl.multiple_of(jnp.minimum(low, KEYS - size), BLK), size)
        scores = product(q_ref[0], kb[at, :])
        before = mx0[0]
        top = jnp.maximum(before, jnp.max(scores, axis=1, keepdims=True))
        keep = jnp.exp2((before - top) * (SCALE * LOG2E))
        weight = jnp.exp2((scores - wide(top, size)) * (SCALE * LOG2E))
        mx[...] = top
        sm[...] = sm0[0] * keep + jnp.sum(weight, axis=1, keepdims=True)
        acc[...] = acc0[0] * wide(keep, 512) + jnp.dot(
            weight.astype(BF), kb[at, 0:512], preferred_element_type=F32
        )

    sizes = (0, 128, 512, 1024, 1536, 2048)
    for small, size in zip(sizes, sizes[1:]):

        @pl.when((extent > small) & (extent <= size))
        def _():
            chunk(size)

    @pl.when(extent <= 0)
    def _():
        acc[...], mx[...], sm[...] = acc0[0], mx0[0], sm0[0]

    lane16 = iota((16, 128), 1)
    stats = jnp.zeros((16, 128), F32)
    heads = []
    for j in range(HEADS):
        at = slice(j * TOK, (j + 1) * TOK)
        mass = sm[at, :]
        none = mass == 0.0
        safe = jnp.where(none, 1.0, mass)
        lse = jnp.where(none, -BIG, mx[at, :] * SCALE + jnp.log(safe))
        latent = (acc[at, :] * wide(1.0 / safe, 512)).astype(BF)
        heads.append(jnp.dot(latent, va_ref[j], preferred_element_type=F32).astype(BF))
        one = lse.astype(BF).astype(F32)
        two = (lse - one).astype(BF).astype(F32)
        three = lse - one - two
        for k in range(TOK // 16):
            base = 12 * k + 3 * j
            cut = slice(k * 16, (k + 1) * 16)
            for i, value in enumerate((one, two, three)):
                stats = jnp.where(lane16 == base + i, value[cut], stats)

    def emit(out_ref, first, count):
        for j in range(HEADS):
            out_ref[0:count, j * 128 : (j + 1) * 128] = heads[j][first : first + count]
        if first + count == TOK:
            out_ref[count : count + STAT, 0:128] = stats.astype(BF)
            out_ref[count : count + STAT, 128:512] = jnp.zeros((STAT, 384), BF)

    for turn, parts in (
        (0, ((kept_ref, 0, TOK),)),
        (1, ((high_ref, 0, TOK),)),
        (2, ((far_a, 0, CUT), (far_b, CUT, TOK - CUT))),
        (3, ((low_ref, 0, TOK),)),
    ):

        @pl.when(step == ORDER.index(turn))
        def _():
            for part in parts:
                emit(*part)


def merge(kept, low, high, far_a, far_b):
    lane_in = iota((128, 512), 0)
    lane_head = iota((128, 512), 1) // 128
    outs = []
    tails = [ref[TOK : TOK + STAT, 0:128] for ref in (kept, low, high)]
    stats = jnp.concatenate([*tails, far_b[TOK - CUT : TOK - CUT + STAT, 0:128]], axis=0)
    for k in range(TOK // 16):
        pickup = ((lane_in >= 12 * k + 3 * lane_head) & (lane_in < 12 * k + 3 * lane_head + 3))
        lse = jnp.dot(stats, pickup.astype(BF), preferred_element_type=F32)
        lse = [lse[c * 16 : (c + 1) * 16] for c in range(4)]
        top = jnp.maximum(jnp.maximum(lse[0], lse[1]), jnp.maximum(lse[2], lse[3]))
        weight = [jnp.exp(v - top) for v in lse]
        total = weight[0] + weight[1] + weight[2] + weight[3]
        at = slice(k * 16, (k + 1) * 16)
        far = far_a[at, :] if k * 16 < CUT else far_b[k * 16 - CUT : k * 16 - CUT + 16, :]
        values = (kept[at, :], low[at, :], high[at, :], far)
        mixed = sum(w * v.astype(F32) for w, v in zip(weight, values))
        outs.append((mixed / total).astype(BF))
    return outs


def fetch(ids, w_ref, held, sem, picks):
    copies = []
    for i, (turn, other) in enumerate(picks):
        y = ((ids[2] >> 1) + turn) & 3
        column = (y * 2 + ((ids[2] & 1) ^ other)) * 896
        copies.append(
            pltpu.make_async_copy(
                w_ref.at[:, pl.ds(pl.multiple_of(column, 128), 896)], held.at[i], sem.at[i]
            )
        )
        copies[-1].start()
    return copies


def first_kernel(ids, g0, g1, g2, g3, g4, w_ref, head_ref, away_ref, home_ref, held, sem):
    copies = fetch(ids, w_ref, held, sem, ((2, 1), (2, 0)))
    for k, value in enumerate(merge(g0, g1, g2, g3, g4)):
        head_ref[k * 16 : (k + 1) * 16, :] = value
    for i, out in enumerate((away_ref, home_ref)):
        copies[i].wait()
        out[...] = jnp.dot(head_ref[...], held[i], preferred_element_type=F32).astype(BF)


def rest_kernel(other, ids, head_ref, w_ref, out_ref, held, sem):
    copies = fetch(ids, w_ref, held, sem, ((1, other), (3, other), (0, other)))
    for i in range(3):
        copies[i].wait()
        out_ref[i] = jnp.dot(head_ref[...], held[i], preferred_element_type=F32).astype(BF)


def shift(value, axis, by, size):
    return lax.ppermute(value, axis, [(i, (i + by) % size) for i in range(size)])


def swap_core(value):
    return lax.ppermute(value, "head", [(i, i ^ 1) for i in range(8)])


def whole(*shape):
    return pl.BlockSpec(shape, lambda i, *_: (0,) * len(shape))


def prepare(ids, hit_holder, prior_blocks, new_counts, queries, key_absorb, new_latent):
    rows = HEADS * TOK
    tile = lambda n: pl.BlockSpec((1, rows, n), lambda i, *_: (i, 0, 0))
    return pl.pallas_call(
        ready_kernel,
        grid_spec=pltpu.PrefetchScalarGridSpec(
            num_scalar_prefetch=4,
            grid=(4,),
            in_specs=[
                whole(TOK, 768), whole(TOK, 768), whole(TOK, 768), whole(80, 768), whole(80, 768),
                whole(HEADS, 128, 512),
                whole(80, WIDE2),
            ],
            out_specs=[
                tile(KW), tile(512), tile(128), tile(128),
                whole(KEYS, 128),
                pl.BlockSpec(memory_space=pltpu.SMEM),
            ],
            scratch_shapes=[
                pltpu.VMEM((TOK, 768), BF),
                pltpu.VMEM((256, KW), BF),
                pltpu.SMEM((8,), jnp.int32),
            ],
        ),
        out_shape=[
            pltpu.HBM((4, rows, KW), BF),
            pltpu.HBM((4, rows, 512), F32),
            pltpu.HBM((4, rows, 128), F32),
            pltpu.HBM((4, rows, 128), F32),
            pltpu.HBM((KEYS, 128), BF),
            jax.ShapeDtypeStruct((32,), jnp.int32),
        ],
        compiler_params=pltpu.CompilerParams(vmem_limit_bytes=28 * 2**20),
        cost_estimate=pl.CostEstimate(
            flops=3 * 10**9, bytes_accessed=14 * 10**6, transcendentals=10**6
        ),
        name="prepare",
    )(ids, hit_holder, prior_blocks, new_counts, *queries, key_absorb, new_latent)


def attend(ids, ready, pieces, value_absorb):
    q_all, acc0, mx0, sm0, marks = [
        pltpu.with_memory_space_constraint(value, pltpu.HBM) for value in ready[:5]
    ]
    rows = HEADS * TOK
    tile = lambda n: pl.BlockSpec((1, rows, n), lambda i, *_: (i, 0, 0))
    out_rows = (CUT, TOK - CUT + STAT, TOK + STAT, TOK + STAT, TOK + STAT)
    return pl.pallas_call(
        attend_kernel,
        grid_spec=pltpu.PrefetchScalarGridSpec(
            num_scalar_prefetch=2,
            grid=(4,),
            in_specs=[tile(KW), tile(512), tile(128), tile(128), whole(HEADS, 512, 128)]
            + [pl.BlockSpec(memory_space=pl.ANY)] * 7,
            out_specs=[whole(n, 512) for n in out_rows],
            scratch_shapes=[
                pltpu.VMEM((2, 2, 8, 32, WIDE2), BF),
                pltpu.VMEM((KEYS, KW), BF),
                pltpu.VMEM((rows, 512), F32),
                pltpu.VMEM((rows, 128), F32),
                pltpu.VMEM((rows, 128), F32),
                pltpu.SemaphoreType.DMA((3,)),
            ],
        ),
        out_shape=[jax.ShapeDtypeStruct((n, 512), BF) for n in out_rows],
        compiler_params=pltpu.CompilerParams(vmem_limit_bytes=40 * 2**20),
        cost_estimate=pl.CostEstimate(
            flops=12 * 10**9, bytes_accessed=15 * 10**6, transcendentals=5 * 10**6
        ),
        name="attend",
    )(ids, ready[5], q_all, acc0, mx0, sm0, value_absorb, marks, *pieces)


def rest(other, ids, heads, out_weight):
    return pl.pallas_call(
        partial(rest_kernel, other),
        grid_spec=pltpu.PrefetchScalarGridSpec(
            num_scalar_prefetch=1,
            grid=(1,),
            in_specs=[whole(TOK, 512), pl.BlockSpec(memory_space=pl.ANY)],
            out_specs=whole(3, TOK, 896),
            scratch_shapes=[pltpu.VMEM((3, 512, 896), BF), pltpu.SemaphoreType.DMA((3,))],
        ),
        out_shape=jax.ShapeDtypeStruct((3, TOK, 896), BF),
        compiler_params=pltpu.CompilerParams(vmem_limit_bytes=12 * 2**20),
        cost_estimate=pl.CostEstimate(
            flops=1 * 10**9, bytes_accessed=4 * 10**6, transcendentals=0
        ),
        name="project_home" if other == 0 else "project_away",
    )(ids, heads, out_weight)


def local(
    query_nope, query_rope, new_latent, cache_pool, hit_holder, hit_block,
    prior_blocks, new_counts, key_absorb, value_absorb, out_weight,
):
    ids = jnp.stack(
        [lax.axis_index("pool"), lax.axis_index("ctx"), lax.axis_index("head")]
    ).astype(jnp.int32)

    half = 32 * WIDE2
    prior = prior_blocks.T
    counts = new_counts.T
    picked, queries = pl.pallas_call(
        pick_kernel,
        grid_spec=pltpu.PrefetchScalarGridSpec(
            num_scalar_prefetch=2,
            grid=(1,),
            in_specs=[
                pl.BlockSpec((16, half), lambda i, ids, _: (0, (ids[2] >> 1) & 1)),
                whole(8, 64),
                whole(8, 64),
                whole(TOK, 512),
                whole(TOK, 256),
            ],
            out_specs=[whole(8, 32, WIDE2), whole(TOK, 768)],
        ),
        out_shape=[
            jax.ShapeDtypeStruct((8, 32, WIDE2), BF),
            jax.ShapeDtypeStruct((TOK, 768), BF),
        ],
        name="pick_blocks",
    )(ids, prior, cache_pool, hit_holder, hit_block, query_nope, query_rope)

    qm = shift(queries, "ctx", 1, 4)
    qp = shift(queries, "ctx", -1, 4)
    qx = shift(qm[:80], "ctx", 1, 4)
    qy = shift(qp[80:], "ctx", -1, 4)

    a0 = lax.all_to_all(picked, "pool", split_axis=0, concat_axis=0, tiled=True)

    a0, qx, qy = lax.optimization_barrier((a0, qx, qy))
    am = shift(a0[:4], "head", 2, 8)
    ap = shift(a0[4:], "head", -2, 8)
    b0 = swap_core(a0)
    ready = prepare(
        ids, hit_holder, prior, counts, (queries, qm, qp, qx, qy), key_absorb, new_latent
    )
    table, am, ap, b0 = lax.optimization_barrier((ready[5], am, ap, b0))
    bm = swap_core(am)
    bp = swap_core(ap)
    far_a, far_b, to_low, to_high, kept = attend(
        ids, (*ready[:5], table), (a0, am, ap, b0, bm, bp), value_absorb
    )
    far_b = shift(far_b, "ctx", -1, 4)
    far_a = shift(far_a, "ctx", 2, 4)
    from_low = shift(to_high, "ctx", 1, 4)
    from_high = shift(to_low, "ctx", -1, 4)
    far_b = shift(far_b, "ctx", -1, 4)

    heads, away2, home2 = pl.pallas_call(
        first_kernel,
        grid_spec=pltpu.PrefetchScalarGridSpec(
            num_scalar_prefetch=1,
            grid=(1,),
            in_specs=[whole(TOK + STAT, 512)] * 3
            + [whole(CUT, 512), whole(TOK - CUT + STAT, 512)]
            + [pl.BlockSpec(memory_space=pl.ANY)],
            out_specs=[whole(TOK, 512), whole(TOK, 896), whole(TOK, 896)],
            scratch_shapes=[pltpu.VMEM((2, 512, 896), BF), pltpu.SemaphoreType.DMA((2,))],
        ),
        out_shape=[
            jax.ShapeDtypeStruct((TOK, 512), BF),
            jax.ShapeDtypeStruct((TOK, 896), BF),
            jax.ShapeDtypeStruct((TOK, 896), BF),
        ],
        compiler_params=pltpu.CompilerParams(vmem_limit_bytes=12 * 2**20),
        name="merge_project",
    )(ids, kept, from_low, from_high, far_a, far_b, out_weight)
    across = swap_core(away2)
    opposite = home2.astype(F32) + across.astype(F32)
    part_a = opposite[:80].astype(BF)
    part_b = opposite[80:].astype(BF)
    heads, part_a, part_b = lax.optimization_barrier((heads, part_a, part_b))
    part_a = shift(part_a, "head", 2, 8)
    part_b = shift(part_b, "head", -2, 8)
    away = rest(1, ids, heads, out_weight)
    arrived = swap_core(away)
    home = rest(0, ids, heads, out_weight)
    both = home.astype(F32) + arrived.astype(F32)
    up = jnp.concatenate([both[0, :80] + part_a.astype(F32), both[0, 80:]], axis=0).astype(BF)
    down = jnp.concatenate([both[1, :80], both[1, 80:] + part_b.astype(F32)], axis=0).astype(BF)
    got_up = shift(up, "head", 2, 8)
    got_down = shift(down, "head", -2, 8)
    return (both[2] + got_up.astype(F32) + got_down.astype(F32)).astype(BF)


def solution(mesh):
    return jax.shard_map(
        local,
        mesh=mesh,
        in_specs=(
            P(("pool", "ctx"), "head"),
            P(("pool", "ctx"), "head"),
            P(("pool", "ctx"), None),
            P(("pool", "ctx"), None),
            P(),
            P(),
            P(),
            P(),
            P("head", None, None),
            P("head", None, None),
            P("head", None),
        ),
        out_specs=P(("pool", "ctx"), "head"),
        check_vma=False,
    )
```

```python
from functools import partial

import jax
import jax.numpy as jnp
from jax import lax
from jax.experimental import pallas as pl
from jax.experimental.pallas import tpu as pltpu
from jax.sharding import PartitionSpec as P

KV_RANK = 512
ROPE = 64
QK_NOPE = 128
VD = 128
BLK = 128
PAIRS = BLK // 2
WIDE2 = 2 * (KV_RANK + ROPE)
HEADS = 4
TOK = 160
SLOTS = 16
KEYS = SLOTS * BLK
KW = 768
BIG = 2.0**100
SCALE = (QK_NOPE + ROPE) ** (-0.5)
LOG2E = 1.4426950408889634
BF = jnp.bfloat16
F32 = jnp.float32
STAT = 16
ORDER = (0, 3, 1, 2)


def iota(shape, dim):
    return lax.broadcasted_iota(jnp.int32, shape, dim)


def pick_kernel(
    ids, prior, cache_ref, holder_ref, block_ref, nope_ref, rope_ref, out_ref, query_ref
):
    query_ref[:, 0:512] = nope_ref[...]
    query_ref[:, 512:768] = rope_ref[...]
    me = ids[0] * 4 + ids[1]
    core = ids[2] & 1
    lane = iota((8, 64), 1)
    group = iota((8, 64), 0)
    count = jnp.zeros((8, 64), jnp.int32)
    for g in range(8):
        count = jnp.where(group == g, prior[0, g] + prior[1, g], count)
    match = (holder_ref[...] == me) & (lane < count)
    first = jnp.min(jnp.where(match, lane, 1000), axis=1, keepdims=True)
    last = jnp.max(jnp.where(match, lane, -1), axis=1, keepdims=True)
    wanted = jnp.where(core == 0, first, jnp.where(last > first, last, -2))
    chosen = match & (lane == wanted)
    index = jnp.sum(jnp.where(chosen, block_ref[...] + 1, 0), axis=1, keepdims=True) - 1
    spread = (iota((128, 8), 0) // 16 == iota((128, 8), 1)).astype(BF)
    rows_index = jnp.dot(
        spread,
        jnp.broadcast_to(index.astype(F32), (8, 256)).astype(BF),
        preferred_element_type=F32,
    )
    row = iota((128, 256), 0)
    col = iota((128, 256), 1)
    onehot = ((col // 16 == row % 16) & ((col % 16).astype(F32) == rows_index)).astype(BF)
    for part in range(2):
        stacked = jnp.concatenate(
            [
                cache_ref[:, p * WIDE2 : (p + 1) * WIDE2]
                for p in range(part * 16, part * 16 + 16)
            ],
            axis=0,
        )
        out = jnp.dot(onehot, stacked, preferred_element_type=F32).astype(BF)
        even, odd, rope = align(out)
        to = slice(part * 16, part * 16 + 16)
        for g in range(8):
            at = slice(g * 16, (g + 1) * 16)
            for j in range(4):
                out_ref[g, to, j * 128 : (j + 1) * 128] = even[j][at]
                out_ref[g, to, 512 + j * 128 : 640 + j * 128] = odd[j][at]
            out_ref[g, to, 1024:1152] = rope[at]


def align(rows):
    low = iota((rows.shape[0], 128), 1) < 64
    tile = [rows[:, j * 128 : (j + 1) * 128] for j in range(9)]
    flip = {j: pltpu.roll(tile[j].astype(F32), 64, 1).astype(BF) for j in range(5, 9)}
    flip[4] = pltpu.roll(tile[4].astype(F32), 64, 1).astype(BF)
    odd = [jnp.where(low, flip[4 + j], flip[5 + j]) for j in range(4)]
    return tile[:4], odd, jnp.where(low, tile[4], tile[8])


def both_ropes(tile):
    low = iota(tile.shape, 1) < 64
    flip = pltpu.roll(tile.astype(F32), 64, 1).astype(BF)
    return jnp.where(low, tile, flip), jnp.where(low, flip, tile)


def wide(value, n):
    return jnp.concatenate([value] * (n // 128), axis=1)


def turn_of(step):
    return jnp.where(step == 0, 0, jnp.where(step == 1, 3, jnp.where(step == 2, 1, 2)))


def product(queries, keys):
    return lax.dot_general(
        queries, keys, (((1,), (1,)), ((), ())), preferred_element_type=F32
    )


def mark(n, base, keys0, keys1):
    row = iota((n, 128), 0) + base
    lane = iota((n, 128), 1)
    miss0 = (lane == 0) & jnp.logical_not(keys0(row))
    miss1 = (lane == 1) & jnp.logical_not(keys1(row))
    return jnp.where(miss0 | miss1, -BIG, 0.0).astype(BF)


def plan(ids, holder, prior, counts, mark_out, table, seen):
    group = ids[0]
    for i in range(SLOTS):
        table[i] = -1
    for i in range(8):
        seen[i] = 0
    own = prior[0, group]
    total = own + prior[1, group]

    def entry(e, carry):
        filled, mine = carry
        where = holder[group, e]
        hit = (where & 3) == ids[1]
        p = where >> 2

        @pl.when(hit)
        def _():
            s = seen[p]
            seen[p] = s + 1
            table[p * 2 + s] = filled

        add = hit.astype(jnp.int32)
        return filled + add, mine + jnp.where(e < own, add, 0)

    filled, mine = lax.fori_loop(0, total, entry, (jnp.int32(0), jnp.int32(0)))
    end0 = mine * BLK
    end1 = filled * BLK
    table[SLOTS] = end0
    table[SLOTS + 1] = end1
    table[SLOTS + 2] = counts[0, group]
    for i in range(SLOTS + 3, 32):
        table[i] = 0
    for i in range(SLOTS):
        dead = table[i] < 0

        @pl.when(dead)
        def _():
            table[i] = filled

        filled = filled + dead.astype(jnp.int32)

    def marks(i, _):
        at = pl.multiple_of(i * BLK, BLK)
        mark_out[pl.ds(at, BLK), :] = mark(
            BLK, at, lambda r: r < end0, lambda r: (r >= end0) & (r < end1)
        )
        return 0

    lax.fori_loop(0, SLOTS, marks, 0)


def ready_kernel(own, ids, holder, prior, counts, *refs):
    if own:
        q0, ka_ref, nl_ref, q_out, acc_out, mx_out, sm_out, mark_out, table, part, kn, seen = refs
    else:
        qm, qp, qx, qy, ka_ref, nl_ref = refs[:6]
        q_out, acc_out, mx_out, sm_out, part, kn = refs[10:]
    step = pl.program_id(0)
    ctx = ids[1]
    n0 = counts[0, ids[0]]

    @pl.when(step == 0)
    def _():
        if own:
            plan(ids, holder, prior, counts, mark_out, table, seen)
        even, odd, rope = align(nl_ref[...])
        rope = both_ropes(rope)
        kn[...] = jnp.zeros(kn.shape, BF)
        for parity, latent in enumerate((even, odd)):
            at = slice(parity * 128, parity * 128 + 80)
            for j in range(4):
                kn[at, j * 128 : (j + 1) * 128] = latent[j]
            kn[at, 512:640] = rope[parity]

        def new_position(row):
            return ctx * TOK + 2 * (row & 127) + (row >> 7)

        kn[:, 640:768] = mark(
            256, 0, lambda r: new_position(r) < n0, lambda r: new_position(r) >= n0
        )

    if own:
        part[...] = q0[...]
    else:
        for i, pieces in enumerate(((qm,), (qp,), (qx, qy))):

            @pl.when(step == i)
            def _():
                n = TOK // len(pieces)
                for k, piece in enumerate(pieces):
                    part[k * n : (k + 1) * n] = piece[...]

        step = step + 1

    rows = HEADS * TOK
    t0 = ((ctx + turn_of(step)) & 3) * TOK
    lane = iota((TOK, 128), 1)
    token = iota((TOK, 128), 0) + t0
    flags = jnp.where(
        ((lane == 0) & (token < n0)) | ((lane == 1) & (token >= n0)), 1.0, 0.0
    ).astype(BF)
    for j in range(HEADS):
        at = slice(j * TOK, (j + 1) * TOK)
        q_out[0, at, 0:512] = jnp.dot(
            part[:, j * 128 : (j + 1) * 128], ka_ref[j], preferred_element_type=F32
        ).astype(BF)
        rope = part[:, 512 + (j // 2) * 128 : 640 + (j // 2) * 128]
        keep = lane < 64 if j % 2 == 0 else lane >= 64
        q_out[0, at, 512:640] = jnp.where(keep, rope, jnp.zeros_like(rope))
        q_out[0, at, 640:768] = flags

    visible = t0 + TOK > ctx * TOK

    @pl.when(visible)
    def _():
        key = iota((rows, 256), 1)
        position = ctx * TOK + 2 * (key & 127) + (key >> 7)
        here = jnp.concatenate([iota((TOK, 256), 0)] * HEADS, axis=0) + t0
        seen_keys = (position <= here) & ((key & 127) < 80)
        scores = jnp.where(seen_keys, product(q_out[0], kn[...]), -BIG)
        top = jnp.maximum(
            jnp.full((rows, 128), -BIG, F32), jnp.max(scores, axis=1, keepdims=True)
        )
        weight = jnp.exp2((scores - wide(top, 256)) * (SCALE * LOG2E))
        mx_out[0] = top
        sm_out[0] = jnp.zeros((rows, 128), F32) + jnp.sum(weight, axis=1, keepdims=True)
        acc_out[0] = jnp.dot(weight.astype(BF), kn[:, 0:512], preferred_element_type=F32)

    @pl.when(jnp.logical_not(visible))
    def _():
        mx_out[0] = jnp.full((rows, 128), -BIG, F32)
        sm_out[0] = jnp.zeros((rows, 128), F32)
        acc_out[0] = jnp.zeros((rows, 512), F32)


def attend_kernel(
    ids, table,
    q_ref, acc0, mx0, sm0, va_ref, mark_ref, a0, am, ap, b0, bm, bp,
    out_ref,
    kc, kb, acc, mx, sm, sem,
):
    step = pl.program_id(0)
    core = ids[2] & 1
    end0 = table[SLOTS]
    end1 = table[SLOTS + 1]
    n0 = table[SLOTS + 2]

    @pl.when(step == 0)
    def _():
        marks = pltpu.make_async_copy(mark_ref, kb.at[:, pl.ds(640, 128)], sem.at[2])
        marks.start()
        for w, (own, first, second) in enumerate(((a0, am, ap), (b0, bm, bp))):
            pltpu.make_async_copy(own, kc.at[w, 0], sem.at[w]).start()
            pltpu.make_async_copy(first, kc.at[w, 1, pl.ds(0, 4)], sem.at[w]).start()
            pltpu.make_async_copy(second, kc.at[w, 1, pl.ds(4, 4)], sem.at[w]).start()
        for w in range(2):
            pltpu.make_async_copy(kc.at[w], kc.at[w], sem.at[w]).wait()
            slot = core if w == 0 else 1 - core

            def shape_up(p, _):
                at = table[p * 2 + slot] * BLK
                for half in range(2):
                    block = kc[w, half, p]
                    ropes = both_ropes(block[:, 1024:1152])
                    for parity in range(2):
                        to = pl.ds(pl.multiple_of(at + half * 64 + parity * 32, 32), 32)
                        kb[to, 0:512] = block[:, parity * 512 : parity * 512 + 512]
                        kb[to, 512:640] = ropes[parity]
                return 0

            lax.fori_loop(0, 8, shape_up, 0)
        marks.wait()

    t0 = ((ids[1] + turn_of(step)) & 3) * TOK
    low = jnp.where(t0 < n0, 0, end0)
    high = jnp.where(t0 + TOK > n0, end1, end0)
    extent = high - low

    def chunk(size):
        at = pl.ds(pl.multiple_of(jnp.minimum(low, KEYS - size), BLK), size)
        scores = product(q_ref[0], kb[at, :])
        before = mx0[0]
        top = jnp.maximum(before, jnp.max(scores, axis=1, keepdims=True))
        keep = jnp.exp2((before - top) * (SCALE * LOG2E))
        weight = jnp.exp2((scores - wide(top, size)) * (SCALE * LOG2E))
        mx[...] = top
        sm[...] = sm0[0] * keep + jnp.sum(weight, axis=1, keepdims=True)
        acc[...] = acc0[0] * wide(keep, 512) + jnp.dot(
            weight.astype(BF), kb[at, 0:512], preferred_element_type=F32
        )

    sizes = (0, 128, 512, 1024, 1536, 2048)
    for small, size in zip(sizes, sizes[1:]):

        @pl.when((extent > small) & (extent <= size))
        def _():
            chunk(size)

    @pl.when(extent <= 0)
    def _():
        acc[...], mx[...], sm[...] = acc0[0], mx0[0], sm0[0]

    lane16 = iota((16, 128), 1)
    stats = jnp.zeros((16, 128), F32)
    heads = []
    for j in range(HEADS):
        at = slice(j * TOK, (j + 1) * TOK)
        mass = sm[at, :]
        none = mass == 0.0
        safe = jnp.where(none, 1.0, mass)
        lse = jnp.where(none, -BIG, mx[at, :] * SCALE + jnp.log(safe))
        latent = (acc[at, :] * wide(1.0 / safe, 512)).astype(BF)
        heads.append(jnp.dot(latent, va_ref[j], preferred_element_type=F32).astype(BF))
        one = lse.astype(BF).astype(F32)
        two = (lse - one).astype(BF).astype(F32)
        three = lse - one - two
        for k in range(TOK // 16):
            base = 12 * k + 3 * j
            cut = slice(k * 16, (k + 1) * 16)
            for i, value in enumerate((one, two, three)):
                stats = jnp.where(lane16 == base + i, value[cut], stats)

    for j in range(HEADS):
        out_ref[0, 0:TOK, j * 128 : (j + 1) * 128] = heads[j]
    out_ref[0, TOK : TOK + STAT, 0:128] = stats.astype(BF)
    out_ref[0, TOK : TOK + STAT, 128:512] = jnp.zeros((STAT, 384), BF)


def merge_kernel(got_ref, head_ref):
    lane_in = iota((128, 512), 0)
    lane_head = iota((128, 512), 1) // 128
    stats = jnp.concatenate([got_ref[c, TOK : TOK + STAT, 0:128] for c in range(4)], axis=0)
    for k in range(TOK // 16):
        pickup = ((lane_in >= 12 * k + 3 * lane_head) & (lane_in < 12 * k + 3 * lane_head + 3))
        lse = jnp.dot(stats, pickup.astype(BF), preferred_element_type=F32)
        lse = [lse[c * 16 : (c + 1) * 16] for c in range(4)]
        top = jnp.maximum(jnp.maximum(lse[0], lse[1]), jnp.maximum(lse[2], lse[3]))
        weight = [jnp.exp(v - top) for v in lse]
        total = weight[0] + weight[1] + weight[2] + weight[3]
        at = slice(k * 16, (k + 1) * 16)
        mixed = sum(w * got_ref[c, at, :].astype(F32) for c, w in enumerate(weight))
        head_ref[at, :] = (mixed / total).astype(BF)


def project_kernel(ids, head_ref, other_ref, w_ref, x_ref, out_ref):
    core = ids[2] & 1
    for y in range(4):
        column = pl.multiple_of((2 * y + core) * 896, 128)
        total = jnp.dot(
            head_ref[...], w_ref[:, pl.ds(column, 896)], preferred_element_type=F32
        )
        total += jnp.dot(
            other_ref[...], x_ref[:, y * 896 : (y + 1) * 896], preferred_element_type=F32
        )
        out_ref[y] = total.astype(BF)


def shift(value, axis, by, size):
    return lax.ppermute(value, axis, [(i, (i + by) % size) for i in range(size)])


def swap_core(value):
    return lax.ppermute(value, "head", [(i, i ^ 1) for i in range(8)])


def whole(*shape):
    return pl.BlockSpec(shape, lambda i, *_: (0,) * len(shape))


def prepare(ids, hit_holder, prior, counts, queries, key_absorb, new_latent, before=None):
    own = before is None
    rows = HEADS * TOK
    tile = lambda n: pl.BlockSpec((1, rows, n), lambda i, *_: (i + (not own), 0, 0))
    kept = [((KW, BF), 0), ((512, F32), 1), ((128, F32), 2), ((128, F32), 3)]
    out_specs = [tile(shape[0]) for shape, _ in kept]
    out_shape = [pltpu.HBM((4, rows, n), kind) for (n, kind), _ in kept]
    scratch = [pltpu.VMEM((TOK, 768), BF), pltpu.VMEM((256, KW), BF)]
    aliases = {}
    if own:
        out_specs += [whole(KEYS, 128), pl.BlockSpec(memory_space=pltpu.SMEM)]
        out_shape += [pltpu.HBM((KEYS, 128), BF), jax.ShapeDtypeStruct((32,), jnp.int32)]
        scratch += [pltpu.SMEM((8,), jnp.int32)]
        before = ()
    else:
        before = [pltpu.with_memory_space_constraint(value, pltpu.HBM) for value in before]
        aliases = {4 + len(queries) + 2 + i: i for i in range(4)}
    return pl.pallas_call(
        partial(ready_kernel, own),
        grid_spec=pltpu.PrefetchScalarGridSpec(
            num_scalar_prefetch=4,
            grid=(1 if own else 3,),
            in_specs=[whole(*value.shape) for value in queries]
            + [whole(HEADS, 128, 512), whole(80, WIDE2)]
            + [pl.BlockSpec(memory_space=pltpu.HBM)] * len(before),
            out_specs=out_specs,
            scratch_shapes=scratch,
        ),
        out_shape=out_shape,
        input_output_aliases=aliases,
        compiler_params=pltpu.CompilerParams(vmem_limit_bytes=28 * 2**20),
        cost_estimate=pl.CostEstimate(
            flops=10**9 * (1 if own else 3),
            bytes_accessed=4 * 10**6 * (1 if own else 3),
            transcendentals=10**6,
        ),
        name="prepare_own" if own else "prepare_others",
    )(ids, hit_holder, prior, counts, *queries, key_absorb, new_latent, *before)


def attend(ids, ready, pieces, value_absorb):
    q_all, acc0, mx0, sm0, marks = [
        pltpu.with_memory_space_constraint(value, pltpu.HBM) for value in ready[:5]
    ]
    rows = HEADS * TOK
    tile = lambda n: pl.BlockSpec((1, rows, n), lambda i, *_: (i, 0, 0))
    return pl.pallas_call(
        attend_kernel,
        grid_spec=pltpu.PrefetchScalarGridSpec(
            num_scalar_prefetch=2,
            grid=(4,),
            in_specs=[tile(KW), tile(512), tile(128), tile(128), whole(HEADS, 512, 128)]
            + [pl.BlockSpec(memory_space=pl.ANY)] * 7,
            out_specs=pl.BlockSpec(
                (1, TOK + STAT, 512), lambda i, ids, _: ((ids[1] + turn_of(i)) & 3, 0, 0)
            ),
            scratch_shapes=[
                pltpu.VMEM((2, 2, 8, 32, WIDE2), BF),
                pltpu.VMEM((KEYS, KW), BF),
                pltpu.VMEM((rows, 512), F32),
                pltpu.VMEM((rows, 128), F32),
                pltpu.VMEM((rows, 128), F32),
                pltpu.SemaphoreType.DMA((3,)),
            ],
        ),
        out_shape=jax.ShapeDtypeStruct((4, TOK + STAT, 512), BF),
        compiler_params=pltpu.CompilerParams(vmem_limit_bytes=40 * 2**20),
        cost_estimate=pl.CostEstimate(
            flops=12 * 10**9, bytes_accessed=15 * 10**6, transcendentals=5 * 10**6
        ),
        name="attend",
    )(ids, ready[5], q_all, acc0, mx0, sm0, value_absorb, marks, *pieces)


def local(
    query_nope, query_rope, new_latent, cache_pool, hit_holder, hit_block,
    prior_blocks, new_counts, key_absorb, value_absorb, out_weight,
):
    ids = jnp.stack(
        [lax.axis_index("pool"), lax.axis_index("ctx"), lax.axis_index("head")]
    ).astype(jnp.int32)

    half = 32 * WIDE2
    prior = prior_blocks.T
    counts = new_counts.T
    picked, queries = pl.pallas_call(
        pick_kernel,
        grid_spec=pltpu.PrefetchScalarGridSpec(
            num_scalar_prefetch=2,
            grid=(1,),
            in_specs=[
                pl.BlockSpec((16, half), lambda i, ids, _: (0, (ids[2] >> 1) & 1)),
                whole(8, 64),
                whole(8, 64),
                whole(TOK, 512),
                whole(TOK, 256),
            ],
            out_specs=[whole(8, 32, WIDE2), whole(TOK, 768)],
        ),
        out_shape=[
            jax.ShapeDtypeStruct((8, 32, WIDE2), BF),
            jax.ShapeDtypeStruct((TOK, 768), BF),
        ],
        name="pick_blocks",
    )(ids, prior, cache_pool, hit_holder, hit_block, query_nope, query_rope)

    qm = shift(queries, "ctx", 1, 4)
    qp = shift(queries, "ctx", -1, 4)
    queries, qm, qp = lax.optimization_barrier((queries, qm, qp))
    qx = shift(qm[:80], "ctx", 1, 4)
    qy = shift(qp[80:], "ctx", -1, 4)

    a0 = lax.all_to_all(picked, "pool", split_axis=0, concat_axis=0, tiled=True)

    prepared = prepare(
        ids, hit_holder, prior, counts, (queries,), key_absorb, new_latent
    )
    a0, qx, qy, table = lax.optimization_barrier((a0, qx, qy, prepared[5]))
    am = shift(a0[:4], "head", 2, 8)
    ap = shift(a0[4:], "head", -2, 8)
    b0 = swap_core(a0)
    ready = prepare(
        ids, hit_holder, prior, counts, (qm, qp, qx, qy), key_absorb, new_latent, prepared[:4]
    )
    queries_ready, am, ap, b0 = lax.optimization_barrier((ready[0], am, ap, b0))
    bm = swap_core(am)
    bp = swap_core(ap)
    partial_out = attend(
        ids,
        (queries_ready, *ready[1:4], prepared[4], table),
        (a0, am, ap, b0, bm, bp),
        value_absorb,
    )
    partial_out, late_weight = lax.optimization_barrier((partial_out, out_weight))
    got = lax.all_to_all(partial_out, "ctx", split_axis=0, concat_axis=0, tiled=True)
    other_columns = [
        lax.dynamic_slice(late_weight, (0, (2 * y + 1 - (ids[2] & 1)) * 896), (512, 896))
        for y in range(4)
    ]
    other_weight = swap_core(jnp.concatenate(other_columns, axis=1))

    heads = pl.pallas_call(
        merge_kernel,
        out_shape=jax.ShapeDtypeStruct((TOK, 512), BF),
        compiler_params=pltpu.CompilerParams(vmem_limit_bytes=8 * 2**20),
        name="merge",
    )(got)
    other_heads = swap_core(heads)
    vmem = pl.BlockSpec(memory_space=pltpu.VMEM)
    shares = pl.pallas_call(
        project_kernel,
        grid_spec=pltpu.PrefetchScalarGridSpec(
            num_scalar_prefetch=1,
            in_specs=[vmem] * 4,
            out_specs=vmem,
        ),
        out_shape=jax.ShapeDtypeStruct((4, TOK, 896), BF),
        compiler_params=pltpu.CompilerParams(vmem_limit_bytes=24 * 2**20),
        name="project",
    )(ids, heads, other_heads, out_weight, other_weight)
    shares = lax.all_to_all(
        shares, "head", split_axis=0, concat_axis=0, tiled=True,
        axis_index_groups=[[0, 2, 4, 6], [1, 3, 5, 7]],
    )
    return jnp.sum(shares.astype(F32), axis=0).astype(BF)


def solution(mesh):
    return jax.shard_map(
        local,
        mesh=mesh,
        in_specs=(
            P(("pool", "ctx"), "head"),
            P(("pool", "ctx"), "head"),
            P(("pool", "ctx"), None),
            P(("pool", "ctx"), None),
            P(),
            P(),
            P(),
            P(),
            P("head", None, None),
            P("head", None, None),
            P("head", None),
        ),
        out_specs=P(("pool", "ctx"), "head"),
        check_vma=False,
    )
```

```python
from functools import partial

import jax
import jax.numpy as jnp
from jax import lax
from jax.experimental import pallas as pl
from jax.experimental.pallas import tpu as pltpu
from jax.sharding import PartitionSpec as P

KV_RANK = 512
ROPE = 64
QK_NOPE = 128
VD = 128
BLK = 128
PAIRS = BLK // 2
WIDE2 = 2 * (KV_RANK + ROPE)
HEADS = 4
TOK = 160
SLOTS = 16
KEYS = SLOTS * BLK
KW = 768
BIG = 2.0**100
SCALE = (QK_NOPE + ROPE) ** (-0.5)
LOG2E = 1.4426950408889634
BF = jnp.bfloat16
F32 = jnp.float32
STAT = 16
ORDER = (0, 3, 1, 2)


def iota(shape, dim):
    return lax.broadcasted_iota(jnp.int32, shape, dim)


def pick_kernel(
    ids, prior, cache_ref, holder_ref, block_ref, nope_ref, rope_ref, out_ref, query_ref
):
    query_ref[:, 0:512] = nope_ref[...]
    query_ref[:, 512:768] = rope_ref[...]
    me = ids[0] * 4 + ids[1]
    core = ids[2] & 1
    lane = iota((8, 64), 1)
    group = iota((8, 64), 0)
    count = jnp.zeros((8, 64), jnp.int32)
    for g in range(8):
        count = jnp.where(group == g, prior[0, g] + prior[1, g], count)
    match = (holder_ref[...] == me) & (lane < count)
    first = jnp.min(jnp.where(match, lane, 1000), axis=1, keepdims=True)
    last = jnp.max(jnp.where(match, lane, -1), axis=1, keepdims=True)
    wanted = jnp.where(core == 0, first, jnp.where(last > first, last, -2))
    chosen = match & (lane == wanted)
    index = jnp.sum(jnp.where(chosen, block_ref[...] + 1, 0), axis=1, keepdims=True) - 1
    spread = (iota((128, 8), 0) // 16 == iota((128, 8), 1)).astype(BF)
    rows_index = jnp.dot(
        spread,
        jnp.broadcast_to(index.astype(F32), (8, 256)).astype(BF),
        preferred_element_type=F32,
    )
    row = iota((128, 256), 0)
    col = iota((128, 256), 1)
    onehot = ((col // 16 == row % 16) & ((col % 16).astype(F32) == rows_index)).astype(BF)
    for part in range(2):
        stacked = jnp.concatenate(
            [
                cache_ref[:, p * WIDE2 : (p + 1) * WIDE2]
                for p in range(part * 16, part * 16 + 16)
            ],
            axis=0,
        )
        out = jnp.dot(onehot, stacked, preferred_element_type=F32).astype(BF)
        even, odd, rope = align(out)
        to = slice(part * 16, part * 16 + 16)
        for g in range(8):
            at = slice(g * 16, (g + 1) * 16)
            for j in range(4):
                out_ref[g, to, j * 128 : (j + 1) * 128] = even[j][at]
                out_ref[g, to, 512 + j * 128 : 640 + j * 128] = odd[j][at]
            out_ref[g, to, 1024:1152] = rope[at]


def align(rows):
    low = iota((rows.shape[0], 128), 1) < 64
    tile = [rows[:, j * 128 : (j + 1) * 128] for j in range(9)]
    flip = {j: pltpu.roll(tile[j].astype(F32), 64, 1).astype(BF) for j in range(5, 9)}
    flip[4] = pltpu.roll(tile[4].astype(F32), 64, 1).astype(BF)
    odd = [jnp.where(low, flip[4 + j], flip[5 + j]) for j in range(4)]
    return tile[:4], odd, jnp.where(low, tile[4], tile[8])


def both_ropes(tile):
    low = iota(tile.shape, 1) < 64
    flip = pltpu.roll(tile.astype(F32), 64, 1).astype(BF)
    return jnp.where(low, tile, flip), jnp.where(low, flip, tile)


def wide(value, n):
    return jnp.concatenate([value] * (n // 128), axis=1)


def turn_of(step):
    return jnp.where(step == 0, 0, jnp.where(step == 1, 3, jnp.where(step == 2, 1, 2)))


def product(queries, keys):
    return lax.dot_general(
        queries, keys, (((1,), (1,)), ((), ())), preferred_element_type=F32
    )


def mark(n, base, keys0, keys1):
    row = iota((n, 128), 0) + base
    lane = iota((n, 128), 1)
    miss0 = (lane == 0) & jnp.logical_not(keys0(row))
    miss1 = (lane == 1) & jnp.logical_not(keys1(row))
    return jnp.where(miss0 | miss1, -BIG, 0.0).astype(BF)


def plan(ids, holder, prior, counts, mark_out, table, seen):
    group = ids[0]
    for i in range(SLOTS):
        table[i] = -1
    for i in range(8):
        seen[i] = 0
    own = prior[0, group]
    total = own + prior[1, group]

    def entry(e, carry):
        filled, mine = carry
        where = holder[group, e]
        hit = (where & 3) == ids[1]
        p = where >> 2

        @pl.when(hit)
        def _():
            s = seen[p]
            seen[p] = s + 1
            table[p * 2 + s] = filled

        add = hit.astype(jnp.int32)
        return filled + add, mine + jnp.where(e < own, add, 0)

    filled, mine = lax.fori_loop(0, total, entry, (jnp.int32(0), jnp.int32(0)))
    end0 = mine * BLK
    end1 = filled * BLK
    table[SLOTS] = end0
    table[SLOTS + 1] = end1
    table[SLOTS + 2] = counts[0, group]
    for i in range(SLOTS + 3, 32):
        table[i] = 0
    for i in range(SLOTS):
        dead = table[i] < 0

        @pl.when(dead)
        def _():
            table[i] = filled

        filled = filled + dead.astype(jnp.int32)

    def marks(i, _):
        at = pl.multiple_of(i * BLK, BLK)
        mark_out[pl.ds(at, BLK), :] = mark(
            BLK, at, lambda r: r < end0, lambda r: (r >= end0) & (r < end1)
        )
        return 0

    lax.fori_loop(0, SLOTS, marks, 0)


def ready_kernel(own, ids, holder, prior, counts, *refs):
    if own:
        q0, ka_ref, nl_ref, q_out, acc_out, mx_out, sm_out, mark_out, table, part, kn, seen = refs
    else:
        qm, qp, qx, qy, ka_ref, nl_ref = refs[:6]
        q_out, acc_out, mx_out, sm_out, part, kn = refs[10:]
    step = pl.program_id(0)
    ctx = ids[1]
    n0 = counts[0, ids[0]]

    @pl.when(step == 0)
    def _():
        if own:
            plan(ids, holder, prior, counts, mark_out, table, seen)
        even, odd, rope = align(nl_ref[...])
        rope = both_ropes(rope)
        kn[...] = jnp.zeros(kn.shape, BF)
        for parity, latent in enumerate((even, odd)):
            at = slice(parity * 128, parity * 128 + 80)
            for j in range(4):
                kn[at, j * 128 : (j + 1) * 128] = latent[j]
            kn[at, 512:640] = rope[parity]

        def new_position(row):
            return ctx * TOK + 2 * (row & 127) + (row >> 7)

        kn[:, 640:768] = mark(
            256, 0, lambda r: new_position(r) < n0, lambda r: new_position(r) >= n0
        )

    if own:
        part[...] = q0[...]
    else:
        for i, pieces in enumerate(((qm,), (qp,), (qx, qy))):

            @pl.when(step == i)
            def _():
                n = TOK // len(pieces)
                for k, piece in enumerate(pieces):
                    part[k * n : (k + 1) * n] = piece[...]

        step = step + 1

    rows = HEADS * TOK
    t0 = ((ctx + turn_of(step)) & 3) * TOK
    lane = iota((TOK, 128), 1)
    token = iota((TOK, 128), 0) + t0
    flags = jnp.where(
        ((lane == 0) & (token < n0)) | ((lane == 1) & (token >= n0)), 1.0, 0.0
    ).astype(BF)
    for j in range(HEADS):
        at = slice(j * TOK, (j + 1) * TOK)
        q_out[0, at, 0:512] = jnp.dot(
            part[:, j * 128 : (j + 1) * 128], ka_ref[j], preferred_element_type=F32
        ).astype(BF)
        rope = part[:, 512 + (j // 2) * 128 : 640 + (j // 2) * 128]
        keep = lane < 64 if j % 2 == 0 else lane >= 64
        q_out[0, at, 512:640] = jnp.where(keep, rope, jnp.zeros_like(rope))
        q_out[0, at, 640:768] = flags

    visible = t0 + TOK > ctx * TOK

    @pl.when(visible)
    def _():
        key = iota((rows, 256), 1)
        position = ctx * TOK + 2 * (key & 127) + (key >> 7)
        here = jnp.concatenate([iota((TOK, 256), 0)] * HEADS, axis=0) + t0
        seen_keys = (position <= here) & ((key & 127) < 80)
        scores = jnp.where(seen_keys, product(q_out[0], kn[...]), -BIG)
        top = jnp.maximum(
            jnp.full((rows, 128), -BIG, F32), jnp.max(scores, axis=1, keepdims=True)
        )
        weight = jnp.exp2((scores - wide(top, 256)) * (SCALE * LOG2E))
        mx_out[0] = top
        sm_out[0] = jnp.zeros((rows, 128), F32) + jnp.sum(weight, axis=1, keepdims=True)
        acc_out[0] = jnp.dot(weight.astype(BF), kn[:, 0:512], preferred_element_type=F32)

    @pl.when(jnp.logical_not(visible))
    def _():
        mx_out[0] = jnp.full((rows, 128), -BIG, F32)
        sm_out[0] = jnp.zeros((rows, 128), F32)
        acc_out[0] = jnp.zeros((rows, 512), F32)


def attend_kernel(
    ids, table,
    q_ref, acc0, mx0, sm0, va_ref, mark_ref, a0, am, ap, b0, bm, bp,
    out_ref,
    kc, kb, acc, mx, sm, sem,
):
    step = pl.program_id(0)
    core = ids[2] & 1
    end0 = table[SLOTS]
    end1 = table[SLOTS + 1]
    n0 = table[SLOTS + 2]

    @pl.when(step == 0)
    def _():
        marks = pltpu.make_async_copy(mark_ref, kb.at[:, pl.ds(640, 128)], sem.at[2])
        marks.start()
        for w, (own, first, second) in enumerate(((a0, am, ap), (b0, bm, bp))):
            pltpu.make_async_copy(own, kc.at[w, 0], sem.at[w]).start()
            pltpu.make_async_copy(first, kc.at[w, 1, pl.ds(0, 4)], sem.at[w]).start()
            pltpu.make_async_copy(second, kc.at[w, 1, pl.ds(4, 4)], sem.at[w]).start()
        for w in range(2):
            pltpu.make_async_copy(kc.at[w], kc.at[w], sem.at[w]).wait()
            slot = core if w == 0 else 1 - core

            def shape_up(p, _):
                at = table[p * 2 + slot] * BLK
                for half in range(2):
                    block = kc[w, half, p]
                    ropes = both_ropes(block[:, 1024:1152])
                    for parity in range(2):
                        to = pl.ds(pl.multiple_of(at + half * 64 + parity * 32, 32), 32)
                        kb[to, 0:512] = block[:, parity * 512 : parity * 512 + 512]
                        kb[to, 512:640] = ropes[parity]
                return 0

            lax.fori_loop(0, 8, shape_up, 0)
        marks.wait()

    t0 = ((ids[1] + turn_of(step)) & 3) * TOK
    low = jnp.where(t0 < n0, 0, end0)
    high = jnp.where(t0 + TOK > n0, end1, end0)
    extent = high - low

    def chunk(size):
        at = pl.ds(pl.multiple_of(jnp.minimum(low, KEYS - size), BLK), size)
        scores = product(q_ref[0], kb[at, :])
        before = mx0[0]
        top = jnp.maximum(before, jnp.max(scores, axis=1, keepdims=True))
        keep = jnp.exp2((before - top) * (SCALE * LOG2E))
        weight = jnp.exp2((scores - wide(top, size)) * (SCALE * LOG2E))
        mx[...] = top
        sm[...] = sm0[0] * keep + jnp.sum(weight, axis=1, keepdims=True)
        acc[...] = acc0[0] * wide(keep, 512) + jnp.dot(
            weight.astype(BF), kb[at, 0:512], preferred_element_type=F32
        )

    sizes = (0, 128, 512, 1024, 1536, 2048)
    for small, size in zip(sizes, sizes[1:]):

        @pl.when((extent > small) & (extent <= size))
        def _():
            chunk(size)

    @pl.when(extent <= 0)
    def _():
        acc[...], mx[...], sm[...] = acc0[0], mx0[0], sm0[0]

    lane16 = iota((16, 128), 1)
    stats = jnp.zeros((16, 128), F32)
    heads = []
    for j in range(HEADS):
        at = slice(j * TOK, (j + 1) * TOK)
        mass = sm[at, :]
        none = mass == 0.0
        safe = jnp.where(none, 1.0, mass)
        lse = jnp.where(none, -BIG, mx[at, :] * SCALE + jnp.log(safe))
        latent = (acc[at, :] * wide(1.0 / safe, 512)).astype(BF)
        heads.append(jnp.dot(latent, va_ref[j], preferred_element_type=F32).astype(BF))
        one = lse.astype(BF).astype(F32)
        two = (lse - one).astype(BF).astype(F32)
        three = lse - one - two
        for k in range(TOK // 16):
            base = 12 * k + 3 * j
            cut = slice(k * 16, (k + 1) * 16)
            for i, value in enumerate((one, two, three)):
                stats = jnp.where(lane16 == base + i, value[cut], stats)

    for j in range(HEADS):
        out_ref[0, 0:TOK, j * 128 : (j + 1) * 128] = heads[j]
    out_ref[0, TOK : TOK + STAT, 0:128] = stats.astype(BF)
    out_ref[0, TOK : TOK + STAT, 128:512] = jnp.zeros((STAT, 384), BF)


def merge_kernel(got_ref, head_ref):
    lane_in = iota((128, 512), 0)
    lane_head = iota((128, 512), 1) // 128
    stats = jnp.concatenate([got_ref[c, TOK : TOK + STAT, 0:128] for c in range(4)], axis=0)
    for k in range(TOK // 16):
        pickup = ((lane_in >= 12 * k + 3 * lane_head) & (lane_in < 12 * k + 3 * lane_head + 3))
        lse = jnp.dot(stats, pickup.astype(BF), preferred_element_type=F32)
        lse = [lse[c * 16 : (c + 1) * 16] for c in range(4)]
        top = jnp.maximum(jnp.maximum(lse[0], lse[1]), jnp.maximum(lse[2], lse[3]))
        weight = [jnp.exp(v - top) for v in lse]
        total = weight[0] + weight[1] + weight[2] + weight[3]
        at = slice(k * 16, (k + 1) * 16)
        mixed = sum(w * got_ref[c, at, :].astype(F32) for c, w in enumerate(weight))
        head_ref[at, :] = (mixed / total).astype(BF)


def project_kernel(ids, head_ref, other_ref, w_ref, x_ref, out_ref):
    core = ids[2] & 1
    for y in range(4):
        column = pl.multiple_of((2 * y + core) * 896, 128)
        total = jnp.dot(
            head_ref[...], w_ref[:, pl.ds(column, 896)], preferred_element_type=F32
        )
        total += jnp.dot(
            other_ref[...], x_ref[:, y * 896 : (y + 1) * 896], preferred_element_type=F32
        )
        out_ref[y] = total.astype(BF)


def shift(value, axis, by, size):
    return lax.ppermute(value, axis, [(i, (i + by) % size) for i in range(size)])


def swap_core(value):
    return lax.ppermute(value, "head", [(i, i ^ 1) for i in range(8)])


def whole(*shape):
    return pl.BlockSpec(shape, lambda i, *_: (0,) * len(shape))


def pin(value):
    return pltpu.with_memory_space_constraint(value, pltpu.HBM)


def prepare(ids, hit_holder, prior, counts, queries, key_absorb, new_latent, before=None):
    own = before is None
    rows = HEADS * TOK
    tile = lambda n: pl.BlockSpec((1, rows, n), lambda i, *_: (i + (not own), 0, 0))
    kept = [((KW, BF), 0), ((512, F32), 1), ((128, F32), 2), ((128, F32), 3)]
    out_specs = [tile(shape[0]) for shape, _ in kept]
    out_shape = [pltpu.HBM((4, rows, n), kind) for (n, kind), _ in kept]
    scratch = [pltpu.VMEM((TOK, 768), BF), pltpu.VMEM((256, KW), BF)]
    aliases = {}
    if own:
        out_specs += [whole(KEYS, 128), pl.BlockSpec(memory_space=pltpu.SMEM)]
        out_shape += [pltpu.HBM((KEYS, 128), BF), jax.ShapeDtypeStruct((32,), jnp.int32)]
        scratch += [pltpu.SMEM((8,), jnp.int32)]
        before = ()
    else:
        before = [pin(value) for value in before]
        aliases = {4 + len(queries) + 2 + i: i for i in range(4)}
    return pl.pallas_call(
        partial(ready_kernel, own),
        grid_spec=pltpu.PrefetchScalarGridSpec(
            num_scalar_prefetch=4,
            grid=(1 if own else 3,),
            in_specs=[whole(*value.shape) for value in queries]
            + [whole(HEADS, 128, 512), whole(80, WIDE2)]
            + [pl.BlockSpec(memory_space=pltpu.HBM)] * len(before),
            out_specs=out_specs,
            scratch_shapes=scratch,
        ),
        out_shape=out_shape,
        input_output_aliases=aliases,
        compiler_params=pltpu.CompilerParams(vmem_limit_bytes=16 * 2**20),
        cost_estimate=pl.CostEstimate(
            flops=10**9 * (1 if own else 3),
            bytes_accessed=4 * 10**6 * (1 if own else 3),
            transcendentals=10**6,
        ),
        name="prepare_own" if own else "prepare_others",
    )(ids, hit_holder, prior, counts, *queries, pin(key_absorb), pin(new_latent), *before)


def attend(ids, ready, pieces, value_absorb):
    q_all, acc0, mx0, sm0, marks = [pin(value) for value in ready[:5]]
    rows = HEADS * TOK
    tile = lambda n: pl.BlockSpec((1, rows, n), lambda i, *_: (i, 0, 0))
    return pl.pallas_call(
        attend_kernel,
        grid_spec=pltpu.PrefetchScalarGridSpec(
            num_scalar_prefetch=2,
            grid=(4,),
            in_specs=[tile(KW), tile(512), tile(128), tile(128), whole(HEADS, 512, 128)]
            + [pl.BlockSpec(memory_space=pl.ANY)] * 7,
            out_specs=pl.BlockSpec(
                (1, TOK + STAT, 512), lambda i, ids, _: ((ids[1] + turn_of(i)) & 3, 0, 0)
            ),
            scratch_shapes=[
                pltpu.VMEM((2, 2, 8, 32, WIDE2), BF),
                pltpu.VMEM((KEYS, KW), BF),
                pltpu.VMEM((rows, 512), F32),
                pltpu.VMEM((rows, 128), F32),
                pltpu.VMEM((rows, 128), F32),
                pltpu.SemaphoreType.DMA((3,)),
            ],
        ),
        out_shape=jax.ShapeDtypeStruct((4, TOK + STAT, 512), BF),
        compiler_params=pltpu.CompilerParams(vmem_limit_bytes=27 * 2**20),
        cost_estimate=pl.CostEstimate(
            flops=12 * 10**9, bytes_accessed=15 * 10**6, transcendentals=5 * 10**6
        ),
        name="attend",
    )(ids, ready[5], q_all, acc0, mx0, sm0, pin(value_absorb), marks, *pieces)


def local(
    query_nope, query_rope, new_latent, cache_pool, hit_holder, hit_block,
    prior_blocks, new_counts, key_absorb, value_absorb, out_weight,
):
    ids = jnp.stack(
        [lax.axis_index("pool"), lax.axis_index("ctx"), lax.axis_index("head")]
    ).astype(jnp.int32)

    half = 32 * WIDE2
    prior = prior_blocks.T
    counts = new_counts.T
    picked, queries = pl.pallas_call(
        pick_kernel,
        grid_spec=pltpu.PrefetchScalarGridSpec(
            num_scalar_prefetch=2,
            grid=(1,),
            in_specs=[
                pl.BlockSpec((16, half), lambda i, ids, _: (0, (ids[2] >> 1) & 1)),
                whole(8, 64),
                whole(8, 64),
                whole(TOK, 512),
                whole(TOK, 256),
            ],
            out_specs=[whole(8, 32, WIDE2), whole(TOK, 768)],
        ),
        out_shape=[
            jax.ShapeDtypeStruct((8, 32, WIDE2), BF),
            jax.ShapeDtypeStruct((TOK, 768), BF),
        ],
        name="pick_blocks",
    )(ids, prior, cache_pool, hit_holder, hit_block, query_nope, query_rope)

    qm = shift(queries, "ctx", 1, 4)
    qp = shift(queries, "ctx", -1, 4)
    prepared = prepare(
        ids, hit_holder, prior, counts, (queries,), key_absorb, new_latent
    )
    qm, qp, table = lax.optimization_barrier((qm, qp, prepared[5]))
    qx = shift(qm[:80], "ctx", 1, 4)
    qy = shift(qp[80:], "ctx", -1, 4)

    a0 = lax.all_to_all(picked, "pool", split_axis=0, concat_axis=0, tiled=True)

    a0, qx, qy = lax.optimization_barrier((a0, qx, qy))
    am = shift(a0[:4], "head", 2, 8)
    ap = shift(a0[4:], "head", -2, 8)
    b0 = swap_core(a0)
    ready = prepare(
        ids, hit_holder, prior, counts, (qm, qp, qx, qy), key_absorb, new_latent, prepared[:4]
    )
    queries_ready, am, ap, b0 = lax.optimization_barrier((ready[0], am, ap, b0))
    bm = swap_core(am)
    bp = swap_core(ap)
    partial_out = attend(
        ids,
        (queries_ready, *ready[1:4], prepared[4], table),
        (a0, am, ap, b0, bm, bp),
        value_absorb,
    )
    partial_out, late_weight = lax.optimization_barrier((partial_out, out_weight))
    got = lax.all_to_all(partial_out, "ctx", split_axis=0, concat_axis=0, tiled=True)
    other_columns = [
        lax.dynamic_slice(late_weight, (0, (2 * y + 1 - (ids[2] & 1)) * 896), (512, 896))
        for y in range(4)
    ]
    other_weight = swap_core(jnp.concatenate(other_columns, axis=1))

    heads = pl.pallas_call(
        merge_kernel,
        out_shape=jax.ShapeDtypeStruct((TOK, 512), BF),
        compiler_params=pltpu.CompilerParams(vmem_limit_bytes=8 * 2**20),
        name="merge",
    )(got)
    other_heads = swap_core(heads)
    vmem = pl.BlockSpec(memory_space=pltpu.VMEM)
    shares = pl.pallas_call(
        project_kernel,
        grid_spec=pltpu.PrefetchScalarGridSpec(
            num_scalar_prefetch=1,
            in_specs=[vmem] * 4,
            out_specs=vmem,
        ),
        out_shape=jax.ShapeDtypeStruct((4, TOK, 896), BF),
        compiler_params=pltpu.CompilerParams(vmem_limit_bytes=24 * 2**20),
        name="project",
    )(ids, heads, other_heads, out_weight, other_weight)
    shares = lax.all_to_all(
        shares, "head", split_axis=0, concat_axis=0, tiled=True,
        axis_index_groups=[[0, 2, 4, 6], [1, 3, 5, 7]],
    )
    return jnp.sum(shares.astype(F32), axis=0).astype(BF)


def solution(mesh):
    return jax.shard_map(
        local,
        mesh=mesh,
        in_specs=(
            P(("pool", "ctx"), "head"),
            P(("pool", "ctx"), "head"),
            P(("pool", "ctx"), None),
            P(("pool", "ctx"), None),
            P(),
            P(),
            P(),
            P(),
            P("head", None, None),
            P("head", None, None),
            P("head", None),
        ),
        out_specs=P(("pool", "ctx"), "head"),
        check_vma=False,
    )
```

```python
from functools import partial

import jax
import jax.numpy as jnp
from jax import lax
from jax.experimental import pallas as pl
from jax.experimental.pallas import tpu as pltpu
from jax.sharding import PartitionSpec as P

KV_RANK = 512
ROPE = 64
QK_NOPE = 128
VD = 128
BLK = 128
PAIRS = BLK // 2
WIDE2 = 2 * (KV_RANK + ROPE)
HEADS = 4
TOK = 160
SLOTS = 16
KEYS = SLOTS * BLK
KW = 768
BIG = 2.0**100
SCALE = (QK_NOPE + ROPE) ** (-0.5)
LOG2E = 1.4426950408889634
BF = jnp.bfloat16
F32 = jnp.float32
STAT = 16
SENT = HEADS * TOK + STAT
ORDER = (0, 3, 1, 2)


def iota(shape, dim):
    return lax.broadcasted_iota(jnp.int32, shape, dim)


def pick_kernel(
    ids, prior, cache_ref, holder_ref, block_ref, nope_ref, rope_ref, out_ref, query_ref
):
    query_ref[:, 0:512] = nope_ref[...]
    query_ref[:, 512:768] = rope_ref[...]
    me = ids[0] * 4 + ids[1]
    core = ids[2] & 1
    lane = iota((8, 64), 1)
    group = iota((8, 64), 0)
    count = jnp.zeros((8, 64), jnp.int32)
    for g in range(8):
        count = jnp.where(group == g, prior[0, g] + prior[1, g], count)
    match = (holder_ref[...] == me) & (lane < count)
    first = jnp.min(jnp.where(match, lane, 1000), axis=1, keepdims=True)
    last = jnp.max(jnp.where(match, lane, -1), axis=1, keepdims=True)
    wanted = jnp.where(core == 0, first, jnp.where(last > first, last, -2))
    chosen = match & (lane == wanted)
    index = jnp.sum(jnp.where(chosen, block_ref[...] + 1, 0), axis=1, keepdims=True) - 1
    spread = (iota((128, 8), 0) // 16 == iota((128, 8), 1)).astype(BF)
    rows_index = jnp.dot(
        spread,
        jnp.broadcast_to(index.astype(F32), (8, 256)).astype(BF),
        preferred_element_type=F32,
    )
    row = iota((128, 256), 0)
    col = iota((128, 256), 1)
    onehot = ((col // 16 == row % 16) & ((col % 16).astype(F32) == rows_index)).astype(BF)
    for part in range(2):
        stacked = jnp.concatenate(
            [
                cache_ref[:, p * WIDE2 : (p + 1) * WIDE2]
                for p in range(part * 16, part * 16 + 16)
            ],
            axis=0,
        )
        out = jnp.dot(onehot, stacked, preferred_element_type=F32).astype(BF)
        even, odd, rope = align(out)
        to = slice(part * 16, part * 16 + 16)
        for g in range(8):
            at = slice(g * 16, (g + 1) * 16)
            for j in range(4):
                out_ref[g, to, j * 128 : (j + 1) * 128] = even[j][at]
                out_ref[g, to, 512 + j * 128 : 640 + j * 128] = odd[j][at]
            out_ref[g, to, 1024:1152] = rope[at]


def align(rows):
    low = iota((rows.shape[0], 128), 1) < 64
    tile = [rows[:, j * 128 : (j + 1) * 128] for j in range(9)]
    flip = {j: pltpu.roll(tile[j].astype(F32), 64, 1).astype(BF) for j in range(5, 9)}
    flip[4] = pltpu.roll(tile[4].astype(F32), 64, 1).astype(BF)
    odd = [jnp.where(low, flip[4 + j], flip[5 + j]) for j in range(4)]
    return tile[:4], odd, jnp.where(low, tile[4], tile[8])


def both_ropes(tile):
    low = iota(tile.shape, 1) < 64
    flip = pltpu.roll(tile.astype(F32), 64, 1).astype(BF)
    return jnp.where(low, tile, flip), jnp.where(low, flip, tile)


def wide(value, n):
    return jnp.concatenate([value] * (n // 128), axis=1)


def turn_of(step):
    return jnp.where(step == 0, 0, jnp.where(step == 1, 3, jnp.where(step == 2, 1, 2)))


def product(queries, keys):
    return lax.dot_general(
        queries, keys, (((1,), (1,)), ((), ())), preferred_element_type=F32
    )


def mark(n, base, keys0, keys1):
    row = iota((n, 128), 0) + base
    lane = iota((n, 128), 1)
    miss0 = (lane == 0) & jnp.logical_not(keys0(row))
    miss1 = (lane == 1) & jnp.logical_not(keys1(row))
    return jnp.where(miss0 | miss1, -BIG, 0.0).astype(BF)


def plan(ids, holder, prior, counts, mark_out, table, seen):
    group = ids[0]
    for i in range(SLOTS):
        table[i] = -1
    for i in range(8):
        seen[i] = 0
    own = prior[0, group]
    total = own + prior[1, group]

    def entry(e, carry):
        filled, mine = carry
        where = holder[group, e]
        hit = (where & 3) == ids[1]
        p = where >> 2

        @pl.when(hit)
        def _():
            s = seen[p]
            seen[p] = s + 1
            table[p * 2 + s] = filled

        add = hit.astype(jnp.int32)
        return filled + add, mine + jnp.where(e < own, add, 0)

    filled, mine = lax.fori_loop(0, total, entry, (jnp.int32(0), jnp.int32(0)))
    end0 = mine * BLK
    end1 = filled * BLK
    table[SLOTS] = end0
    table[SLOTS + 1] = end1
    table[SLOTS + 2] = counts[0, group]
    for i in range(SLOTS + 3, 32):
        table[i] = 0
    for i in range(SLOTS):
        dead = table[i] < 0

        @pl.when(dead)
        def _():
            table[i] = filled

        filled = filled + dead.astype(jnp.int32)

    def marks(i, _):
        at = pl.multiple_of(i * BLK, BLK)
        mark_out[pl.ds(at, BLK), :] = mark(
            BLK, at, lambda r: r < end0, lambda r: (r >= end0) & (r < end1)
        )
        return 0

    lax.fori_loop(0, SLOTS, marks, 0)


def ready_kernel(first, count, ids, holder, prior, counts, *refs):
    own = first == 0
    sources, refs = refs[:count], refs[count:]
    ka_ref, nl_ref = refs[:2]
    if own:
        q_out, acc_out, mx_out, sm_out, mark_out, table, part, kn, seen = refs[2:]
    else:
        q_out, acc_out, mx_out, sm_out, part, kn = refs[6:]
    step = pl.program_id(0)
    ctx = ids[1]
    n0 = counts[0, ids[0]]

    @pl.when(step == 0)
    def _():
        if own:
            plan(ids, holder, prior, counts, mark_out, table, seen)
        even, odd, rope = align(nl_ref[...])
        rope = both_ropes(rope)
        kn[...] = jnp.zeros(kn.shape, BF)
        for parity, latent in enumerate((even, odd)):
            at = slice(parity * 128, parity * 128 + 80)
            for j in range(4):
                kn[at, j * 128 : (j + 1) * 128] = latent[j]
            kn[at, 512:640] = rope[parity]

        def new_position(row):
            return ctx * TOK + 2 * (row & 127) + (row >> 7)

        kn[:, 640:768] = mark(
            256, 0, lambda r: new_position(r) < n0, lambda r: new_position(r) >= n0
        )

    for i, source in enumerate(sources):

        @pl.when(step == i)
        def _():
            part[...] = source[...]

    step = step + first
    rows = HEADS * TOK
    t0 = ((ctx + turn_of(step)) & 3) * TOK
    lane = iota((TOK, 128), 1)
    token = iota((TOK, 128), 0) + t0
    flags = jnp.where(
        ((lane == 0) & (token < n0)) | ((lane == 1) & (token >= n0)), 1.0, 0.0
    ).astype(BF)
    for j in range(HEADS):
        at = slice(j * TOK, (j + 1) * TOK)
        q_out[0, at, 0:512] = jnp.dot(
            part[:, j * 128 : (j + 1) * 128], ka_ref[j], preferred_element_type=F32
        ).astype(BF)
        rope = part[:, 512 + (j // 2) * 128 : 640 + (j // 2) * 128]
        keep = lane < 64 if j % 2 == 0 else lane >= 64
        q_out[0, at, 512:640] = jnp.where(keep, rope, jnp.zeros_like(rope))
        q_out[0, at, 640:768] = flags

    visible = t0 + TOK > ctx * TOK

    @pl.when(visible)
    def _():
        key = iota((rows, 256), 1)
        position = ctx * TOK + 2 * (key & 127) + (key >> 7)
        here = jnp.concatenate([iota((TOK, 256), 0)] * HEADS, axis=0) + t0
        seen_keys = (position <= here) & ((key & 127) < 80)
        scores = jnp.where(seen_keys, product(q_out[0], kn[...]), -BIG)
        top = jnp.maximum(
            jnp.full((rows, 128), -BIG, F32), jnp.max(scores, axis=1, keepdims=True)
        )
        weight = jnp.exp2((scores - wide(top, 256)) * (SCALE * LOG2E))
        mx_out[0] = top
        sm_out[0] = jnp.zeros((rows, 128), F32) + jnp.sum(weight, axis=1, keepdims=True)
        acc_out[0] = jnp.dot(weight.astype(BF), kn[:, 0:512], preferred_element_type=F32)

    @pl.when(jnp.logical_not(visible))
    def _():
        mx_out[0] = jnp.full((rows, 128), -BIG, F32)
        sm_out[0] = jnp.zeros((rows, 128), F32)
        acc_out[0] = jnp.zeros((rows, 512), F32)


def attend_kernel(
    ids, table,
    q_ref, acc0, mx0, sm0, va_ref, mark_ref, a0, am, ap, b0, bm, bp,
    out_ref,
    kc, kb, acc, mx, sm, sem,
):
    step = pl.program_id(0)
    core = ids[2] & 1
    end0 = table[SLOTS]
    end1 = table[SLOTS + 1]
    n0 = table[SLOTS + 2]

    @pl.when(step == 0)
    def _():
        marks = pltpu.make_async_copy(mark_ref, kb.at[:, pl.ds(640, 128)], sem.at[2])
        marks.start()
        for w, (own, first, second) in enumerate(((a0, am, ap), (b0, bm, bp))):
            pltpu.make_async_copy(own, kc.at[w, 0], sem.at[w]).start()
            pltpu.make_async_copy(first, kc.at[w, 1, pl.ds(0, 4)], sem.at[w]).start()
            pltpu.make_async_copy(second, kc.at[w, 1, pl.ds(4, 4)], sem.at[w]).start()
        for w in range(2):
            pltpu.make_async_copy(kc.at[w], kc.at[w], sem.at[w]).wait()
            slot = core if w == 0 else 1 - core

            def shape_up(p, _):
                at = table[p * 2 + slot] * BLK
                for half in range(2):
                    block = kc[w, half, p]
                    ropes = both_ropes(block[:, 1024:1152])
                    for parity in range(2):
                        to = pl.ds(pl.multiple_of(at + half * 64 + parity * 32, 32), 32)
                        kb[to, 0:512] = block[:, parity * 512 : parity * 512 + 512]
                        kb[to, 512:640] = ropes[parity]
                return 0

            lax.fori_loop(0, 8, shape_up, 0, unroll=True)
        marks.wait()

    t0 = ((ids[1] + turn_of(step)) & 3) * TOK
    low = jnp.where(t0 < n0, 0, end0)
    high = jnp.where(t0 + TOK > n0, end1, end0)
    extent = high - low

    def chunk(size):
        at = pl.ds(pl.multiple_of(jnp.minimum(low, KEYS - size), BLK), size)
        scores = product(q_ref[0], kb[at, :])
        before = mx0[0]
        top = jnp.maximum(before, jnp.max(scores, axis=1, keepdims=True))
        keep = jnp.exp2((before - top) * (SCALE * LOG2E))
        weight = jnp.exp2((scores - wide(top, size)) * (SCALE * LOG2E))
        mx[...] = top
        sm[...] = sm0[0] * keep + jnp.sum(weight, axis=1, keepdims=True)
        acc[...] = acc0[0] * wide(keep, 512) + jnp.dot(
            weight.astype(BF), kb[at, 0:512], preferred_element_type=F32
        )

    sizes = (0, 128, 512, 1024, 1536, 2048)
    for small, size in zip(sizes, sizes[1:]):

        @pl.when((extent > small) & (extent <= size))
        def _():
            chunk(size)

    @pl.when(extent <= 0)
    def _():
        acc[...], mx[...], sm[...] = acc0[0], mx0[0], sm0[0]

    lane16 = iota((16, 128), 1)
    stats = jnp.zeros((16, 128), F32)
    heads = []
    for j in range(HEADS):
        at = slice(j * TOK, (j + 1) * TOK)
        mass = sm[at, :]
        none = mass == 0.0
        safe = jnp.where(none, 1.0, mass)
        lse = jnp.where(none, -BIG, mx[at, :] * SCALE + jnp.log(safe))
        latent = (acc[at, :] * wide(1.0 / safe, 512)).astype(BF)
        heads.append(jnp.dot(latent, va_ref[j], preferred_element_type=F32).astype(BF))
        one = lse.astype(BF).astype(F32)
        two = (lse - one).astype(BF).astype(F32)
        three = lse - one - two
        for k in range(TOK // 16):
            base = 12 * k + 3 * j
            cut = slice(k * 16, (k + 1) * 16)
            for i, value in enumerate((one, two, three)):
                stats = jnp.where(lane16 == base + i, value[cut], stats)

    for j in range(HEADS):
        out_ref[0, j * TOK : (j + 1) * TOK, :] = heads[j]
    out_ref[0, HEADS * TOK : SENT, :] = stats.astype(BF)


def merge_kernel(got_ref, head_ref):
    lane_in = iota((128, 512), 0)
    lane_head = iota((128, 512), 1) // 128
    stats = jnp.concatenate([got_ref[c, HEADS * TOK : SENT, :] for c in range(4)], axis=0)
    for k in range(TOK // 16):
        pickup = ((lane_in >= 12 * k + 3 * lane_head) & (lane_in < 12 * k + 3 * lane_head + 3))
        lse = jnp.dot(stats, pickup.astype(BF), preferred_element_type=F32)
        lse = [lse[c * 16 : (c + 1) * 16] for c in range(4)]
        top = jnp.maximum(jnp.maximum(lse[0], lse[1]), jnp.maximum(lse[2], lse[3]))
        weight = [jnp.exp(v - top) for v in lse]
        total = weight[0] + weight[1] + weight[2] + weight[3]
        for j in range(HEADS):
            at = slice(j * TOK + k * 16, j * TOK + (k + 1) * 16)
            cut = slice(j * 128, (j + 1) * 128)
            mixed = sum(w[:, cut] * got_ref[c, at, :].astype(F32) for c, w in enumerate(weight))
            head_ref[k * 16 : (k + 1) * 16, cut] = (mixed / total[:, cut]).astype(BF)


def project_kernel(ids, head_ref, other_ref, w_ref, x_ref, out_ref):
    core = ids[2] & 1
    for y in range(4):
        column = pl.multiple_of((2 * y + core) * 896, 128)
        total = jnp.dot(
            head_ref[...], w_ref[:, pl.ds(column, 896)], preferred_element_type=F32
        )
        total += jnp.dot(
            other_ref[...], x_ref[:, y * 896 : (y + 1) * 896], preferred_element_type=F32
        )
        out_ref[y] = total.astype(BF)


def shift(value, axis, by, size):
    return lax.ppermute(value, axis, [(i, (i + by) % size) for i in range(size)])


def swap_core(value):
    return lax.ppermute(value, "head", [(i, i ^ 1) for i in range(8)])


def whole(*shape):
    return pl.BlockSpec(shape, lambda i, *_: (0,) * len(shape))


def pin(value):
    return pltpu.with_memory_space_constraint(value, pltpu.HBM)


def prepare(ids, hit_holder, prior, counts, queries, key_absorb, new_latent, first, before=()):
    own = first == 0
    rows = HEADS * TOK
    tile = lambda n: pl.BlockSpec((1, rows, n), lambda i, *_: (i + first, 0, 0))
    kept = [((KW, BF), 0), ((512, F32), 1), ((128, F32), 2), ((128, F32), 3)]
    out_specs = [tile(shape[0]) for shape, _ in kept]
    out_shape = [pltpu.HBM((4, rows, n), kind) for (n, kind), _ in kept]
    scratch = [pltpu.VMEM((TOK, 768), BF), pltpu.VMEM((256, KW), BF)]
    aliases = {}
    if own:
        out_specs += [whole(KEYS, 128), pl.BlockSpec(memory_space=pltpu.SMEM)]
        out_shape += [pltpu.HBM((KEYS, 128), BF), jax.ShapeDtypeStruct((32,), jnp.int32)]
        scratch += [pltpu.SMEM((8,), jnp.int32)]
    else:
        before = [pin(value) for value in before]
        aliases = {4 + len(queries) + 2 + i: i for i in range(4)}
    return pl.pallas_call(
        partial(ready_kernel, first, len(queries)),
        grid_spec=pltpu.PrefetchScalarGridSpec(
            num_scalar_prefetch=4,
            grid=(len(queries),),
            in_specs=[whole(*value.shape) for value in queries]
            + [whole(HEADS, 128, 512), whole(80, WIDE2)]
            + [pl.BlockSpec(memory_space=pltpu.HBM)] * len(before),
            out_specs=out_specs,
            scratch_shapes=scratch,
        ),
        out_shape=out_shape,
        input_output_aliases=aliases,
        compiler_params=pltpu.CompilerParams(vmem_limit_bytes=16 * 2**20),
        cost_estimate=pl.CostEstimate(
            flops=10**9 * len(queries),
            bytes_accessed=4 * 10**6 * len(queries),
            transcendentals=10**6,
        ),
        name=("prepare_own", "prepare_near", "", "prepare_far")[first],
    )(
        ids, hit_holder, prior, counts,
        *queries,
        pin(key_absorb),
        pin(new_latent),
        *before,
    )


def attend(ids, ready, pieces, value_absorb):
    q_all, acc0, mx0, sm0, marks = [pin(value) for value in ready[:5]]
    rows = HEADS * TOK
    tile = lambda n: pl.BlockSpec((1, rows, n), lambda i, *_: (i, 0, 0))
    return pl.pallas_call(
        attend_kernel,
        grid_spec=pltpu.PrefetchScalarGridSpec(
            num_scalar_prefetch=2,
            grid=(4,),
            in_specs=[tile(KW), tile(512), tile(128), tile(128), whole(HEADS, 512, 128)]
            + [pl.BlockSpec(memory_space=pl.ANY)] * 7,
            out_specs=pl.BlockSpec(
                (1, SENT, 128), lambda i, ids, _: ((ids[1] + turn_of(i)) & 3, 0, 0)
            ),
            scratch_shapes=[
                pltpu.VMEM((2, 2, 8, 32, WIDE2), BF),
                pltpu.VMEM((KEYS, KW), BF),
                pltpu.VMEM((rows, 512), F32),
                pltpu.VMEM((rows, 128), F32),
                pltpu.VMEM((rows, 128), F32),
                pltpu.SemaphoreType.DMA((3,)),
            ],
        ),
        out_shape=jax.ShapeDtypeStruct((4, SENT, 128), BF),
        compiler_params=pltpu.CompilerParams(vmem_limit_bytes=27 * 2**20),
        cost_estimate=pl.CostEstimate(
            flops=12 * 10**9, bytes_accessed=15 * 10**6, transcendentals=5 * 10**6
        ),
        name="attend",
    )(
        ids, ready[5], q_all, acc0, mx0, sm0, pin(value_absorb), marks,
        *pieces,
    )


def local(
    query_nope, query_rope, new_latent, cache_pool, hit_holder, hit_block,
    prior_blocks, new_counts, key_absorb, value_absorb, out_weight,
):
    ids = jnp.stack(
        [lax.axis_index("pool"), lax.axis_index("ctx"), lax.axis_index("head")]
    ).astype(jnp.int32)

    half = 32 * WIDE2
    prior = prior_blocks.T
    counts = new_counts.T
    picked, queries = pl.pallas_call(
        pick_kernel,
        grid_spec=pltpu.PrefetchScalarGridSpec(
            num_scalar_prefetch=2,
            grid=(1,),
            in_specs=[
                pl.BlockSpec((16, half), lambda i, ids, _: (0, (ids[2] >> 1) & 1)),
                whole(8, 64),
                whole(8, 64),
                whole(TOK, 512),
                whole(TOK, 256),
            ],
            out_specs=[whole(8, 32, WIDE2), whole(TOK, 768)],
        ),
        out_shape=[
            jax.ShapeDtypeStruct((8, 32, WIDE2), BF),
            jax.ShapeDtypeStruct((TOK, 768), BF),
        ],
        name="pick_blocks",
    )(ids, prior, cache_pool, hit_holder, hit_block, query_nope, query_rope)

    qm = shift(queries, "ctx", 1, 4)
    qp = shift(queries, "ctx", -1, 4)
    q2 = shift(queries, "ctx", 2, 4)
    a0 = lax.all_to_all(picked, "pool", split_axis=0, concat_axis=0, tiled=True)

    ready = partial(prepare, ids, hit_holder, prior, counts)
    state = ready((pin(queries),), key_absorb, new_latent, 0)
    state, marks, table = state[:4], state[4], state[5]
    state = ready((qm, qp), key_absorb, new_latent, 1, state)
    near, a0 = lax.optimization_barrier((state[0], a0))
    am = shift(a0[:4], "head", 2, 8)
    ap = shift(a0[4:], "head", -2, 8)
    b0 = swap_core(a0)
    state = ready((q2,), key_absorb, new_latent, 3, (near, *state[1:]))
    far, am, ap = lax.optimization_barrier((state[0], am, ap))
    bm = swap_core(am)
    bp = swap_core(ap)
    partial_out = attend(
        ids,
        (far, *state[1:], marks, table),
        (a0, am, ap, b0, bm, bp),
        value_absorb,
    )
    partial_out, late_weight = lax.optimization_barrier((partial_out, out_weight))
    got = lax.all_to_all(partial_out, "ctx", split_axis=0, concat_axis=0, tiled=True)
    other_columns = [
        lax.dynamic_slice(late_weight, (0, (2 * y + 1 - (ids[2] & 1)) * 896), (512, 896))
        for y in range(4)
    ]
    other_weight = swap_core(jnp.concatenate(other_columns, axis=1))

    heads = pl.pallas_call(
        merge_kernel,
        out_shape=jax.ShapeDtypeStruct((TOK, 512), BF),
        compiler_params=pltpu.CompilerParams(vmem_limit_bytes=8 * 2**20),
        name="merge",
    )(got)
    other_heads = swap_core(heads)
    vmem = pl.BlockSpec(memory_space=pltpu.VMEM)
    shares = pl.pallas_call(
        project_kernel,
        grid_spec=pltpu.PrefetchScalarGridSpec(
            num_scalar_prefetch=1,
            in_specs=[vmem] * 4,
            out_specs=vmem,
        ),
        out_shape=jax.ShapeDtypeStruct((4, TOK, 896), BF),
        compiler_params=pltpu.CompilerParams(vmem_limit_bytes=24 * 2**20),
        name="project",
    )(ids, heads, other_heads, out_weight, other_weight)
    shares = lax.all_to_all(
        shares, "head", split_axis=0, concat_axis=0, tiled=True,
        axis_index_groups=[[0, 2, 4, 6], [1, 3, 5, 7]],
    )
    return jnp.sum(shares.astype(F32), axis=0).astype(BF)


def solution(mesh):
    return jax.shard_map(
        local,
        mesh=mesh,
        in_specs=(
            P(("pool", "ctx"), "head"),
            P(("pool", "ctx"), "head"),
            P(("pool", "ctx"), None),
            P(("pool", "ctx"), None),
            P(),
            P(),
            P(),
            P(),
            P("head", None, None),
            P("head", None, None),
            P("head", None),
        ),
        out_specs=P(("pool", "ctx"), "head"),
        check_vma=False,
    )
```

```python
from functools import partial

import jax
import jax.numpy as jnp
from jax import lax
from jax.experimental import pallas as pl
from jax.experimental.pallas import tpu as pltpu
from jax.sharding import PartitionSpec as P

KV_RANK = 512
ROPE = 64
QK_NOPE = 128
VD = 128
BLK = 128
PAIRS = BLK // 2
WIDE2 = 2 * (KV_RANK + ROPE)
HEADS = 4
TOK = 160
SLOTS = 16
KEYS = SLOTS * BLK
KW = 768
BIG = 2.0**100
SCALE = (QK_NOPE + ROPE) ** (-0.5)
LOG2E = 1.4426950408889634
BF = jnp.bfloat16
F32 = jnp.float32
STAT = 16
SENT = HEADS * TOK + STAT
ORDER = (0, 3, 1, 2)


def iota(shape, dim):
    return lax.broadcasted_iota(jnp.int32, shape, dim)


def pick_kernel(
    ids, prior, cache_ref, holder_ref, block_ref, nope_ref, rope_ref, out_ref, query_ref, onehot_ref
):
    @pl.when(pl.program_id(0) == 0)
    def _():
        query_ref[:, 0:512] = nope_ref[...]
        query_ref[:, 512:768] = rope_ref[...]
        onehot_ref[...] = choose(ids, prior, holder_ref, block_ref)

    stacked = jnp.concatenate(
        [cache_ref[:, p * WIDE2 : (p + 1) * WIDE2] for p in range(16)], axis=0
    )
    out = jnp.dot(onehot_ref[...], stacked, preferred_element_type=F32).astype(BF)
    even, odd, rope = align(out)
    for g in range(8):
        at = slice(g * 16, (g + 1) * 16)
        for j in range(4):
            out_ref[g, :, j * 128 : (j + 1) * 128] = even[j][at]
            out_ref[g, :, 512 + j * 128 : 640 + j * 128] = odd[j][at]
        out_ref[g, :, 1024:1152] = rope[at]


def choose(ids, prior, holder_ref, block_ref):
    me = ids[0] * 4 + ids[1]
    core = ids[2] & 1
    lane = iota((8, 64), 1)
    group = iota((8, 64), 0)
    count = jnp.zeros((8, 64), jnp.int32)
    for g in range(8):
        count = jnp.where(group == g, prior[0, g] + prior[1, g], count)
    match = (holder_ref[...] == me) & (lane < count)
    first = jnp.min(jnp.where(match, lane, 1000), axis=1, keepdims=True)
    last = jnp.max(jnp.where(match, lane, -1), axis=1, keepdims=True)
    wanted = jnp.where(core == 0, first, jnp.where(last > first, last, -2))
    chosen = match & (lane == wanted)
    index = jnp.sum(jnp.where(chosen, block_ref[...] + 1, 0), axis=1, keepdims=True) - 1
    spread = (iota((128, 8), 0) // 16 == iota((128, 8), 1)).astype(BF)
    rows_index = jnp.dot(
        spread,
        jnp.broadcast_to(index.astype(F32), (8, 256)).astype(BF),
        preferred_element_type=F32,
    )
    row = iota((128, 256), 0)
    col = iota((128, 256), 1)
    return ((col // 16 == row % 16) & ((col % 16).astype(F32) == rows_index)).astype(BF)


def align(rows):
    low = iota((rows.shape[0], 128), 1) < 64
    tile = [rows[:, j * 128 : (j + 1) * 128] for j in range(9)]
    flip = {j: pltpu.roll(tile[j].astype(F32), 64, 1).astype(BF) for j in range(5, 9)}
    flip[4] = pltpu.roll(tile[4].astype(F32), 64, 1).astype(BF)
    odd = [jnp.where(low, flip[4 + j], flip[5 + j]) for j in range(4)]
    return tile[:4], odd, jnp.where(low, tile[4], tile[8])


def both_ropes(tile):
    low = iota(tile.shape, 1) < 64
    flip = pltpu.roll(tile.astype(F32), 64, 1).astype(BF)
    return jnp.where(low, tile, flip), jnp.where(low, flip, tile)


def wide(value, n):
    return jnp.concatenate([value] * (n // 128), axis=1)


def turn_of(step):
    return jnp.where(step == 0, 0, jnp.where(step == 1, 3, jnp.where(step == 2, 1, 2)))


def product(queries, keys):
    return lax.dot_general(
        queries, keys, (((1,), (1,)), ((), ())), preferred_element_type=F32
    )


def mark(n, base, keys0, keys1):
    row = iota((n, 128), 0) + base
    lane = iota((n, 128), 1)
    miss0 = (lane == 0) & jnp.logical_not(keys0(row))
    miss1 = (lane == 1) & jnp.logical_not(keys1(row))
    return jnp.where(miss0 | miss1, -BIG, 0.0).astype(BF)


def plan(ids, holder, prior, counts, mark_out, table, seen):
    group = ids[0]
    for i in range(SLOTS):
        table[i] = -1
    for i in range(8):
        seen[i] = 0
    own = prior[0, group]
    total = own + prior[1, group]

    def entry(e, carry):
        filled, mine = carry
        where = holder[group, e]
        hit = (where & 3) == ids[1]
        p = where >> 2

        @pl.when(hit)
        def _():
            s = seen[p]
            seen[p] = s + 1
            table[p * 2 + s] = filled

        add = hit.astype(jnp.int32)
        return filled + add, mine + jnp.where(e < own, add, 0)

    filled, mine = lax.fori_loop(0, total, entry, (jnp.int32(0), jnp.int32(0)))
    end0 = mine * BLK
    end1 = filled * BLK
    table[SLOTS] = end0
    table[SLOTS + 1] = end1
    table[SLOTS + 2] = counts[0, group]
    for i in range(SLOTS + 3, 32):
        table[i] = 0
    for i in range(SLOTS):
        dead = table[i] < 0

        @pl.when(dead)
        def _():
            table[i] = filled

        filled = filled + dead.astype(jnp.int32)

    def marks(i, _):
        at = pl.multiple_of(i * BLK, BLK)
        mark_out[pl.ds(at, BLK), :] = mark(
            BLK, at, lambda r: r < end0, lambda r: (r >= end0) & (r < end1)
        )
        return 0

    lax.fori_loop(0, SLOTS, marks, 0)


def ready_kernel(first, count, ids, holder, prior, counts, *refs):
    own = first == 0
    sources, refs = refs[:count], refs[count:]
    ka_ref, nl_ref = refs[:2]
    if own:
        q_out, acc_out, mx_out, sm_out, mark_out, table, part, kn, seen = refs[2:]
    else:
        q_out, acc_out, mx_out, sm_out, part, kn = refs[6:]
    step = pl.program_id(0)
    ctx = ids[1]
    n0 = counts[0, ids[0]]

    @pl.when(step == 0)
    def _():
        if own:
            plan(ids, holder, prior, counts, mark_out, table, seen)
        even, odd, rope = align(nl_ref[...])
        rope = both_ropes(rope)
        kn[...] = jnp.zeros(kn.shape, BF)
        for parity, latent in enumerate((even, odd)):
            at = slice(parity * 128, parity * 128 + 80)
            for j in range(4):
                kn[at, j * 128 : (j + 1) * 128] = latent[j]
            kn[at, 512:640] = rope[parity]

        def new_position(row):
            return ctx * TOK + 2 * (row & 127) + (row >> 7)

        kn[:, 640:768] = mark(
            256, 0, lambda r: new_position(r) < n0, lambda r: new_position(r) >= n0
        )

    for i, source in enumerate(sources):

        @pl.when(step == i)
        def _():
            part[...] = source[...]

    step = step + first
    rows = HEADS * TOK
    t0 = ((ctx + turn_of(step)) & 3) * TOK
    lane = iota((TOK, 128), 1)
    token = iota((TOK, 128), 0) + t0
    flags = jnp.where(
        ((lane == 0) & (token < n0)) | ((lane == 1) & (token >= n0)), 1.0, 0.0
    ).astype(BF)
    for j in range(HEADS):
        at = slice(j * TOK, (j + 1) * TOK)
        q_out[0, at, 0:512] = jnp.dot(
            part[:, j * 128 : (j + 1) * 128], ka_ref[j], preferred_element_type=F32
        ).astype(BF)
        rope = part[:, 512 + (j // 2) * 128 : 640 + (j // 2) * 128]
        keep = lane < 64 if j % 2 == 0 else lane >= 64
        q_out[0, at, 512:640] = jnp.where(keep, rope, jnp.zeros_like(rope))
        q_out[0, at, 640:768] = flags

    visible = t0 + TOK > ctx * TOK

    @pl.when(visible)
    def _():
        key = iota((rows, 256), 1)
        position = ctx * TOK + 2 * (key & 127) + (key >> 7)
        here = jnp.concatenate([iota((TOK, 256), 0)] * HEADS, axis=0) + t0
        seen_keys = (position <= here) & ((key & 127) < 80)
        scores = jnp.where(seen_keys, product(q_out[0], kn[...]), -BIG)
        top = jnp.maximum(
            jnp.full((rows, 128), -BIG, F32), jnp.max(scores, axis=1, keepdims=True)
        )
        weight = jnp.exp2((scores - wide(top, 256)) * (SCALE * LOG2E))
        mx_out[0] = top
        sm_out[0] = jnp.zeros((rows, 128), F32) + jnp.sum(weight, axis=1, keepdims=True)
        acc_out[0] = jnp.dot(weight.astype(BF), kn[:, 0:512], preferred_element_type=F32)

    @pl.when(jnp.logical_not(visible))
    def _():
        mx_out[0] = jnp.full((rows, 128), -BIG, F32)
        sm_out[0] = jnp.zeros((rows, 128), F32)
        acc_out[0] = jnp.zeros((rows, 512), F32)


def attend_kernel(
    ids, table,
    q_ref, acc0, mx0, sm0, va_ref, mark_ref, a0, am, ap, b0, bm, bp,
    out_ref,
    kc, kb, acc, mx, sm, sem,
):
    step = pl.program_id(0)
    core = ids[2] & 1
    end0 = table[SLOTS]
    end1 = table[SLOTS + 1]
    n0 = table[SLOTS + 2]

    @pl.when(step == 0)
    def _():
        marks = pltpu.make_async_copy(mark_ref, kb.at[:, pl.ds(640, 128)], sem.at[2])
        marks.start()
        for w, (own, first, second) in enumerate(((a0, am, ap), (b0, bm, bp))):
            pltpu.make_async_copy(own, kc.at[w, 0], sem.at[w]).start()
            pltpu.make_async_copy(first, kc.at[w, 1, pl.ds(0, 4)], sem.at[w]).start()
            pltpu.make_async_copy(second, kc.at[w, 1, pl.ds(4, 4)], sem.at[w]).start()
        for w in range(2):
            pltpu.make_async_copy(kc.at[w], kc.at[w], sem.at[w]).wait()
            slot = core if w == 0 else 1 - core

            def shape_up(p, _):
                at = table[p * 2 + slot] * BLK
                for half in range(2):
                    block = kc[w, half, p]
                    ropes = both_ropes(block[:, 1024:1152])
                    for parity in range(2):
                        to = pl.ds(pl.multiple_of(at + half * 64 + parity * 32, 32), 32)
                        kb[to, 0:512] = block[:, parity * 512 : parity * 512 + 512]
                        kb[to, 512:640] = ropes[parity]
                return 0

            lax.fori_loop(0, 8, shape_up, 0, unroll=True)
        marks.wait()

    t0 = ((ids[1] + turn_of(step)) & 3) * TOK
    low = jnp.where(t0 < n0, 0, end0)
    high = jnp.where(t0 + TOK > n0, end1, end0)
    extent = high - low

    def chunk(size):
        at = pl.ds(pl.multiple_of(jnp.minimum(low, KEYS - size), BLK), size)
        scores = product(q_ref[0], kb[at, :])
        before = mx0[0]
        top = jnp.maximum(before, jnp.max(scores, axis=1, keepdims=True))
        keep = jnp.exp2((before - top) * (SCALE * LOG2E))
        weight = jnp.exp2((scores - wide(top, size)) * (SCALE * LOG2E))
        mx[...] = top
        sm[...] = sm0[0] * keep + jnp.sum(weight, axis=1, keepdims=True)
        acc[...] = acc0[0] * wide(keep, 512) + jnp.dot(
            weight.astype(BF), kb[at, 0:512], preferred_element_type=F32
        )

    sizes = (0, 128, 512, 1024, 1536, 2048)
    for small, size in zip(sizes, sizes[1:]):

        @pl.when((extent > small) & (extent <= size))
        def _():
            chunk(size)

    @pl.when(extent <= 0)
    def _():
        acc[...], mx[...], sm[...] = acc0[0], mx0[0], sm0[0]

    lane16 = iota((16, 128), 1)
    stats = jnp.zeros((16, 128), F32)
    heads = []
    for j in range(HEADS):
        at = slice(j * TOK, (j + 1) * TOK)
        mass = sm[at, :]
        none = mass == 0.0
        safe = jnp.where(none, 1.0, mass)
        lse = jnp.where(none, -BIG, mx[at, :] * SCALE + jnp.log(safe))
        latent = (acc[at, :] * wide(1.0 / safe, 512)).astype(BF)
        heads.append(jnp.dot(latent, va_ref[j], preferred_element_type=F32).astype(BF))
        one = lse.astype(BF).astype(F32)
        two = (lse - one).astype(BF).astype(F32)
        three = lse - one - two
        for k in range(TOK // 16):
            base = 12 * k + 3 * j
            cut = slice(k * 16, (k + 1) * 16)
            for i, value in enumerate((one, two, three)):
                stats = jnp.where(lane16 == base + i, value[cut], stats)

    for j in range(HEADS):
        out_ref[0, j * TOK : (j + 1) * TOK, :] = heads[j]
    out_ref[0, HEADS * TOK : SENT, :] = stats.astype(BF)


def merge_kernel(got_ref, head_ref):
    lane_in = iota((128, 512), 0)
    lane_head = iota((128, 512), 1) // 128
    stats = jnp.concatenate([got_ref[c, HEADS * TOK : SENT, :] for c in range(4)], axis=0)
    for k in range(TOK // 16):
        pickup = ((lane_in >= 12 * k + 3 * lane_head) & (lane_in < 12 * k + 3 * lane_head + 3))
        lse = jnp.dot(stats, pickup.astype(BF), preferred_element_type=F32)
        lse = [lse[c * 16 : (c + 1) * 16] for c in range(4)]
        top = jnp.maximum(jnp.maximum(lse[0], lse[1]), jnp.maximum(lse[2], lse[3]))
        weight = [jnp.exp(v - top) for v in lse]
        total = weight[0] + weight[1] + weight[2] + weight[3]
        for j in range(HEADS):
            at = slice(j * TOK + k * 16, j * TOK + (k + 1) * 16)
            cut = slice(j * 128, (j + 1) * 128)
            mixed = sum(w[:, cut] * got_ref[c, at, :].astype(F32) for c, w in enumerate(weight))
            head_ref[k * 16 : (k + 1) * 16, cut] = (mixed / total[:, cut]).astype(BF)


def project_kernel(ids, head_ref, other_ref, w_ref, x_ref, out_ref):
    core = ids[2] & 1
    for y in range(4):
        column = pl.multiple_of((2 * y + core) * 896, 128)
        total = jnp.dot(
            head_ref[...], w_ref[:, pl.ds(column, 896)], preferred_element_type=F32
        )
        total += jnp.dot(
            other_ref[...], x_ref[:, pl.ds(column, 896)], preferred_element_type=F32
        )
        out_ref[y] = total.astype(BF)


def shift(value, axis, by, size):
    return lax.ppermute(value, axis, [(i, (i + by) % size) for i in range(size)])


def swap_core(value):
    return lax.ppermute(value, "head", [(i, i ^ 1) for i in range(8)])


def whole(*shape):
    return pl.BlockSpec(shape, lambda i, *_: (0,) * len(shape))


def pin(value):
    return pltpu.with_memory_space_constraint(value, pltpu.HBM)


def prepare(ids, hit_holder, prior, counts, queries, key_absorb, new_latent, first, before=()):
    own = first == 0
    rows = HEADS * TOK
    tile = lambda n: pl.BlockSpec((1, rows, n), lambda i, *_: (i + first, 0, 0))
    kept = [((KW, BF), 0), ((512, F32), 1), ((128, F32), 2), ((128, F32), 3)]
    out_specs = [tile(shape[0]) for shape, _ in kept]
    out_shape = [pltpu.HBM((4, rows, n), kind) for (n, kind), _ in kept]
    scratch = [pltpu.VMEM((TOK, 768), BF), pltpu.VMEM((256, KW), BF)]
    aliases = {}
    if own:
        out_specs += [whole(KEYS, 128), pl.BlockSpec(memory_space=pltpu.SMEM)]
        out_shape += [pltpu.HBM((KEYS, 128), BF), jax.ShapeDtypeStruct((32,), jnp.int32)]
        scratch += [pltpu.SMEM((8,), jnp.int32)]
    else:
        before = [pin(value) for value in before]
        aliases = {4 + len(queries) + 2 + i: i for i in range(4)}
    return pl.pallas_call(
        partial(ready_kernel, first, len(queries)),
        grid_spec=pltpu.PrefetchScalarGridSpec(
            num_scalar_prefetch=4,
            grid=(len(queries),),
            in_specs=[whole(*value.shape) for value in queries]
            + [whole(HEADS, 128, 512), whole(80, WIDE2)]
            + [pl.BlockSpec(memory_space=pltpu.HBM)] * len(before),
            out_specs=out_specs,
            scratch_shapes=scratch,
        ),
        out_shape=out_shape,
        input_output_aliases=aliases,
        compiler_params=pltpu.CompilerParams(vmem_limit_bytes=16 * 2**20),
        cost_estimate=pl.CostEstimate(
            flops=10**9 * len(queries),
            bytes_accessed=4 * 10**6 * len(queries),
            transcendentals=10**6,
        ),
        name=("prepare_own", "prepare_near", "", "prepare_far")[first],
    )(
        ids, hit_holder, prior, counts,
        *queries,
        pin(key_absorb),
        pin(new_latent),
        *before,
    )


def attend(ids, ready, pieces, value_absorb):
    q_all, acc0, mx0, sm0, marks = [pin(value) for value in ready[:5]]
    rows = HEADS * TOK
    tile = lambda n: pl.BlockSpec((1, rows, n), lambda i, *_: (i, 0, 0))
    return pl.pallas_call(
        attend_kernel,
        grid_spec=pltpu.PrefetchScalarGridSpec(
            num_scalar_prefetch=2,
            grid=(4,),
            in_specs=[tile(KW), tile(512), tile(128), tile(128), whole(HEADS, 512, 128)]
            + [pl.BlockSpec(memory_space=pl.ANY)] * 7,
            out_specs=pl.BlockSpec(
                (1, SENT, 128), lambda i, ids, _: ((ids[1] + turn_of(i)) & 3, 0, 0)
            ),
            scratch_shapes=[
                pltpu.VMEM((2, 2, 8, 32, WIDE2), BF),
                pltpu.VMEM((KEYS, KW), BF),
                pltpu.VMEM((rows, 512), F32),
                pltpu.VMEM((rows, 128), F32),
                pltpu.VMEM((rows, 128), F32),
                pltpu.SemaphoreType.DMA((3,)),
            ],
        ),
        out_shape=jax.ShapeDtypeStruct((4, SENT, 128), BF),
        compiler_params=pltpu.CompilerParams(vmem_limit_bytes=27 * 2**20),
        cost_estimate=pl.CostEstimate(
            flops=12 * 10**9, bytes_accessed=15 * 10**6, transcendentals=5 * 10**6
        ),
        name="attend",
    )(
        ids, ready[5], q_all, acc0, mx0, sm0, pin(value_absorb), marks,
        *pieces,
    )


def local(
    query_nope, query_rope, new_latent, cache_pool, hit_holder, hit_block,
    prior_blocks, new_counts, key_absorb, value_absorb, out_weight,
):
    ids = jnp.stack(
        [lax.axis_index("pool"), lax.axis_index("ctx"), lax.axis_index("head")]
    ).astype(jnp.int32)

    prior = prior_blocks.T
    counts = new_counts.T
    picked, queries = pl.pallas_call(
        pick_kernel,
        grid_spec=pltpu.PrefetchScalarGridSpec(
            num_scalar_prefetch=2,
            grid=(2,),
            in_specs=[
                pl.BlockSpec((16, 16 * WIDE2), lambda i, ids, _: (0, (ids[2] & 2) + i)),
                whole(8, 64),
                whole(8, 64),
                whole(TOK, 512),
                whole(TOK, 256),
            ],
            out_specs=[
                pl.BlockSpec((8, 16, WIDE2), lambda i, *_: (0, i, 0)),
                whole(TOK, 768),
            ],
            scratch_shapes=[pltpu.VMEM((128, 256), BF)],
        ),
        out_shape=[
            jax.ShapeDtypeStruct((8, 32, WIDE2), BF),
            jax.ShapeDtypeStruct((TOK, 768), BF),
        ],
        name="pick_blocks",
    )(ids, prior, cache_pool, hit_holder, hit_block, query_nope, query_rope)

    qm = shift(queries, "ctx", 1, 4)
    qp = shift(queries, "ctx", -1, 4)
    q2 = shift(queries, "ctx", 2, 4)
    a0 = lax.all_to_all(picked, "pool", split_axis=0, concat_axis=0, tiled=True)

    ready = partial(prepare, ids, hit_holder, prior, counts)
    state = ready((pin(queries),), key_absorb, new_latent, 0)
    state, marks, table = state[:4], state[4], state[5]
    state = ready((qm, qp), key_absorb, new_latent, 1, state)
    near, a0 = lax.optimization_barrier((state[0], a0))
    am = shift(a0[:4], "head", 2, 8)
    ap = shift(a0[4:], "head", -2, 8)
    b0 = swap_core(a0)
    state = ready((q2,), key_absorb, new_latent, 3, (near, *state[1:]))
    far, am, ap = lax.optimization_barrier((state[0], am, ap))
    bm = swap_core(am)
    bp = swap_core(ap)
    b0, bm, bp, late_weight = lax.optimization_barrier((b0, bm, bp, out_weight))
    other_weight = swap_core(late_weight)
    partial_out = attend(
        ids,
        (far, *state[1:], marks, table),
        (a0, am, ap, b0, bm, bp),
        value_absorb,
    )
    got = lax.all_to_all(partial_out, "ctx", split_axis=0, concat_axis=0, tiled=True)

    heads = pl.pallas_call(
        merge_kernel,
        out_shape=jax.ShapeDtypeStruct((TOK, 512), BF),
        compiler_params=pltpu.CompilerParams(vmem_limit_bytes=8 * 2**20),
        name="merge",
    )(got)
    other_heads = swap_core(heads)
    vmem = pl.BlockSpec(memory_space=pltpu.VMEM)
    shares = pl.pallas_call(
        project_kernel,
        grid_spec=pltpu.PrefetchScalarGridSpec(
            num_scalar_prefetch=1,
            in_specs=[vmem] * 4,
            out_specs=vmem,
        ),
        out_shape=jax.ShapeDtypeStruct((4, TOK, 896), BF),
        compiler_params=pltpu.CompilerParams(vmem_limit_bytes=20 * 2**20),
        name="project",
    )(ids, heads, other_heads, out_weight, other_weight)
    shares = lax.all_to_all(
        shares, "head", split_axis=0, concat_axis=0, tiled=True,
        axis_index_groups=[[0, 2, 4, 6], [1, 3, 5, 7]],
    )
    return jnp.sum(shares.astype(F32), axis=0).astype(BF)


def solution(mesh):
    return jax.shard_map(
        local,
        mesh=mesh,
        in_specs=(
            P(("pool", "ctx"), "head"),
            P(("pool", "ctx"), "head"),
            P(("pool", "ctx"), None),
            P(("pool", "ctx"), None),
            P(),
            P(),
            P(),
            P(),
            P("head", None, None),
            P("head", None, None),
            P("head", None),
        ),
        out_specs=P(("pool", "ctx"), "head"),
        check_vma=False,
    )
```

```python
from functools import partial

import jax
import jax.numpy as jnp
from jax import lax
from jax.experimental import pallas as pl
from jax.experimental.pallas import tpu as pltpu
from jax.sharding import PartitionSpec as P

KV_RANK = 512
ROPE = 64
QK_NOPE = 128
VD = 128
BLK = 128
PAIRS = BLK // 2
WIDE2 = 2 * (KV_RANK + ROPE)
HEADS = 4
TOK = 160
SLOTS = 16
KEYS = SLOTS * BLK
KW = 768
BIG = 2.0**100
SCALE = (QK_NOPE + ROPE) ** (-0.5)
LOG2E = 1.4426950408889634
BF = jnp.bfloat16
F32 = jnp.float32
STAT = 16
SENT = HEADS * TOK + STAT
ORDER = (0, 3, 1, 2)


def iota(shape, dim):
    return lax.broadcasted_iota(jnp.int32, shape, dim)


def pick_kernel(
    ids, prior, cache_ref, holder_ref, block_ref, nope_ref, rope_ref, out_ref, query_ref, onehot_ref
):
    @pl.when(pl.program_id(0) == 0)
    def _():
        query_ref[:, 0:512] = nope_ref[...]
        query_ref[:, 512:768] = rope_ref[...]
        onehot_ref[...] = choose(ids, prior, holder_ref, block_ref)

    stacked = jnp.concatenate(
        [cache_ref[:, p * WIDE2 : (p + 1) * WIDE2] for p in range(16)], axis=0
    )
    out = jnp.dot(onehot_ref[...], stacked, preferred_element_type=F32).astype(BF)
    even, odd, rope = align(out)
    for g in range(8):
        at = slice(g * 16, (g + 1) * 16)
        for j in range(4):
            out_ref[g, :, j * 128 : (j + 1) * 128] = even[j][at]
            out_ref[g, :, 512 + j * 128 : 640 + j * 128] = odd[j][at]
        out_ref[g, :, 1024:1152] = rope[at]


def choose(ids, prior, holder_ref, block_ref):
    me = ids[0] * 4 + ids[1]
    core = ids[2] & 1
    lane = iota((8, 64), 1)
    group = iota((8, 64), 0)
    count = jnp.zeros((8, 64), jnp.int32)
    for g in range(8):
        count = jnp.where(group == g, prior[0, g] + prior[1, g], count)
    match = (holder_ref[...] == me) & (lane < count)
    first = jnp.min(jnp.where(match, lane, 1000), axis=1, keepdims=True)
    last = jnp.max(jnp.where(match, lane, -1), axis=1, keepdims=True)
    wanted = jnp.where(core == 0, first, jnp.where(last > first, last, -2))
    chosen = match & (lane == wanted)
    index = jnp.sum(jnp.where(chosen, block_ref[...] + 1, 0), axis=1, keepdims=True) - 1
    spread = (iota((128, 8), 0) // 16 == iota((128, 8), 1)).astype(BF)
    rows_index = jnp.dot(
        spread,
        jnp.broadcast_to(index.astype(F32), (8, 256)).astype(BF),
        preferred_element_type=F32,
    )
    row = iota((128, 256), 0)
    col = iota((128, 256), 1)
    return ((col // 16 == row % 16) & ((col % 16).astype(F32) == rows_index)).astype(BF)


def align(rows):
    low = iota((rows.shape[0], 128), 1) < 64
    tile = [rows[:, j * 128 : (j + 1) * 128] for j in range(9)]
    flip = {j: pltpu.roll(tile[j].astype(F32), 64, 1).astype(BF) for j in range(5, 9)}
    flip[4] = pltpu.roll(tile[4].astype(F32), 64, 1).astype(BF)
    odd = [jnp.where(low, flip[4 + j], flip[5 + j]) for j in range(4)]
    return tile[:4], odd, jnp.where(low, tile[4], tile[8])


def both_ropes(tile):
    low = iota(tile.shape, 1) < 64
    flip = pltpu.roll(tile.astype(F32), 64, 1).astype(BF)
    return jnp.where(low, tile, flip), jnp.where(low, flip, tile)


def wide(value, n):
    return jnp.concatenate([value] * (n // 128), axis=1)


def turn_of(step):
    return jnp.where(step == 0, 0, jnp.where(step == 1, 3, jnp.where(step == 2, 1, 2)))


def product(queries, keys):
    return lax.dot_general(
        queries, keys, (((1,), (1,)), ((), ())), preferred_element_type=F32
    )


def mark(n, base, keys0, keys1):
    row = iota((n, 128), 0) + base
    lane = iota((n, 128), 1)
    miss0 = (lane == 0) & jnp.logical_not(keys0(row))
    miss1 = (lane == 1) & jnp.logical_not(keys1(row))
    return jnp.where(miss0 | miss1, -BIG, 0.0).astype(BF)


def plan(ids, holder, prior, counts, mark_out, table, seen):
    group = ids[0]
    for i in range(SLOTS):
        table[i] = -1
    for i in range(8):
        seen[i] = 0
    own = prior[0, group]
    total = own + prior[1, group]

    def entry(e, carry):
        filled, mine = carry
        where = holder[group, e]
        hit = (where & 3) == ids[1]
        p = where >> 2

        @pl.when(hit)
        def _():
            s = seen[p]
            seen[p] = s + 1
            table[p * 2 + s] = filled

        add = hit.astype(jnp.int32)
        return filled + add, mine + jnp.where(e < own, add, 0)

    filled, mine = lax.fori_loop(0, total, entry, (jnp.int32(0), jnp.int32(0)))
    end0 = mine * BLK
    end1 = filled * BLK
    table[SLOTS] = end0
    table[SLOTS + 1] = end1
    table[SLOTS + 2] = counts[0, group]
    for i in range(SLOTS + 3, 32):
        table[i] = 0
    for i in range(SLOTS):
        dead = table[i] < 0

        @pl.when(dead)
        def _():
            table[i] = filled

        filled = filled + dead.astype(jnp.int32)

    def marks(i, _):
        at = pl.multiple_of(i * BLK, BLK)
        mark_out[pl.ds(at, BLK), :] = mark(
            BLK, at, lambda r: r < end0, lambda r: (r >= end0) & (r < end1)
        )
        return 0

    lax.fori_loop(0, SLOTS, marks, 0)


def ready_kernel(first, count, ids, holder, prior, counts, *refs):
    own = first == 0
    sources, refs = refs[:count], refs[count:]
    ka_ref, nl_ref = refs[:2]
    if own:
        q_out, acc_out, mx_out, sm_out, mark_out, table, part, kn, seen = refs[2:]
    else:
        q_out, acc_out, mx_out, sm_out, part, kn = refs[6:]
    step = pl.program_id(0)
    ctx = ids[1]
    n0 = counts[0, ids[0]]

    @pl.when(step == 0)
    def _():
        if own:
            plan(ids, holder, prior, counts, mark_out, table, seen)
        even, odd, rope = align(nl_ref[...])
        rope = both_ropes(rope)
        kn[...] = jnp.zeros(kn.shape, BF)
        for parity, latent in enumerate((even, odd)):
            at = slice(parity * 128, parity * 128 + 80)
            for j in range(4):
                kn[at, j * 128 : (j + 1) * 128] = latent[j]
            kn[at, 512:640] = rope[parity]

        def new_position(row):
            return ctx * TOK + 2 * (row & 127) + (row >> 7)

        kn[:, 640:768] = mark(
            256, 0, lambda r: new_position(r) < n0, lambda r: new_position(r) >= n0
        )

    for i, source in enumerate(sources):

        @pl.when(step == i)
        def _():
            part[...] = source[...]

    step = step + first
    rows = HEADS * TOK
    t0 = ((ctx + turn_of(step)) & 3) * TOK
    lane = iota((TOK, 128), 1)
    token = iota((TOK, 128), 0) + t0
    flags = jnp.where(
        ((lane == 0) & (token < n0)) | ((lane == 1) & (token >= n0)), 1.0, 0.0
    ).astype(BF)
    for j in range(HEADS):
        at = slice(j * TOK, (j + 1) * TOK)
        q_out[0, at, 0:512] = jnp.dot(
            part[:, j * 128 : (j + 1) * 128], ka_ref[j], preferred_element_type=F32
        ).astype(BF)
        rope = part[:, 512 + (j // 2) * 128 : 640 + (j // 2) * 128]
        keep = lane < 64 if j % 2 == 0 else lane >= 64
        q_out[0, at, 512:640] = jnp.where(keep, rope, jnp.zeros_like(rope))
        q_out[0, at, 640:768] = flags

    visible = t0 + TOK > ctx * TOK

    @pl.when(visible)
    def _():
        key = iota((rows, 256), 1)
        position = ctx * TOK + 2 * (key & 127) + (key >> 7)
        here = jnp.concatenate([iota((TOK, 256), 0)] * HEADS, axis=0) + t0
        seen_keys = (position <= here) & ((key & 127) < 80)
        scores = jnp.where(seen_keys, product(q_out[0], kn[...]), -BIG)
        top = jnp.maximum(
            jnp.full((rows, 128), -BIG, F32), jnp.max(scores, axis=1, keepdims=True)
        )
        weight = jnp.exp2((scores - wide(top, 256)) * (SCALE * LOG2E))
        mx_out[0] = top
        sm_out[0] = jnp.zeros((rows, 128), F32) + jnp.sum(weight, axis=1, keepdims=True)
        acc_out[0] = jnp.dot(weight.astype(BF), kn[:, 0:512], preferred_element_type=F32)

    @pl.when(jnp.logical_not(visible))
    def _():
        mx_out[0] = jnp.full((rows, 128), -BIG, F32)
        sm_out[0] = jnp.zeros((rows, 128), F32)
        acc_out[0] = jnp.zeros((rows, 512), F32)


def attend_kernel(
    ids, table,
    q_ref, acc0, mx0, sm0, va_ref, mark_ref, a0, am, ap, b0, bm, bp,
    out_ref,
    kc, kb, acc, mx, sm, sem,
):
    step = pl.program_id(0)
    core = ids[2] & 1
    end0 = table[SLOTS]
    end1 = table[SLOTS + 1]
    n0 = table[SLOTS + 2]

    @pl.when(step == 0)
    def _():
        marks = pltpu.make_async_copy(mark_ref, kb.at[:, pl.ds(640, 128)], sem.at[2])
        marks.start()
        for w, (own, first, second) in enumerate(((a0, am, ap), (b0, bm, bp))):
            pltpu.make_async_copy(own, kc.at[w, 0], sem.at[w]).start()
            pltpu.make_async_copy(first, kc.at[w, 1, pl.ds(0, 4)], sem.at[w]).start()
            pltpu.make_async_copy(second, kc.at[w, 1, pl.ds(4, 4)], sem.at[w]).start()
        for w in range(2):
            pltpu.make_async_copy(kc.at[w], kc.at[w], sem.at[w]).wait()
            slot = core if w == 0 else 1 - core

            def shape_up(p, _):
                at = table[p * 2 + slot] * BLK
                for half in range(2):
                    block = kc[w, half, p]
                    ropes = both_ropes(block[:, 1024:1152])
                    for parity in range(2):
                        to = pl.ds(pl.multiple_of(at + half * 64 + parity * 32, 32), 32)
                        kb[to, 0:512] = block[:, parity * 512 : parity * 512 + 512]
                        kb[to, 512:640] = ropes[parity]
                return 0

            lax.fori_loop(0, 8, shape_up, 0, unroll=True)
        marks.wait()

    t0 = ((ids[1] + turn_of(step)) & 3) * TOK
    low = jnp.where(t0 < n0, 0, end0)
    high = jnp.where(t0 + TOK > n0, end1, end0)
    extent = high - low

    def chunk(size):
        at = pl.ds(pl.multiple_of(jnp.minimum(low, KEYS - size), BLK), size)
        scores = product(q_ref[0], kb[at, :])
        before = mx0[0]
        top = jnp.maximum(before, jnp.max(scores, axis=1, keepdims=True))
        keep = jnp.exp2((before - top) * (SCALE * LOG2E))
        weight = jnp.exp2((scores - wide(top, size)) * (SCALE * LOG2E))
        mx[...] = top
        sm[...] = sm0[0] * keep + jnp.sum(weight, axis=1, keepdims=True)
        acc[...] = acc0[0] * wide(keep, 512) + jnp.dot(
            weight.astype(BF), kb[at, 0:512], preferred_element_type=F32
        )

    sizes = (0, 128, 512, 1024, 1536, 2048)
    for small, size in zip(sizes, sizes[1:]):

        @pl.when((extent > small) & (extent <= size))
        def _():
            chunk(size)

    @pl.when(extent <= 0)
    def _():
        acc[...], mx[...], sm[...] = acc0[0], mx0[0], sm0[0]

    lane16 = iota((16, 128), 1)
    stats = jnp.zeros((16, 128), F32)
    heads = []
    for j in range(HEADS):
        at = slice(j * TOK, (j + 1) * TOK)
        mass = sm[at, :]
        none = mass == 0.0
        safe = jnp.where(none, 1.0, mass)
        lse = jnp.where(none, -BIG, mx[at, :] * SCALE + jnp.log(safe))
        latent = (acc[at, :] * wide(1.0 / safe, 512)).astype(BF)
        heads.append(jnp.dot(latent, va_ref[j], preferred_element_type=F32).astype(BF))
        one = lse.astype(BF).astype(F32)
        two = (lse - one).astype(BF).astype(F32)
        three = lse - one - two
        for k in range(TOK // 16):
            base = 12 * k + 3 * j
            cut = slice(k * 16, (k + 1) * 16)
            for i, value in enumerate((one, two, three)):
                stats = jnp.where(lane16 == base + i, value[cut], stats)

    for j in range(HEADS):
        out_ref[0, j * TOK : (j + 1) * TOK, :] = heads[j]
    out_ref[0, HEADS * TOK : SENT, :] = stats.astype(BF)


def merge_kernel(got_ref, head_ref):
    lane_in = iota((128, 512), 0)
    lane_head = iota((128, 512), 1) // 128
    stats = jnp.concatenate([got_ref[c, HEADS * TOK : SENT, :] for c in range(4)], axis=0)
    for k in range(TOK // 16):
        pickup = ((lane_in >= 12 * k + 3 * lane_head) & (lane_in < 12 * k + 3 * lane_head + 3))
        lse = jnp.dot(stats, pickup.astype(BF), preferred_element_type=F32)
        lse = [lse[c * 16 : (c + 1) * 16] for c in range(4)]
        top = jnp.maximum(jnp.maximum(lse[0], lse[1]), jnp.maximum(lse[2], lse[3]))
        weight = [jnp.exp(v - top) for v in lse]
        total = weight[0] + weight[1] + weight[2] + weight[3]
        for j in range(HEADS):
            at = slice(j * TOK + k * 16, j * TOK + (k + 1) * 16)
            cut = slice(j * 128, (j + 1) * 128)
            mixed = sum(w[:, cut] * got_ref[c, at, :].astype(F32) for c, w in enumerate(weight))
            head_ref[k * 16 : (k + 1) * 16, cut] = (mixed / total[:, cut]).astype(BF)


def project_kernel(ids, head_ref, other_ref, w_ref, x_ref, out_ref):
    core = ids[2] & 1
    for y in range(4):
        column = pl.multiple_of((2 * y + core) * 896, 128)
        total = jnp.dot(
            head_ref[...], w_ref[:, pl.ds(column, 896)], preferred_element_type=F32
        )
        total += jnp.dot(
            other_ref[...], x_ref[:, pl.ds(column, 896)], preferred_element_type=F32
        )
        out_ref[y] = total.astype(BF)


def shift(value, axis, by, size):
    return lax.ppermute(value, axis, [(i, (i + by) % size) for i in range(size)])


def swap_core(value):
    return lax.ppermute(value, "head", [(i, i ^ 1) for i in range(8)])


def whole(*shape):
    return pl.BlockSpec(shape, lambda i, *_: (0,) * len(shape))


def pin(value):
    return pltpu.with_memory_space_constraint(value, pltpu.HBM)


def prepare(ids, hit_holder, prior, counts, queries, key_absorb, new_latent, first, before=()):
    own = first == 0
    rows = HEADS * TOK
    tile = lambda n: pl.BlockSpec((1, rows, n), lambda i, *_: (i + first, 0, 0))
    kept = [((KW, BF), 0), ((512, F32), 1), ((128, F32), 2), ((128, F32), 3)]
    out_specs = [tile(shape[0]) for shape, _ in kept]
    out_shape = [pltpu.HBM((4, rows, n), kind) for (n, kind), _ in kept]
    scratch = [pltpu.VMEM((TOK, 768), BF), pltpu.VMEM((256, KW), BF)]
    aliases = {}
    if own:
        out_specs += [whole(KEYS, 128), pl.BlockSpec(memory_space=pltpu.SMEM)]
        out_shape += [pltpu.HBM((KEYS, 128), BF), jax.ShapeDtypeStruct((32,), jnp.int32)]
        scratch += [pltpu.SMEM((8,), jnp.int32)]
    else:
        before = [pin(value) for value in before]
        aliases = {4 + len(queries) + 2 + i: i for i in range(4)}
    return pl.pallas_call(
        partial(ready_kernel, first, len(queries)),
        grid_spec=pltpu.PrefetchScalarGridSpec(
            num_scalar_prefetch=4,
            grid=(len(queries),),
            in_specs=[whole(*value.shape) for value in queries]
            + [whole(HEADS, 128, 512), whole(80, WIDE2)]
            + [pl.BlockSpec(memory_space=pltpu.HBM)] * len(before),
            out_specs=out_specs,
            scratch_shapes=scratch,
        ),
        out_shape=out_shape,
        input_output_aliases=aliases,
        compiler_params=pltpu.CompilerParams(vmem_limit_bytes=16 * 2**20),
        cost_estimate=pl.CostEstimate(
            flops=10**9 * len(queries),
            bytes_accessed=4 * 10**6 * len(queries),
            transcendentals=10**6,
        ),
        name=("prepare_own", "prepare_near", "", "prepare_far")[first],
    )(
        ids, hit_holder, prior, counts,
        *queries,
        pin(key_absorb),
        pin(new_latent),
        *before,
    )


def attend(ids, ready, pieces, value_absorb):
    q_all, acc0, mx0, sm0, marks = [pin(value) for value in ready[:5]]
    rows = HEADS * TOK
    tile = lambda n: pl.BlockSpec((1, rows, n), lambda i, *_: (i, 0, 0))
    return pl.pallas_call(
        attend_kernel,
        grid_spec=pltpu.PrefetchScalarGridSpec(
            num_scalar_prefetch=2,
            grid=(4,),
            in_specs=[tile(KW), tile(512), tile(128), tile(128), whole(HEADS, 512, 128)]
            + [pl.BlockSpec(memory_space=pl.ANY)] * 7,
            out_specs=pl.BlockSpec(
                (1, SENT, 128), lambda i, ids, _: ((ids[1] + turn_of(i)) & 3, 0, 0)
            ),
            scratch_shapes=[
                pltpu.VMEM((2, 2, 8, 32, WIDE2), BF),
                pltpu.VMEM((KEYS, KW), BF),
                pltpu.VMEM((rows, 512), F32),
                pltpu.VMEM((rows, 128), F32),
                pltpu.VMEM((rows, 128), F32),
                pltpu.SemaphoreType.DMA((3,)),
            ],
        ),
        out_shape=jax.ShapeDtypeStruct((4, SENT, 128), BF),
        compiler_params=pltpu.CompilerParams(vmem_limit_bytes=27 * 2**20),
        cost_estimate=pl.CostEstimate(
            flops=12 * 10**9, bytes_accessed=15 * 10**6, transcendentals=5 * 10**6
        ),
        name="attend",
    )(
        ids, ready[5], q_all, acc0, mx0, sm0, pin(value_absorb), marks,
        *pieces,
    )


def local(
    query_nope, query_rope, new_latent, cache_pool, hit_holder, hit_block,
    prior_blocks, new_counts, key_absorb, value_absorb, out_weight,
):
    ids = jnp.stack(
        [lax.axis_index("pool"), lax.axis_index("ctx"), lax.axis_index("head")]
    ).astype(jnp.int32)

    prior = prior_blocks.T
    counts = new_counts.T
    picked, queries = pl.pallas_call(
        pick_kernel,
        grid_spec=pltpu.PrefetchScalarGridSpec(
            num_scalar_prefetch=2,
            grid=(2,),
            in_specs=[
                pl.BlockSpec((16, 16 * WIDE2), lambda i, ids, _: (0, (ids[2] & 2) + i)),
                whole(8, 64),
                whole(8, 64),
                whole(TOK, 512),
                whole(TOK, 256),
            ],
            out_specs=[
                pl.BlockSpec((8, 16, WIDE2), lambda i, *_: (0, i, 0)),
                whole(TOK, 768),
            ],
            scratch_shapes=[pltpu.VMEM((128, 256), BF)],
        ),
        out_shape=[
            jax.ShapeDtypeStruct((8, 32, WIDE2), BF),
            jax.ShapeDtypeStruct((TOK, 768), BF),
        ],
        name="pick_blocks",
    )(ids, prior, cache_pool, hit_holder, hit_block, query_nope, query_rope)

    qm = shift(queries, "ctx", 1, 4)
    qp = shift(queries, "ctx", -1, 4)
    late_queries, qm, qp = lax.optimization_barrier((queries, qm, qp))
    q2 = shift(late_queries, "ctx", 2, 4)
    a0 = lax.all_to_all(picked, "pool", split_axis=0, concat_axis=0, tiled=True)

    ready = partial(prepare, ids, hit_holder, prior, counts)
    state = ready((pin(queries),), key_absorb, new_latent, 0)
    state, marks, table = state[:4], state[4], state[5]
    state = ready((qm, qp), key_absorb, new_latent, 1, state)
    near, a0 = lax.optimization_barrier((state[0], a0))
    am = shift(a0[:4], "head", 2, 8)
    ap = shift(a0[4:], "head", -2, 8)
    b0 = swap_core(a0)
    state = ready((q2,), key_absorb, new_latent, 3, (near, *state[1:]))
    far, am, ap = lax.optimization_barrier((state[0], am, ap))
    bm = swap_core(am)
    bp = swap_core(ap)
    b0, bm, bp, late_weight = lax.optimization_barrier((b0, bm, bp, out_weight))
    other_weight = swap_core(late_weight)
    partial_out = attend(
        ids,
        (far, *state[1:], marks, table),
        (a0, am, ap, b0, bm, bp),
        value_absorb,
    )
    got = lax.all_to_all(partial_out, "ctx", split_axis=0, concat_axis=0, tiled=True)

    heads = pl.pallas_call(
        merge_kernel,
        out_shape=jax.ShapeDtypeStruct((TOK, 512), BF),
        compiler_params=pltpu.CompilerParams(vmem_limit_bytes=8 * 2**20),
        name="merge",
    )(got)
    other_heads = swap_core(heads)
    vmem = pl.BlockSpec(memory_space=pltpu.VMEM)
    shares = pl.pallas_call(
        project_kernel,
        grid_spec=pltpu.PrefetchScalarGridSpec(
            num_scalar_prefetch=1,
            in_specs=[vmem] * 4,
            out_specs=vmem,
        ),
        out_shape=jax.ShapeDtypeStruct((4, TOK, 896), BF),
        compiler_params=pltpu.CompilerParams(vmem_limit_bytes=20 * 2**20),
        name="project",
    )(ids, heads, other_heads, out_weight, other_weight)
    shares = lax.all_to_all(
        shares, "head", split_axis=0, concat_axis=0, tiled=True,
        axis_index_groups=[[0, 2, 4, 6], [1, 3, 5, 7]],
    )
    return jnp.sum(shares.astype(F32), axis=0).astype(BF)


def solution(mesh):
    return jax.shard_map(
        local,
        mesh=mesh,
        in_specs=(
            P(("pool", "ctx"), "head"),
            P(("pool", "ctx"), "head"),
            P(("pool", "ctx"), None),
            P(("pool", "ctx"), None),
            P(),
            P(),
            P(),
            P(),
            P("head", None, None),
            P("head", None, None),
            P("head", None),
        ),
        out_specs=P(("pool", "ctx"), "head"),
        check_vma=False,
    )
```

```python
from functools import partial

import jax
import jax.numpy as jnp
from jax import lax
from jax.experimental import pallas as pl
from jax.experimental.pallas import tpu as pltpu
from jax.sharding import PartitionSpec as P

KV_RANK = 512
ROPE = 64
QK_NOPE = 128
VD = 128
BLK = 128
PAIRS = BLK // 2
WIDE2 = 2 * (KV_RANK + ROPE)
HEADS = 4
TOK = 160
SLOTS = 16
KEYS = SLOTS * BLK
KW = 768
BIG = 2.0**100
SCALE = (QK_NOPE + ROPE) ** (-0.5)
LOG2E = 1.4426950408889634
BF = jnp.bfloat16
F32 = jnp.float32
STAT = 16
SENT = HEADS * TOK + STAT
ORDER = (0, 3, 1, 2)


def iota(shape, dim):
    return lax.broadcasted_iota(jnp.int32, shape, dim)


def pick_kernel(
    ids, prior, cache_ref, holder_ref, block_ref, nope_ref, rope_ref, out_ref, query_ref,
    held, sem,
):
    size = 16 * WIDE2
    copies = []
    for i in range(2):
        column = pl.multiple_of(((ids[2] & 2) + i) * size, size)
        copies.append(
            pltpu.make_async_copy(cache_ref.at[:, pl.ds(column, size)], held.at[i], sem.at[i])
        )
        copies[i].start()
    query_ref[:, 0:512] = nope_ref[...]
    query_ref[:, 512:768] = rope_ref[...]
    onehot = choose(ids, prior, holder_ref, block_ref)
    for i in range(2):
        copies[i].wait()
        stacked = jnp.concatenate(
            [held[i, :, p * WIDE2 : (p + 1) * WIDE2] for p in range(16)], axis=0
        )
        out = jnp.dot(onehot, stacked, preferred_element_type=F32).astype(BF)
        even, odd, rope = align(out)
        to = slice(i * 16, i * 16 + 16)
        for g in range(8):
            at = slice(g * 16, (g + 1) * 16)
            for j in range(4):
                out_ref[g, to, j * 128 : (j + 1) * 128] = even[j][at]
                out_ref[g, to, 512 + j * 128 : 640 + j * 128] = odd[j][at]
            out_ref[g, to, 1024:1152] = rope[at]


def choose(ids, prior, holder_ref, block_ref):
    me = ids[0] * 4 + ids[1]
    core = ids[2] & 1
    lane = iota((8, 64), 1)
    group = iota((8, 64), 0)
    count = jnp.zeros((8, 64), jnp.int32)
    for g in range(8):
        count = jnp.where(group == g, prior[0, g] + prior[1, g], count)
    match = (holder_ref[...] == me) & (lane < count)
    first = jnp.min(jnp.where(match, lane, 1000), axis=1, keepdims=True)
    last = jnp.max(jnp.where(match, lane, -1), axis=1, keepdims=True)
    wanted = jnp.where(core == 0, first, jnp.where(last > first, last, -2))
    chosen = match & (lane == wanted)
    index = jnp.sum(jnp.where(chosen, block_ref[...] + 1, 0), axis=1, keepdims=True) - 1
    spread = (iota((128, 8), 0) // 16 == iota((128, 8), 1)).astype(BF)
    rows_index = jnp.dot(
        spread,
        jnp.broadcast_to(index.astype(F32), (8, 256)).astype(BF),
        preferred_element_type=F32,
    )
    row = iota((128, 256), 0)
    col = iota((128, 256), 1)
    return ((col // 16 == row % 16) & ((col % 16).astype(F32) == rows_index)).astype(BF)


def align(rows):
    low = iota((rows.shape[0], 128), 1) < 64
    tile = [rows[:, j * 128 : (j + 1) * 128] for j in range(9)]
    flip = {j: pltpu.roll(tile[j].astype(F32), 64, 1).astype(BF) for j in range(5, 9)}
    flip[4] = pltpu.roll(tile[4].astype(F32), 64, 1).astype(BF)
    odd = [jnp.where(low, flip[4 + j], flip[5 + j]) for j in range(4)]
    return tile[:4], odd, jnp.where(low, tile[4], tile[8])


def both_ropes(tile):
    low = iota(tile.shape, 1) < 64
    flip = pltpu.roll(tile.astype(F32), 64, 1).astype(BF)
    return jnp.where(low, tile, flip), jnp.where(low, flip, tile)


def wide(value, n):
    return jnp.concatenate([value] * (n // 128), axis=1)


def turn_of(step):
    return jnp.where(step == 0, 0, jnp.where(step == 1, 3, jnp.where(step == 2, 1, 2)))


def product(queries, keys):
    return lax.dot_general(
        queries, keys, (((1,), (1,)), ((), ())), preferred_element_type=F32
    )


def mark(n, base, keys0, keys1):
    row = iota((n, 128), 0) + base
    lane = iota((n, 128), 1)
    miss0 = (lane == 0) & jnp.logical_not(keys0(row))
    miss1 = (lane == 1) & jnp.logical_not(keys1(row))
    return jnp.where(miss0 | miss1, -BIG, 0.0).astype(BF)


def plan(ids, holder, prior, counts, mark_out, table, seen):
    group = ids[0]
    for i in range(SLOTS):
        table[i] = -1
    for i in range(8):
        seen[i] = 0
    own = prior[0, group]
    total = own + prior[1, group]

    def entry(e, carry):
        filled, mine = carry
        where = holder[group, e]
        hit = (where & 3) == ids[1]
        p = where >> 2

        @pl.when(hit)
        def _():
            s = seen[p]
            seen[p] = s + 1
            table[p * 2 + s] = filled

        add = hit.astype(jnp.int32)
        return filled + add, mine + jnp.where(e < own, add, 0)

    filled, mine = lax.fori_loop(0, total, entry, (jnp.int32(0), jnp.int32(0)))
    end0 = mine * BLK
    end1 = filled * BLK
    table[SLOTS] = end0
    table[SLOTS + 1] = end1
    table[SLOTS + 2] = counts[0, group]
    for i in range(SLOTS + 3, 32):
        table[i] = 0
    for i in range(SLOTS):
        dead = table[i] < 0

        @pl.when(dead)
        def _():
            table[i] = filled

        filled = filled + dead.astype(jnp.int32)

    def marks(i, _):
        at = pl.multiple_of(i * BLK, BLK)
        mark_out[pl.ds(at, BLK), :] = mark(
            BLK, at, lambda r: r < end0, lambda r: (r >= end0) & (r < end1)
        )
        return 0

    lax.fori_loop(0, SLOTS, marks, 0)


def ready_kernel(first, count, ids, holder, prior, counts, *refs):
    own = first == 0
    sources, refs = refs[:count], refs[count:]
    ka_ref, nl_ref = refs[:2]
    if own:
        q_out, acc_out, mx_out, sm_out, mark_out, table, part, kn, seen = refs[2:]
    else:
        q_out, acc_out, mx_out, sm_out, part, kn = refs[6:]
    step = pl.program_id(0)
    ctx = ids[1]
    n0 = counts[0, ids[0]]

    @pl.when(step == 0)
    def _():
        if own:
            plan(ids, holder, prior, counts, mark_out, table, seen)
        even, odd, rope = align(nl_ref[...])
        rope = both_ropes(rope)
        kn[...] = jnp.zeros(kn.shape, BF)
        for parity, latent in enumerate((even, odd)):
            at = slice(parity * 128, parity * 128 + 80)
            for j in range(4):
                kn[at, j * 128 : (j + 1) * 128] = latent[j]
            kn[at, 512:640] = rope[parity]

        def new_position(row):
            return ctx * TOK + 2 * (row & 127) + (row >> 7)

        kn[:, 640:768] = mark(
            256, 0, lambda r: new_position(r) < n0, lambda r: new_position(r) >= n0
        )

    for i, source in enumerate(sources):

        @pl.when(step == i)
        def _():
            part[...] = source[...]

    step = step + first
    rows = HEADS * TOK
    t0 = ((ctx + turn_of(step)) & 3) * TOK
    lane = iota((TOK, 128), 1)
    token = iota((TOK, 128), 0) + t0
    flags = jnp.where(
        ((lane == 0) & (token < n0)) | ((lane == 1) & (token >= n0)), 1.0, 0.0
    ).astype(BF)
    for j in range(HEADS):
        at = slice(j * TOK, (j + 1) * TOK)
        q_out[0, at, 0:512] = jnp.dot(
            part[:, j * 128 : (j + 1) * 128], ka_ref[j], preferred_element_type=F32
        ).astype(BF)
        rope = part[:, 512 + (j // 2) * 128 : 640 + (j // 2) * 128]
        keep = lane < 64 if j % 2 == 0 else lane >= 64
        q_out[0, at, 512:640] = jnp.where(keep, rope, jnp.zeros_like(rope))
        q_out[0, at, 640:768] = flags

    visible = t0 + TOK > ctx * TOK

    @pl.when(visible)
    def _():
        key = iota((rows, 256), 1)
        position = ctx * TOK + 2 * (key & 127) + (key >> 7)
        here = jnp.concatenate([iota((TOK, 256), 0)] * HEADS, axis=0) + t0
        seen_keys = (position <= here) & ((key & 127) < 80)
        scores = jnp.where(seen_keys, product(q_out[0], kn[...]), -BIG)
        top = jnp.maximum(
            jnp.full((rows, 128), -BIG, F32), jnp.max(scores, axis=1, keepdims=True)
        )
        weight = jnp.exp2((scores - wide(top, 256)) * (SCALE * LOG2E))
        mx_out[0] = top
        sm_out[0] = jnp.zeros((rows, 128), F32) + jnp.sum(weight, axis=1, keepdims=True)
        acc_out[0] = jnp.dot(weight.astype(BF), kn[:, 0:512], preferred_element_type=F32)

    @pl.when(jnp.logical_not(visible))
    def _():
        mx_out[0] = jnp.full((rows, 128), -BIG, F32)
        sm_out[0] = jnp.zeros((rows, 128), F32)
        acc_out[0] = jnp.zeros((rows, 512), F32)


def attend_kernel(
    ids, table,
    q_ref, acc0, mx0, sm0, va_ref, mark_ref, a0, am, ap, b0, bm, bp,
    out_ref,
    kc, kb, acc, mx, sm, sem,
):
    step = pl.program_id(0)
    core = ids[2] & 1
    end0 = table[SLOTS]
    end1 = table[SLOTS + 1]
    n0 = table[SLOTS + 2]

    @pl.when(step == 0)
    def _():
        marks = pltpu.make_async_copy(mark_ref, kb.at[:, pl.ds(640, 128)], sem.at[2])
        marks.start()
        for w, (own, first, second) in enumerate(((a0, am, ap), (b0, bm, bp))):
            pltpu.make_async_copy(own, kc.at[w, 0], sem.at[w]).start()
            pltpu.make_async_copy(first, kc.at[w, 1, pl.ds(0, 4)], sem.at[w]).start()
            pltpu.make_async_copy(second, kc.at[w, 1, pl.ds(4, 4)], sem.at[w]).start()
        for w in range(2):
            pltpu.make_async_copy(kc.at[w], kc.at[w], sem.at[w]).wait()
            slot = core if w == 0 else 1 - core

            def shape_up(p, _):
                at = table[p * 2 + slot] * BLK
                for half in range(2):
                    block = kc[w, half, p]
                    ropes = both_ropes(block[:, 1024:1152])
                    for parity in range(2):
                        to = pl.ds(pl.multiple_of(at + half * 64 + parity * 32, 32), 32)
                        kb[to, 0:512] = block[:, parity * 512 : parity * 512 + 512]
                        kb[to, 512:640] = ropes[parity]
                return 0

            lax.fori_loop(0, 8, shape_up, 0, unroll=True)
        marks.wait()

    t0 = ((ids[1] + turn_of(step)) & 3) * TOK
    low = jnp.where(t0 < n0, 0, end0)
    high = jnp.where(t0 + TOK > n0, end1, end0)
    extent = high - low

    def chunk(size):
        at = pl.ds(pl.multiple_of(jnp.minimum(low, KEYS - size), BLK), size)
        scores = product(q_ref[0], kb[at, :])
        before = mx0[0]
        top = jnp.maximum(before, jnp.max(scores, axis=1, keepdims=True))
        keep = jnp.exp2((before - top) * (SCALE * LOG2E))
        weight = jnp.exp2((scores - wide(top, size)) * (SCALE * LOG2E))
        mx[...] = top
        sm[...] = sm0[0] * keep + jnp.sum(weight, axis=1, keepdims=True)
        acc[...] = acc0[0] * wide(keep, 512) + jnp.dot(
            weight.astype(BF), kb[at, 0:512], preferred_element_type=F32
        )

    sizes = (0, 128, 512, 1024, 1536, 2048)
    for small, size in zip(sizes, sizes[1:]):

        @pl.when((extent > small) & (extent <= size))
        def _():
            chunk(size)

    @pl.when(extent <= 0)
    def _():
        acc[...], mx[...], sm[...] = acc0[0], mx0[0], sm0[0]

    lane16 = iota((16, 128), 1)
    stats = jnp.zeros((16, 128), F32)
    heads = []
    for j in range(HEADS):
        at = slice(j * TOK, (j + 1) * TOK)
        mass = sm[at, :]
        none = mass == 0.0
        safe = jnp.where(none, 1.0, mass)
        lse = jnp.where(none, -BIG, mx[at, :] * SCALE + jnp.log(safe))
        latent = (acc[at, :] * wide(1.0 / safe, 512)).astype(BF)
        heads.append(jnp.dot(latent, va_ref[j], preferred_element_type=F32).astype(BF))
        one = lse.astype(BF).astype(F32)
        two = (lse - one).astype(BF).astype(F32)
        three = lse - one - two
        for k in range(TOK // 16):
            base = 12 * k + 3 * j
            cut = slice(k * 16, (k + 1) * 16)
            for i, value in enumerate((one, two, three)):
                stats = jnp.where(lane16 == base + i, value[cut], stats)

    for j in range(HEADS):
        out_ref[0, j * TOK : (j + 1) * TOK, :] = heads[j]
    out_ref[0, HEADS * TOK : SENT, :] = stats.astype(BF)


def merge_kernel(got_ref, head_ref):
    lane_in = iota((128, 512), 0)
    lane_head = iota((128, 512), 1) // 128
    stats = jnp.concatenate([got_ref[c, HEADS * TOK : SENT, :] for c in range(4)], axis=0)
    for k in range(TOK // 16):
        pickup = ((lane_in >= 12 * k + 3 * lane_head) & (lane_in < 12 * k + 3 * lane_head + 3))
        lse = jnp.dot(stats, pickup.astype(BF), preferred_element_type=F32)
        lse = [lse[c * 16 : (c + 1) * 16] for c in range(4)]
        top = jnp.maximum(jnp.maximum(lse[0], lse[1]), jnp.maximum(lse[2], lse[3]))
        weight = [jnp.exp(v - top) for v in lse]
        total = weight[0] + weight[1] + weight[2] + weight[3]
        for j in range(HEADS):
            at = slice(j * TOK + k * 16, j * TOK + (k + 1) * 16)
            cut = slice(j * 128, (j + 1) * 128)
            mixed = sum(w[:, cut] * got_ref[c, at, :].astype(F32) for c, w in enumerate(weight))
            head_ref[k * 16 : (k + 1) * 16, cut] = (mixed / total[:, cut]).astype(BF)


def project_kernel(ids, head_ref, other_ref, w_ref, x_ref, out_ref):
    core = ids[2] & 1
    for y in range(4):
        column = pl.multiple_of((2 * y + core) * 896, 128)
        total = jnp.dot(
            head_ref[...], w_ref[:, pl.ds(column, 896)], preferred_element_type=F32
        )
        total += jnp.dot(
            other_ref[...], x_ref[:, pl.ds(column, 896)], preferred_element_type=F32
        )
        out_ref[y] = total.astype(BF)


def shift(value, axis, by, size):
    return lax.ppermute(value, axis, [(i, (i + by) % size) for i in range(size)])


def swap_core(value):
    return lax.ppermute(value, "head", [(i, i ^ 1) for i in range(8)])


def whole(*shape):
    return pl.BlockSpec(shape, lambda i, *_: (0,) * len(shape))


def pin(value):
    return pltpu.with_memory_space_constraint(value, pltpu.HBM)


def prepare(ids, hit_holder, prior, counts, queries, key_absorb, new_latent, first, before=()):
    own = first == 0
    rows = HEADS * TOK
    tile = lambda n: pl.BlockSpec((1, rows, n), lambda i, *_: (i + first, 0, 0))
    kept = [((KW, BF), 0), ((512, F32), 1), ((128, F32), 2), ((128, F32), 3)]
    out_specs = [tile(shape[0]) for shape, _ in kept]
    out_shape = [pltpu.HBM((4, rows, n), kind) for (n, kind), _ in kept]
    scratch = [pltpu.VMEM((TOK, 768), BF), pltpu.VMEM((256, KW), BF)]
    aliases = {}
    if own:
        out_specs += [whole(KEYS, 128), pl.BlockSpec(memory_space=pltpu.SMEM)]
        out_shape += [pltpu.HBM((KEYS, 128), BF), jax.ShapeDtypeStruct((32,), jnp.int32)]
        scratch += [pltpu.SMEM((8,), jnp.int32)]
    else:
        before = [pin(value) for value in before]
        aliases = {4 + len(queries) + 2 + i: i for i in range(4)}
    return pl.pallas_call(
        partial(ready_kernel, first, len(queries)),
        grid_spec=pltpu.PrefetchScalarGridSpec(
            num_scalar_prefetch=4,
            grid=(len(queries),),
            in_specs=[whole(*value.shape) for value in queries]
            + [whole(HEADS, 128, 512), whole(80, WIDE2)]
            + [pl.BlockSpec(memory_space=pltpu.HBM)] * len(before),
            out_specs=out_specs,
            scratch_shapes=scratch,
        ),
        out_shape=out_shape,
        input_output_aliases=aliases,
        compiler_params=pltpu.CompilerParams(vmem_limit_bytes=16 * 2**20),
        cost_estimate=pl.CostEstimate(
            flops=10**9 * len(queries),
            bytes_accessed=4 * 10**6 * len(queries),
            transcendentals=10**6,
        ),
        name=("prepare_own", "prepare_near", "", "prepare_far")[first],
    )(
        ids, hit_holder, prior, counts,
        *queries,
        pin(key_absorb),
        pin(new_latent),
        *before,
    )


def attend(ids, ready, pieces, value_absorb):
    q_all, acc0, mx0, sm0, marks = [pin(value) for value in ready[:5]]
    rows = HEADS * TOK
    tile = lambda n: pl.BlockSpec((1, rows, n), lambda i, *_: (i, 0, 0))
    return pl.pallas_call(
        attend_kernel,
        grid_spec=pltpu.PrefetchScalarGridSpec(
            num_scalar_prefetch=2,
            grid=(4,),
            in_specs=[tile(KW), tile(512), tile(128), tile(128), whole(HEADS, 512, 128)]
            + [pl.BlockSpec(memory_space=pl.ANY)] * 7,
            out_specs=pl.BlockSpec(
                (1, SENT, 128), lambda i, ids, _: ((ids[1] + turn_of(i)) & 3, 0, 0)
            ),
            scratch_shapes=[
                pltpu.VMEM((2, 2, 8, 32, WIDE2), BF),
                pltpu.VMEM((KEYS, KW), BF),
                pltpu.VMEM((rows, 512), F32),
                pltpu.VMEM((rows, 128), F32),
                pltpu.VMEM((rows, 128), F32),
                pltpu.SemaphoreType.DMA((3,)),
            ],
        ),
        out_shape=jax.ShapeDtypeStruct((4, SENT, 128), BF),
        compiler_params=pltpu.CompilerParams(vmem_limit_bytes=27 * 2**20),
        cost_estimate=pl.CostEstimate(
            flops=12 * 10**9, bytes_accessed=15 * 10**6, transcendentals=5 * 10**6
        ),
        name="attend",
    )(
        ids, ready[5], q_all, acc0, mx0, sm0, pin(value_absorb), marks,
        *pieces,
    )


def local(
    query_nope, query_rope, new_latent, cache_pool, hit_holder, hit_block,
    prior_blocks, new_counts, key_absorb, value_absorb, out_weight,
):
    ids = jnp.stack(
        [lax.axis_index("pool"), lax.axis_index("ctx"), lax.axis_index("head")]
    ).astype(jnp.int32)

    prior = prior_blocks.T
    counts = new_counts.T
    picked, queries = pl.pallas_call(
        pick_kernel,
        grid_spec=pltpu.PrefetchScalarGridSpec(
            num_scalar_prefetch=2,
            grid=(1,),
            in_specs=[
                pl.BlockSpec(memory_space=pl.ANY),
                whole(8, 64),
                whole(8, 64),
                whole(TOK, 512),
                whole(TOK, 256),
            ],
            out_specs=[whole(8, 32, WIDE2), whole(TOK, 768)],
            scratch_shapes=[
                pltpu.VMEM((2, 16, 16 * WIDE2), BF),
                pltpu.SemaphoreType.DMA((2,)),
            ],
        ),
        out_shape=[
            jax.ShapeDtypeStruct((8, 32, WIDE2), BF),
            jax.ShapeDtypeStruct((TOK, 768), BF),
        ],
        name="pick_blocks",
    )(ids, prior, pin(cache_pool), hit_holder, hit_block, query_nope, query_rope)

    qm = shift(queries, "ctx", 1, 4)
    qp = shift(queries, "ctx", -1, 4)
    late_queries, qm, qp = lax.optimization_barrier((queries, qm, qp))
    q2 = shift(late_queries, "ctx", 2, 4)
    a0 = lax.all_to_all(picked, "pool", split_axis=0, concat_axis=0, tiled=True)

    ready = partial(prepare, ids, hit_holder, prior, counts)
    state = ready((pin(queries),), key_absorb, new_latent, 0)
    state, marks, table = state[:4], state[4], state[5]
    state = ready((qm, qp), key_absorb, new_latent, 1, state)
    near, a0 = lax.optimization_barrier((state[0], a0))
    am = shift(a0[:4], "head", 2, 8)
    ap = shift(a0[4:], "head", -2, 8)
    b0 = swap_core(a0)
    state = ready((q2,), key_absorb, new_latent, 3, (near, *state[1:]))
    far, am, ap = lax.optimization_barrier((state[0], am, ap))
    bm = swap_core(am)
    bp = swap_core(ap)
    b0, bm, bp, late_weight = lax.optimization_barrier((b0, bm, bp, out_weight))
    other_weight = swap_core(late_weight)
    partial_out = attend(
        ids,
        (far, *state[1:], marks, table),
        (a0, am, ap, b0, bm, bp),
        value_absorb,
    )
    got = lax.all_to_all(partial_out, "ctx", split_axis=0, concat_axis=0, tiled=True)

    heads = pl.pallas_call(
        merge_kernel,
        out_shape=jax.ShapeDtypeStruct((TOK, 512), BF),
        compiler_params=pltpu.CompilerParams(vmem_limit_bytes=8 * 2**20),
        name="merge",
    )(got)
    other_heads = swap_core(heads)
    vmem = pl.BlockSpec(memory_space=pltpu.VMEM)
    shares = pl.pallas_call(
        project_kernel,
        grid_spec=pltpu.PrefetchScalarGridSpec(
            num_scalar_prefetch=1,
            in_specs=[vmem] * 4,
            out_specs=vmem,
        ),
        out_shape=jax.ShapeDtypeStruct((4, TOK, 896), BF),
        compiler_params=pltpu.CompilerParams(vmem_limit_bytes=20 * 2**20),
        name="project",
    )(ids, heads, other_heads, out_weight, other_weight)
    shares = lax.all_to_all(
        shares, "head", split_axis=0, concat_axis=0, tiled=True,
        axis_index_groups=[[0, 2, 4, 6], [1, 3, 5, 7]],
    )
    return jnp.sum(shares.astype(F32), axis=0).astype(BF)


def solution(mesh):
    return jax.shard_map(
        local,
        mesh=mesh,
        in_specs=(
            P(("pool", "ctx"), "head"),
            P(("pool", "ctx"), "head"),
            P(("pool", "ctx"), None),
            P(("pool", "ctx"), None),
            P(),
            P(),
            P(),
            P(),
            P("head", None, None),
            P("head", None, None),
            P("head", None),
        ),
        out_specs=P(("pool", "ctx"), "head"),
        check_vma=False,
    )
```

```python
from functools import partial

import jax
import jax.numpy as jnp
from jax import lax
from jax.experimental import pallas as pl
from jax.experimental.pallas import tpu as pltpu
from jax.sharding import PartitionSpec as P

KV_RANK = 512
ROPE = 64
QK_NOPE = 128
VD = 128
BLK = 128
PAIRS = BLK // 2
WIDE2 = 2 * (KV_RANK + ROPE)
HEADS = 4
TOK = 160
SLOTS = 16
KEYS = SLOTS * BLK
KW = 768
BIG = 2.0**100
SCALE = (QK_NOPE + ROPE) ** (-0.5)
LOG2E = 1.4426950408889634
BF = jnp.bfloat16
F32 = jnp.float32
STAT = 16
SENT = HEADS * TOK + STAT


def iota(shape, dim):
    return lax.broadcasted_iota(jnp.int32, shape, dim)


def pick_kernel(
    ids, prior, cache_ref, holder_ref, block_ref, nope_ref, rope_ref, out_ref, query_ref, onehot_ref
):
    @pl.when(pl.program_id(0) == 0)
    def _():
        query_ref[:, 0:512] = nope_ref[...]
        query_ref[:, 512:768] = rope_ref[...]
        onehot_ref[...] = choose(ids, prior, holder_ref, block_ref)

    stacked = jnp.concatenate(
        [cache_ref[:, p * WIDE2 : (p + 1) * WIDE2] for p in range(16)], axis=0
    )
    out = jnp.dot(onehot_ref[...], stacked, preferred_element_type=F32).astype(BF)
    even, odd, rope = align(out)
    for g in range(8):
        at = slice(g * 16, (g + 1) * 16)
        for j in range(4):
            out_ref[g, :, j * 128 : (j + 1) * 128] = even[j][at]
            out_ref[g, :, 512 + j * 128 : 640 + j * 128] = odd[j][at]
        out_ref[g, :, 1024:1152] = rope[at]


def choose(ids, prior, holder_ref, block_ref):
    me = ids[0] * 4 + ids[1]
    core = ids[2] & 1
    lane = iota((8, 64), 1)
    group = iota((8, 64), 0)
    count = jnp.zeros((8, 64), jnp.int32)
    for g in range(8):
        count = jnp.where(group == g, prior[0, g] + prior[1, g], count)
    match = (holder_ref[...] == me) & (lane < count)
    first = jnp.min(jnp.where(match, lane, 1000), axis=1, keepdims=True)
    last = jnp.max(jnp.where(match, lane, -1), axis=1, keepdims=True)
    wanted = jnp.where(core == 0, first, jnp.where(last > first, last, -2))
    chosen = match & (lane == wanted)
    index = jnp.sum(jnp.where(chosen, block_ref[...] + 1, 0), axis=1, keepdims=True) - 1
    spread = (iota((128, 8), 0) // 16 == iota((128, 8), 1)).astype(BF)
    rows_index = jnp.dot(
        spread,
        jnp.broadcast_to(index.astype(F32), (8, 256)).astype(BF),
        preferred_element_type=F32,
    )
    row = iota((128, 256), 0)
    col = iota((128, 256), 1)
    return ((col // 16 == row % 16) & ((col % 16).astype(F32) == rows_index)).astype(BF)


def align(rows):
    low = iota((rows.shape[0], 128), 1) < 64
    tile = [rows[:, j * 128 : (j + 1) * 128] for j in range(9)]
    flip = {j: pltpu.roll(tile[j].astype(F32), 64, 1).astype(BF) for j in range(5, 9)}
    flip[4] = pltpu.roll(tile[4].astype(F32), 64, 1).astype(BF)
    odd = [jnp.where(low, flip[4 + j], flip[5 + j]) for j in range(4)]
    return tile[:4], odd, jnp.where(low, tile[4], tile[8])


def both_ropes(tile):
    low = iota(tile.shape, 1) < 64
    flip = pltpu.roll(tile.astype(F32), 64, 1).astype(BF)
    return jnp.where(low, tile, flip), jnp.where(low, flip, tile)


def wide(value, n):
    return jnp.concatenate([value] * (n // 128), axis=1)


def turn_of(step):
    return jnp.where(step == 0, 0, jnp.where(step == 1, 1, jnp.where(step == 2, 3, 2)))


def product(queries, keys):
    return lax.dot_general(
        queries, keys, (((1,), (1,)), ((), ())), preferred_element_type=F32
    )


def mark(n, base, keys0, keys1):
    row = iota((n, 128), 0) + base
    lane = iota((n, 128), 1)
    miss0 = (lane == 0) & jnp.logical_not(keys0(row))
    miss1 = (lane == 1) & jnp.logical_not(keys1(row))
    return jnp.where(miss0 | miss1, -BIG, 0.0).astype(BF)


def plan(ids, holder, prior, counts, mark_out, table, seen):
    group = ids[0]
    for i in range(SLOTS):
        table[i] = -1
    for i in range(8):
        seen[i] = 0
    own = prior[0, group]
    total = own + prior[1, group]

    def entry(e, carry):
        filled, mine = carry
        where = holder[group, e]
        hit = (where & 3) == ids[1]
        p = where >> 2

        @pl.when(hit)
        def _():
            s = seen[p]
            seen[p] = s + 1
            table[p * 2 + s] = filled

        add = hit.astype(jnp.int32)
        return filled + add, mine + jnp.where(e < own, add, 0)

    filled, mine = lax.fori_loop(0, total, entry, (jnp.int32(0), jnp.int32(0)))
    end0 = mine * BLK
    end1 = filled * BLK
    table[SLOTS] = end0
    table[SLOTS + 1] = end1
    table[SLOTS + 2] = counts[0, group]
    for i in range(SLOTS + 3, 32):
        table[i] = 0
    for i in range(SLOTS):
        dead = table[i] < 0

        @pl.when(dead)
        def _():
            table[i] = filled

        filled = filled + dead.astype(jnp.int32)

    def marks(i, _):
        at = pl.multiple_of(i * BLK, BLK)
        mark_out[pl.ds(at, BLK), :] = mark(
            BLK, at, lambda r: r < end0, lambda r: (r >= end0) & (r < end1)
        )
        return 0

    lax.fori_loop(0, SLOTS, marks, 0)


def ready_kernel(first, count, ids, holder, prior, counts, *refs):
    own = first == 0
    sources, refs = refs[:count], refs[count:]
    ka_ref, nl_ref = refs[:2]
    if own:
        q_out, acc_out, mx_out, sm_out, mark_out, table, part, kn, seen = refs[2:]
    else:
        q_out, acc_out, mx_out, sm_out, part, kn = refs[6:]
    step = pl.program_id(0)
    ctx = ids[1]
    n0 = counts[0, ids[0]]

    @pl.when(step == 0)
    def _():
        if own:
            plan(ids, holder, prior, counts, mark_out, table, seen)
        even, odd, rope = align(nl_ref[...])
        rope = both_ropes(rope)
        kn[...] = jnp.zeros(kn.shape, BF)
        for parity, latent in enumerate((even, odd)):
            at = slice(parity * 128, parity * 128 + 80)
            for j in range(4):
                kn[at, j * 128 : (j + 1) * 128] = latent[j]
            kn[at, 512:640] = rope[parity]

        def new_position(row):
            return ctx * TOK + 2 * (row & 127) + (row >> 7)

        kn[:, 640:768] = mark(
            256, 0, lambda r: new_position(r) < n0, lambda r: new_position(r) >= n0
        )

    for i, source in enumerate(sources):

        @pl.when(step == i)
        def _():
            part[...] = source[...]

    step = step + first
    rows = HEADS * TOK
    t0 = ((ctx + turn_of(step)) & 3) * TOK
    lane = iota((TOK, 128), 1)
    token = iota((TOK, 128), 0) + t0
    flags = jnp.where(
        ((lane == 0) & (token < n0)) | ((lane == 1) & (token >= n0)), 1.0, 0.0
    ).astype(BF)
    for j in range(HEADS):
        at = slice(j * TOK, (j + 1) * TOK)
        q_out[0, at, 0:512] = jnp.dot(
            part[:, j * 128 : (j + 1) * 128], ka_ref[j], preferred_element_type=F32
        ).astype(BF)
        rope = part[:, 512 + (j // 2) * 128 : 640 + (j // 2) * 128]
        keep = lane < 64 if j % 2 == 0 else lane >= 64
        q_out[0, at, 512:640] = jnp.where(keep, rope, jnp.zeros_like(rope))
        q_out[0, at, 640:768] = flags

    visible = t0 + TOK > ctx * TOK

    @pl.when(visible)
    def _():
        key = iota((rows, 256), 1)
        position = ctx * TOK + 2 * (key & 127) + (key >> 7)
        here = jnp.concatenate([iota((TOK, 256), 0)] * HEADS, axis=0) + t0
        seen_keys = (position <= here) & ((key & 127) < 80)
        scores = jnp.where(seen_keys, product(q_out[0], kn[...]), -BIG)
        top = jnp.maximum(
            jnp.full((rows, 128), -BIG, F32), jnp.max(scores, axis=1, keepdims=True)
        )
        weight = jnp.exp2((scores - wide(top, 256)) * (SCALE * LOG2E))
        mx_out[0] = top
        sm_out[0] = jnp.zeros((rows, 128), F32) + jnp.sum(weight, axis=1, keepdims=True)
        acc_out[0] = jnp.dot(weight.astype(BF), kn[:, 0:512], preferred_element_type=F32)

    @pl.when(jnp.logical_not(visible))
    def _():
        mx_out[0] = jnp.full((rows, 128), -BIG, F32)
        sm_out[0] = jnp.zeros((rows, 128), F32)
        acc_out[0] = jnp.zeros((rows, 512), F32)


def attend_kernel(
    ids, table,
    q_ref, acc0, mx0, sm0, va_ref, mark_ref, a0, am, ap, b0, bm, bp,
    out_ref,
    kc, kb, acc, mx, sm, sem,
):
    step = pl.program_id(0)
    core = ids[2] & 1
    end0 = table[SLOTS]
    end1 = table[SLOTS + 1]
    n0 = table[SLOTS + 2]

    @pl.when(step == 0)
    def _():
        marks = pltpu.make_async_copy(mark_ref, kb.at[:, pl.ds(640, 128)], sem.at[2])
        marks.start()
        for w, (own, first, second) in enumerate(((a0, am, ap), (b0, bm, bp))):
            pltpu.make_async_copy(own, kc.at[w, 0], sem.at[w]).start()
            pltpu.make_async_copy(first, kc.at[w, 1, pl.ds(0, 4)], sem.at[w]).start()
            pltpu.make_async_copy(second, kc.at[w, 1, pl.ds(4, 4)], sem.at[w]).start()
        for w in range(2):
            pltpu.make_async_copy(kc.at[w], kc.at[w], sem.at[w]).wait()
            slot = core if w == 0 else 1 - core

            def shape_up(p, _):
                at = table[p * 2 + slot] * BLK
                for half in range(2):
                    block = kc[w, half, p]
                    ropes = both_ropes(block[:, 1024:1152])
                    for parity in range(2):
                        to = pl.ds(pl.multiple_of(at + half * 64 + parity * 32, 32), 32)
                        kb[to, 0:512] = block[:, parity * 512 : parity * 512 + 512]
                        kb[to, 512:640] = ropes[parity]
                return 0

            lax.fori_loop(0, 8, shape_up, 0, unroll=True)
        marks.wait()

    t0 = ((ids[1] + turn_of(step)) & 3) * TOK
    low = jnp.where(t0 < n0, 0, end0)
    high = jnp.where(t0 + TOK > n0, end1, end0)
    extent = high - low

    def chunk(size):
        at = pl.ds(pl.multiple_of(jnp.minimum(low, KEYS - size), BLK), size)
        scores = product(q_ref[0], kb[at, :])
        before = mx0[0]
        top = jnp.maximum(before, jnp.max(scores, axis=1, keepdims=True))
        keep = jnp.exp2((before - top) * (SCALE * LOG2E))
        weight = jnp.exp2((scores - wide(top, size)) * (SCALE * LOG2E))
        mx[...] = top
        sm[...] = sm0[0] * keep + jnp.sum(weight, axis=1, keepdims=True)
        acc[...] = acc0[0] * wide(keep, 512) + jnp.dot(
            weight.astype(BF), kb[at, 0:512], preferred_element_type=F32
        )

    sizes = (0, 128, 512, 1024, 1536, 2048)
    for small, size in zip(sizes, sizes[1:]):

        @pl.when((extent > small) & (extent <= size))
        def _():
            chunk(size)

    @pl.when(extent <= 0)
    def _():
        acc[...], mx[...], sm[...] = acc0[0], mx0[0], sm0[0]

    lane16 = iota((16, 128), 1)
    stats = jnp.zeros((16, 128), F32)
    heads = []
    for j in range(HEADS):
        at = slice(j * TOK, (j + 1) * TOK)
        mass = sm[at, :]
        none = mass == 0.0
        safe = jnp.where(none, 1.0, mass)
        lse = jnp.where(none, -BIG, mx[at, :] * SCALE + jnp.log(safe))
        latent = (acc[at, :] * wide(1.0 / safe, 512)).astype(BF)
        heads.append(jnp.dot(latent, va_ref[j], preferred_element_type=F32).astype(BF))
        one = lse.astype(BF).astype(F32)
        two = (lse - one).astype(BF).astype(F32)
        three = lse - one - two
        for k in range(TOK // 16):
            base = 12 * k + 3 * j
            cut = slice(k * 16, (k + 1) * 16)
            for i, value in enumerate((one, two, three)):
                stats = jnp.where(lane16 == base + i, value[cut], stats)

    for j in range(HEADS):
        out_ref[0, j * TOK : (j + 1) * TOK, :] = heads[j]
    out_ref[0, HEADS * TOK : SENT, :] = stats.astype(BF)


def merge_kernel(got_ref, head_ref):
    lane_in = iota((128, 512), 0)
    lane_head = iota((128, 512), 1) // 128
    stats = jnp.concatenate([got_ref[c, HEADS * TOK : SENT, :] for c in range(4)], axis=0)
    for k in range(TOK // 16):
        pickup = ((lane_in >= 12 * k + 3 * lane_head) & (lane_in < 12 * k + 3 * lane_head + 3))
        lse = jnp.dot(stats, pickup.astype(BF), preferred_element_type=F32)
        lse = [lse[c * 16 : (c + 1) * 16] for c in range(4)]
        top = jnp.maximum(jnp.maximum(lse[0], lse[1]), jnp.maximum(lse[2], lse[3]))
        weight = [jnp.exp(v - top) for v in lse]
        total = weight[0] + weight[1] + weight[2] + weight[3]
        for j in range(HEADS):
            at = slice(j * TOK + k * 16, j * TOK + (k + 1) * 16)
            cut = slice(j * 128, (j + 1) * 128)
            mixed = sum(w[:, cut] * got_ref[c, at, :].astype(F32) for c, w in enumerate(weight))
            head_ref[k * 16 : (k + 1) * 16, cut] = (mixed / total[:, cut]).astype(BF)


def project_kernel(ids, head_ref, other_ref, w_ref, x_ref, out_ref):
    core = ids[2] & 1
    for y in range(4):
        column = pl.multiple_of((2 * y + core) * 896, 128)
        total = jnp.dot(
            head_ref[...], w_ref[:, pl.ds(column, 896)], preferred_element_type=F32
        )
        total += jnp.dot(
            other_ref[...], x_ref[:, pl.ds(column, 896)], preferred_element_type=F32
        )
        out_ref[y] = total.astype(BF)


def shift(value, axis, by, size):
    return lax.ppermute(value, axis, [(i, (i + by) % size) for i in range(size)])


def swap_core(value):
    return lax.ppermute(value, "head", [(i, i ^ 1) for i in range(8)])


def whole(*shape):
    return pl.BlockSpec(shape, lambda i, *_: (0,) * len(shape))


def pin(value):
    return pltpu.with_memory_space_constraint(value, pltpu.HBM)


def prepare(ids, hit_holder, prior, counts, queries, key_absorb, new_latent, first, before=()):
    own = first == 0
    rows = HEADS * TOK
    tile = lambda n: pl.BlockSpec((1, rows, n), lambda i, *_: (i + first, 0, 0))
    kept = [((KW, BF), 0), ((512, F32), 1), ((128, F32), 2), ((128, F32), 3)]
    out_specs = [tile(shape[0]) for shape, _ in kept]
    out_shape = [pltpu.HBM((4, rows, n), kind) for (n, kind), _ in kept]
    scratch = [pltpu.VMEM((TOK, 768), BF), pltpu.VMEM((256, KW), BF)]
    aliases = {}
    if own:
        out_specs += [whole(KEYS, 128), pl.BlockSpec(memory_space=pltpu.SMEM)]
        out_shape += [pltpu.HBM((KEYS, 128), BF), jax.ShapeDtypeStruct((32,), jnp.int32)]
        scratch += [pltpu.SMEM((8,), jnp.int32)]
    else:
        before = [pin(value) for value in before]
        aliases = {4 + len(queries) + 2 + i: i for i in range(4)}
    return pl.pallas_call(
        partial(ready_kernel, first, len(queries)),
        grid_spec=pltpu.PrefetchScalarGridSpec(
            num_scalar_prefetch=4,
            grid=(len(queries),),
            in_specs=[whole(*value.shape) for value in queries]
            + [whole(HEADS, 128, 512), whole(80, WIDE2)]
            + [pl.BlockSpec(memory_space=pltpu.HBM)] * len(before),
            out_specs=out_specs,
            scratch_shapes=scratch,
        ),
        out_shape=out_shape,
        input_output_aliases=aliases,
        compiler_params=pltpu.CompilerParams(vmem_limit_bytes=16 * 2**20),
        cost_estimate=pl.CostEstimate(
            flops=10**9 * len(queries),
            bytes_accessed=4 * 10**6 * len(queries),
            transcendentals=10**6,
        ),
        name=("prepare_own", "prepare_near", "prepare_far")[first],
    )(
        ids, hit_holder, prior, counts,
        *queries,
        pin(key_absorb),
        pin(new_latent),
        *before,
    )


def attend(ids, ready, pieces, value_absorb):
    q_all, acc0, mx0, sm0, marks = [pin(value) for value in ready[:5]]
    rows = HEADS * TOK
    tile = lambda n: pl.BlockSpec((1, rows, n), lambda i, *_: (i, 0, 0))
    return pl.pallas_call(
        attend_kernel,
        grid_spec=pltpu.PrefetchScalarGridSpec(
            num_scalar_prefetch=2,
            grid=(4,),
            in_specs=[tile(KW), tile(512), tile(128), tile(128), whole(HEADS, 512, 128)]
            + [pl.BlockSpec(memory_space=pl.ANY)] * 7,
            out_specs=pl.BlockSpec(
                (1, SENT, 128), lambda i, ids, _: ((ids[1] + turn_of(i)) & 3, 0, 0)
            ),
            scratch_shapes=[
                pltpu.VMEM((2, 2, 8, 32, WIDE2), BF),
                pltpu.VMEM((KEYS, KW), BF),
                pltpu.VMEM((rows, 512), F32),
                pltpu.VMEM((rows, 128), F32),
                pltpu.VMEM((rows, 128), F32),
                pltpu.SemaphoreType.DMA((3,)),
            ],
        ),
        out_shape=jax.ShapeDtypeStruct((4, SENT, 128), BF),
        compiler_params=pltpu.CompilerParams(vmem_limit_bytes=27 * 2**20),
        cost_estimate=pl.CostEstimate(
            flops=12 * 10**9, bytes_accessed=15 * 10**6, transcendentals=5 * 10**6
        ),
        name="attend",
    )(
        ids, ready[5], q_all, acc0, mx0, sm0, pin(value_absorb), marks,
        *pieces,
    )


def local(
    query_nope, query_rope, new_latent, cache_pool, hit_holder, hit_block,
    prior_blocks, new_counts, key_absorb, value_absorb, out_weight,
):
    ids = jnp.stack(
        [lax.axis_index("pool"), lax.axis_index("ctx"), lax.axis_index("head")]
    ).astype(jnp.int32)

    prior = prior_blocks.T
    counts = new_counts.T
    picked, queries = pl.pallas_call(
        pick_kernel,
        grid_spec=pltpu.PrefetchScalarGridSpec(
            num_scalar_prefetch=2,
            grid=(2,),
            in_specs=[
                pl.BlockSpec((16, 16 * WIDE2), lambda i, ids, _: (0, (ids[2] & 2) + i)),
                whole(8, 64),
                whole(8, 64),
                whole(TOK, 512),
                whole(TOK, 256),
            ],
            out_specs=[
                pl.BlockSpec((8, 16, WIDE2), lambda i, *_: (0, i, 0)),
                whole(TOK, 768),
            ],
            scratch_shapes=[pltpu.VMEM((128, 256), BF)],
        ),
        out_shape=[
            jax.ShapeDtypeStruct((8, 32, WIDE2), BF),
            jax.ShapeDtypeStruct((TOK, 768), BF),
        ],
        name="pick_blocks",
    )(ids, prior, cache_pool, hit_holder, hit_block, query_nope, query_rope)

    qm = shift(queries, "ctx", 1, 4)
    qp = shift(queries, "ctx", -1, 4)
    late_queries, qp = lax.optimization_barrier((queries, qp))
    q2 = shift(late_queries, "ctx", 2, 4)
    a0 = lax.all_to_all(picked, "pool", split_axis=0, concat_axis=0, tiled=True)

    ready = partial(prepare, ids, hit_holder, prior, counts)
    state = ready((pin(queries),), key_absorb, new_latent, 0)
    state, marks, table = state[:4], state[4], state[5]
    state = ready((qp,), key_absorb, new_latent, 1, state)
    near, a0 = lax.optimization_barrier((state[0], a0))
    am = shift(a0[:4], "head", 2, 8)
    ap = shift(a0[4:], "head", -2, 8)
    b0 = swap_core(a0)
    state = ready((qm, q2), key_absorb, new_latent, 2, (near, *state[1:]))
    far, am, ap = lax.optimization_barrier((state[0], am, ap))
    bm = swap_core(am)
    bp = swap_core(ap)
    b0, bm, bp, late_weight = lax.optimization_barrier((b0, bm, bp, out_weight))
    other_weight = swap_core(late_weight)
    partial_out = attend(
        ids,
        (far, *state[1:], marks, table),
        (a0, am, ap, b0, bm, bp),
        value_absorb,
    )
    got = lax.all_to_all(partial_out, "ctx", split_axis=0, concat_axis=0, tiled=True)

    heads = pl.pallas_call(
        merge_kernel,
        out_shape=jax.ShapeDtypeStruct((TOK, 512), BF),
        compiler_params=pltpu.CompilerParams(vmem_limit_bytes=8 * 2**20),
        name="merge",
    )(got)
    other_heads = swap_core(heads)
    vmem = pl.BlockSpec(memory_space=pltpu.VMEM)
    shares = pl.pallas_call(
        project_kernel,
        grid_spec=pltpu.PrefetchScalarGridSpec(
            num_scalar_prefetch=1,
            in_specs=[vmem] * 4,
            out_specs=vmem,
        ),
        out_shape=jax.ShapeDtypeStruct((4, TOK, 896), BF),
        compiler_params=pltpu.CompilerParams(vmem_limit_bytes=20 * 2**20),
        name="project",
    )(ids, heads, other_heads, out_weight, other_weight)
    shares = lax.all_to_all(
        shares, "head", split_axis=0, concat_axis=0, tiled=True,
        axis_index_groups=[[0, 2, 4, 6], [1, 3, 5, 7]],
    )
    return jnp.sum(shares.astype(F32), axis=0).astype(BF)


def solution(mesh):
    return jax.shard_map(
        local,
        mesh=mesh,
        in_specs=(
            P(("pool", "ctx"), "head"),
            P(("pool", "ctx"), "head"),
            P(("pool", "ctx"), None),
            P(("pool", "ctx"), None),
            P(),
            P(),
            P(),
            P(),
            P("head", None, None),
            P("head", None, None),
            P("head", None),
        ),
        out_specs=P(("pool", "ctx"), "head"),
        check_vma=False,
    )
```

```python
from functools import partial

import jax
import jax.numpy as jnp
from jax import lax
from jax.experimental import pallas as pl
from jax.experimental.pallas import tpu as pltpu
from jax.sharding import PartitionSpec as P

KV_RANK = 512
ROPE = 64
QK_NOPE = 128
VD = 128
BLK = 128
PAIRS = BLK // 2
WIDE2 = 2 * (KV_RANK + ROPE)
HEADS = 4
TOK = 160
SLOTS = 16
KEYS = SLOTS * BLK
KW = 768
BIG = 2.0**100
SCALE = (QK_NOPE + ROPE) ** (-0.5)
LOG2E = 1.4426950408889634
BF = jnp.bfloat16
F32 = jnp.float32
STAT = 16
SENT = HEADS * TOK + STAT


def iota(shape, dim):
    return lax.broadcasted_iota(jnp.int32, shape, dim)


def pick_kernel(
    ids, prior, cache_ref, holder_ref, block_ref, nope_ref, rope_ref, out_ref, query_ref, onehot_ref
):
    @pl.when(pl.program_id(0) == 0)
    def _():
        query_ref[:, 0:512] = nope_ref[...]
        query_ref[:, 512:768] = rope_ref[...]
        onehot_ref[...] = choose(ids, prior, holder_ref, block_ref)

    stacked = jnp.concatenate(
        [cache_ref[:, p * WIDE2 : (p + 1) * WIDE2] for p in range(16)], axis=0
    )
    out = jnp.dot(onehot_ref[...], stacked, preferred_element_type=F32).astype(BF)
    even, odd, rope = align(out)
    for g in range(8):
        at = slice(g * 16, (g + 1) * 16)
        for j in range(4):
            out_ref[g, :, j * 128 : (j + 1) * 128] = even[j][at]
            out_ref[g, :, 512 + j * 128 : 640 + j * 128] = odd[j][at]
        out_ref[g, :, 1024:1152] = rope[at]


def choose(ids, prior, holder_ref, block_ref):
    me = ids[0] * 4 + ids[1]
    core = ids[2] & 1
    lane = iota((8, 64), 1)
    group = iota((8, 64), 0)
    count = jnp.zeros((8, 64), jnp.int32)
    for g in range(8):
        count = jnp.where(group == g, prior[0, g] + prior[1, g], count)
    match = (holder_ref[...] == me) & (lane < count)
    first = jnp.min(jnp.where(match, lane, 1000), axis=1, keepdims=True)
    last = jnp.max(jnp.where(match, lane, -1), axis=1, keepdims=True)
    wanted = jnp.where(core == 0, first, jnp.where(last > first, last, -2))
    chosen = match & (lane == wanted)
    index = jnp.sum(jnp.where(chosen, block_ref[...] + 1, 0), axis=1, keepdims=True) - 1
    spread = (iota((128, 8), 0) // 16 == iota((128, 8), 1)).astype(BF)
    rows_index = jnp.dot(
        spread,
        jnp.broadcast_to(index.astype(F32), (8, 256)).astype(BF),
        preferred_element_type=F32,
    )
    row = iota((128, 256), 0)
    col = iota((128, 256), 1)
    return ((col // 16 == row % 16) & ((col % 16).astype(F32) == rows_index)).astype(BF)


def align(rows):
    low = iota((rows.shape[0], 128), 1) < 64
    tile = [rows[:, j * 128 : (j + 1) * 128] for j in range(9)]
    flip = {j: pltpu.roll(tile[j].astype(F32), 64, 1).astype(BF) for j in range(5, 9)}
    flip[4] = pltpu.roll(tile[4].astype(F32), 64, 1).astype(BF)
    odd = [jnp.where(low, flip[4 + j], flip[5 + j]) for j in range(4)]
    return tile[:4], odd, jnp.where(low, tile[4], tile[8])


def both_ropes(tile):
    low = iota(tile.shape, 1) < 64
    flip = pltpu.roll(tile.astype(F32), 64, 1).astype(BF)
    return jnp.where(low, tile, flip), jnp.where(low, flip, tile)


def wide(value, n):
    return jnp.concatenate([value] * (n // 128), axis=1)


def turn_of(step):
    return jnp.where(step == 0, 0, jnp.where(step == 1, 1, jnp.where(step == 2, 3, 2)))


def product(queries, keys):
    return lax.dot_general(
        queries, keys, (((1,), (1,)), ((), ())), preferred_element_type=F32
    )


def mark(n, base, keys0, keys1):
    row = iota((n, 128), 0) + base
    lane = iota((n, 128), 1)
    miss0 = (lane == 0) & jnp.logical_not(keys0(row))
    miss1 = (lane == 1) & jnp.logical_not(keys1(row))
    return jnp.where(miss0 | miss1, -BIG, 0.0).astype(BF)


def plan(ids, holder, prior, counts, mark_out, table, seen):
    group = ids[0]
    for i in range(SLOTS):
        table[i] = -1
    for i in range(8):
        seen[i] = 0
    own = prior[0, group]
    total = own + prior[1, group]

    def entry(e, carry):
        filled, mine = carry
        where = holder[group, e]
        hit = (where & 3) == ids[1]
        p = where >> 2

        @pl.when(hit)
        def _():
            s = seen[p]
            seen[p] = s + 1
            table[p * 2 + s] = filled

        add = hit.astype(jnp.int32)
        return filled + add, mine + jnp.where(e < own, add, 0)

    filled, mine = lax.fori_loop(0, total, entry, (jnp.int32(0), jnp.int32(0)))
    end0 = mine * BLK
    end1 = filled * BLK
    table[SLOTS] = end0
    table[SLOTS + 1] = end1
    table[SLOTS + 2] = counts[0, group]
    for i in range(SLOTS + 3, 32):
        table[i] = 0
    for i in range(SLOTS):
        dead = table[i] < 0

        @pl.when(dead)
        def _():
            table[i] = filled

        filled = filled + dead.astype(jnp.int32)

    def marks(i, _):
        at = pl.multiple_of(i * BLK, BLK)
        mark_out[pl.ds(at, BLK), :] = mark(
            BLK, at, lambda r: r < end0, lambda r: (r >= end0) & (r < end1)
        )
        return 0

    lax.fori_loop(0, SLOTS, marks, 0)


def ready_kernel(first, count, ids, holder, prior, counts, *refs):
    own = first == 0
    sources, refs = refs[:count], refs[count:]
    ka_ref, nl_ref = refs[:2]
    if own:
        q_out, acc_out, mx_out, sm_out, mark_out, table, part, kn, seen = refs[2:]
    else:
        q_out, acc_out, mx_out, sm_out, part, kn = refs[6:]
    step = pl.program_id(0)
    ctx = ids[1]
    n0 = counts[0, ids[0]]

    @pl.when(step == 0)
    def _():
        if own:
            plan(ids, holder, prior, counts, mark_out, table, seen)
        even, odd, rope = align(nl_ref[...])
        rope = both_ropes(rope)
        kn[...] = jnp.zeros(kn.shape, BF)
        for parity, latent in enumerate((even, odd)):
            at = slice(parity * 128, parity * 128 + 80)
            for j in range(4):
                kn[at, j * 128 : (j + 1) * 128] = latent[j]
            kn[at, 512:640] = rope[parity]

        def new_position(row):
            return ctx * TOK + 2 * (row & 127) + (row >> 7)

        kn[:, 640:768] = mark(
            256, 0, lambda r: new_position(r) < n0, lambda r: new_position(r) >= n0
        )

    for i, source in enumerate(sources):

        @pl.when(step == i)
        def _():
            part[...] = source[...]

    step = step + first
    rows = HEADS * TOK
    t0 = ((ctx + turn_of(step)) & 3) * TOK
    lane = iota((TOK, 128), 1)
    token = iota((TOK, 128), 0) + t0
    flags = jnp.where(
        ((lane == 0) & (token < n0)) | ((lane == 1) & (token >= n0)), 1.0, 0.0
    ).astype(BF)
    for j in range(HEADS):
        at = slice(j * TOK, (j + 1) * TOK)
        q_out[0, at, 0:512] = jnp.dot(
            part[:, j * 128 : (j + 1) * 128], ka_ref[j], preferred_element_type=F32
        ).astype(BF)
        rope = part[:, 512 + (j // 2) * 128 : 640 + (j // 2) * 128]
        keep = lane < 64 if j % 2 == 0 else lane >= 64
        q_out[0, at, 512:640] = jnp.where(keep, rope, jnp.zeros_like(rope))
        q_out[0, at, 640:768] = flags

    visible = t0 + TOK > ctx * TOK

    @pl.when(visible)
    def _():
        key = iota((rows, 256), 1)
        position = ctx * TOK + 2 * (key & 127) + (key >> 7)
        here = jnp.concatenate([iota((TOK, 256), 0)] * HEADS, axis=0) + t0
        seen_keys = (position <= here) & ((key & 127) < 80)
        scores = jnp.where(seen_keys, product(q_out[0], kn[...]), -BIG)
        top = jnp.maximum(
            jnp.full((rows, 128), -BIG, F32), jnp.max(scores, axis=1, keepdims=True)
        )
        weight = jnp.exp2((scores - wide(top, 256)) * (SCALE * LOG2E))
        mx_out[0] = top
        sm_out[0] = jnp.zeros((rows, 128), F32) + jnp.sum(weight, axis=1, keepdims=True)
        acc_out[0] = jnp.dot(weight.astype(BF), kn[:, 0:512], preferred_element_type=F32)

    @pl.when(jnp.logical_not(visible))
    def _():
        mx_out[0] = jnp.full((rows, 128), -BIG, F32)
        sm_out[0] = jnp.zeros((rows, 128), F32)
        acc_out[0] = jnp.zeros((rows, 512), F32)


def attend_kernel(
    ids, table,
    q_ref, acc0, mx0, sm0, va_ref, mark_ref, a0, am, ap, b0, bm, bp,
    out_ref,
    kc, kb, acc, mx, sm, sem,
):
    step = pl.program_id(0)
    core = ids[2] & 1
    end0 = table[SLOTS]
    end1 = table[SLOTS + 1]
    n0 = table[SLOTS + 2]

    @pl.when(step == 0)
    def _():
        marks = pltpu.make_async_copy(mark_ref, kb.at[:, pl.ds(640, 128)], sem.at[2])
        marks.start()
        for w, (own, first, second) in enumerate(((a0, am, ap), (b0, bm, bp))):
            pltpu.make_async_copy(own, kc.at[w, 0], sem.at[w]).start()
            pltpu.make_async_copy(first, kc.at[w, 1, pl.ds(0, 4)], sem.at[w]).start()
            pltpu.make_async_copy(second, kc.at[w, 1, pl.ds(4, 4)], sem.at[w]).start()
        for w in range(2):
            pltpu.make_async_copy(kc.at[w], kc.at[w], sem.at[w]).wait()
            slot = core if w == 0 else 1 - core

            def shape_up(p, _):
                at = table[p * 2 + slot] * BLK
                for half in range(2):
                    block = kc[w, half, p]
                    ropes = both_ropes(block[:, 1024:1152])
                    for parity in range(2):
                        to = pl.ds(pl.multiple_of(at + half * 64 + parity * 32, 32), 32)
                        kb[to, 0:512] = block[:, parity * 512 : parity * 512 + 512]
                        kb[to, 512:640] = ropes[parity]
                return 0

            lax.fori_loop(0, 8, shape_up, 0, unroll=True)
        marks.wait()

    t0 = ((ids[1] + turn_of(step)) & 3) * TOK
    low = jnp.where(t0 < n0, 0, end0)
    high = jnp.where(t0 + TOK > n0, end1, end0)
    extent = high - low

    def chunk(size):
        at = pl.ds(pl.multiple_of(jnp.minimum(low, KEYS - size), BLK), size)
        scores = product(q_ref[0], kb[at, :])
        before = mx0[0]
        top = jnp.maximum(before, jnp.max(scores, axis=1, keepdims=True))
        keep = jnp.exp2((before - top) * (SCALE * LOG2E))
        weight = jnp.exp2((scores - wide(top, size)) * (SCALE * LOG2E))
        mx[...] = top
        sm[...] = sm0[0] * keep + jnp.sum(weight, axis=1, keepdims=True)
        acc[...] = acc0[0] * wide(keep, 512) + jnp.dot(
            weight.astype(BF), kb[at, 0:512], preferred_element_type=F32
        )

    sizes = (0, 128, 512, 1024, 1536, 2048)
    for small, size in zip(sizes, sizes[1:]):

        @pl.when((extent > small) & (extent <= size))
        def _():
            chunk(size)

    @pl.when(extent <= 0)
    def _():
        acc[...], mx[...], sm[...] = acc0[0], mx0[0], sm0[0]

    lane16 = iota((16, 128), 1)
    stats = jnp.zeros((16, 128), F32)
    heads = []
    for j in range(HEADS):
        at = slice(j * TOK, (j + 1) * TOK)
        mass = sm[at, :]
        none = mass == 0.0
        safe = jnp.where(none, 1.0, mass)
        lse = jnp.where(none, -BIG, mx[at, :] * SCALE + jnp.log(safe))
        latent = (acc[at, :] * wide(1.0 / safe, 512)).astype(BF)
        heads.append(jnp.dot(latent, va_ref[j], preferred_element_type=F32).astype(BF))
        one = lse.astype(BF).astype(F32)
        two = (lse - one).astype(BF).astype(F32)
        three = lse - one - two
        for k in range(TOK // 16):
            base = 12 * k + 3 * j
            cut = slice(k * 16, (k + 1) * 16)
            for i, value in enumerate((one, two, three)):
                stats = jnp.where(lane16 == base + i, value[cut], stats)

    for j in range(HEADS):
        out_ref[0, j * TOK : (j + 1) * TOK, :] = heads[j]
    out_ref[0, HEADS * TOK : SENT, :] = stats.astype(BF)


def merge_kernel(got_ref, head_ref):
    lane_in = iota((128, 512), 0)
    lane_head = iota((128, 512), 1) // 128
    stats = jnp.concatenate([got_ref[c, HEADS * TOK : SENT, :] for c in range(4)], axis=0)
    for k in range(TOK // 16):
        pickup = ((lane_in >= 12 * k + 3 * lane_head) & (lane_in < 12 * k + 3 * lane_head + 3))
        lse = jnp.dot(stats, pickup.astype(BF), preferred_element_type=F32)
        lse = [lse[c * 16 : (c + 1) * 16] for c in range(4)]
        top = jnp.maximum(jnp.maximum(lse[0], lse[1]), jnp.maximum(lse[2], lse[3]))
        weight = [jnp.exp(v - top) for v in lse]
        total = weight[0] + weight[1] + weight[2] + weight[3]
        for j in range(HEADS):
            at = slice(j * TOK + k * 16, j * TOK + (k + 1) * 16)
            cut = slice(j * 128, (j + 1) * 128)
            mixed = sum(w[:, cut] * got_ref[c, at, :].astype(F32) for c, w in enumerate(weight))
            head_ref[k * 16 : (k + 1) * 16, cut] = (mixed / total[:, cut]).astype(BF)


def project_kernel(ids, head_ref, other_ref, w_ref, x_ref, out_ref):
    core = ids[2] & 1
    for y in range(4):
        column = pl.multiple_of((2 * y + core) * 896, 128)
        total = jnp.dot(
            head_ref[...], w_ref[:, pl.ds(column, 896)], preferred_element_type=F32
        )
        total += jnp.dot(
            other_ref[...], x_ref[:, pl.ds(column, 896)], preferred_element_type=F32
        )
        out_ref[y] = total.astype(BF)


def shift(value, axis, by, size):
    return lax.ppermute(value, axis, [(i, (i + by) % size) for i in range(size)])


def swap_core(value):
    return lax.ppermute(value, "head", [(i, i ^ 1) for i in range(8)])


def whole(*shape):
    return pl.BlockSpec(shape, lambda i, *_: (0,) * len(shape))


def pin(value):
    return pltpu.with_memory_space_constraint(value, pltpu.HBM)


def prepare(ids, hit_holder, prior, counts, queries, key_absorb, new_latent, first, before=()):
    own = first == 0
    rows = HEADS * TOK
    tile = lambda n: pl.BlockSpec((1, rows, n), lambda i, *_: (i + first, 0, 0))
    kept = [((KW, BF), 0), ((512, F32), 1), ((128, F32), 2), ((128, F32), 3)]
    out_specs = [tile(shape[0]) for shape, _ in kept]
    out_shape = [pltpu.HBM((4, rows, n), kind) for (n, kind), _ in kept]
    scratch = [pltpu.VMEM((TOK, 768), BF), pltpu.VMEM((256, KW), BF)]
    aliases = {}
    if own:
        out_specs += [whole(KEYS, 128), pl.BlockSpec(memory_space=pltpu.SMEM)]
        out_shape += [pltpu.HBM((KEYS, 128), BF), jax.ShapeDtypeStruct((32,), jnp.int32)]
        scratch += [pltpu.SMEM((8,), jnp.int32)]
    else:
        before = [pin(value) for value in before]
        aliases = {4 + len(queries) + 2 + i: i for i in range(4)}
    return pl.pallas_call(
        partial(ready_kernel, first, len(queries)),
        grid_spec=pltpu.PrefetchScalarGridSpec(
            num_scalar_prefetch=4,
            grid=(len(queries),),
            in_specs=[whole(*value.shape) for value in queries]
            + [whole(HEADS, 128, 512), whole(80, WIDE2)]
            + [pl.BlockSpec(memory_space=pltpu.HBM)] * len(before),
            out_specs=out_specs,
            scratch_shapes=scratch,
        ),
        out_shape=out_shape,
        input_output_aliases=aliases,
        compiler_params=pltpu.CompilerParams(vmem_limit_bytes=16 * 2**20),
        cost_estimate=pl.CostEstimate(
            flops=10**9 * len(queries),
            bytes_accessed=4 * 10**6 * len(queries),
            transcendentals=10**6,
        ),
        name=("prepare_own", "prepare_near", "prepare_far")[first],
    )(
        ids, hit_holder, prior, counts,
        *queries,
        pin(key_absorb),
        pin(new_latent),
        *before,
    )


def attend(ids, ready, pieces, value_absorb):
    q_all, acc0, mx0, sm0, marks = [pin(value) for value in ready[:5]]
    rows = HEADS * TOK
    tile = lambda n: pl.BlockSpec((1, rows, n), lambda i, *_: (i, 0, 0))
    return pl.pallas_call(
        attend_kernel,
        grid_spec=pltpu.PrefetchScalarGridSpec(
            num_scalar_prefetch=2,
            grid=(4,),
            in_specs=[tile(KW), tile(512), tile(128), tile(128), whole(HEADS, 512, 128)]
            + [pl.BlockSpec(memory_space=pl.ANY)] * 7,
            out_specs=pl.BlockSpec(
                (1, SENT, 128), lambda i, ids, _: ((ids[1] + turn_of(i)) & 3, 0, 0)
            ),
            scratch_shapes=[
                pltpu.VMEM((2, 2, 8, 32, WIDE2), BF),
                pltpu.VMEM((KEYS, KW), BF),
                pltpu.VMEM((rows, 512), F32),
                pltpu.VMEM((rows, 128), F32),
                pltpu.VMEM((rows, 128), F32),
                pltpu.SemaphoreType.DMA((3,)),
            ],
        ),
        out_shape=jax.ShapeDtypeStruct((4, SENT, 128), BF),
        compiler_params=pltpu.CompilerParams(vmem_limit_bytes=27 * 2**20),
        cost_estimate=pl.CostEstimate(
            flops=12 * 10**9, bytes_accessed=15 * 10**6, transcendentals=5 * 10**6
        ),
        name="attend",
    )(
        ids, ready[5], q_all, acc0, mx0, sm0, pin(value_absorb), marks,
        *pieces,
    )


def local(
    query_nope, query_rope, new_latent, cache_pool, hit_holder, hit_block,
    prior_blocks, new_counts, key_absorb, value_absorb, out_weight,
):
    ids = jnp.stack(
        [lax.axis_index("pool"), lax.axis_index("ctx"), lax.axis_index("head")]
    ).astype(jnp.int32)

    prior = prior_blocks.T
    counts = new_counts.T
    picked, queries = pl.pallas_call(
        pick_kernel,
        grid_spec=pltpu.PrefetchScalarGridSpec(
            num_scalar_prefetch=2,
            grid=(2,),
            in_specs=[
                pl.BlockSpec((16, 16 * WIDE2), lambda i, ids, _: (0, (ids[2] & 2) + i)),
                whole(8, 64),
                whole(8, 64),
                whole(TOK, 512),
                whole(TOK, 256),
            ],
            out_specs=[
                pl.BlockSpec((8, 16, WIDE2), lambda i, *_: (0, i, 0)),
                whole(TOK, 768),
            ],
            scratch_shapes=[pltpu.VMEM((128, 256), BF)],
        ),
        out_shape=[
            jax.ShapeDtypeStruct((8, 32, WIDE2), BF),
            jax.ShapeDtypeStruct((TOK, 768), BF),
        ],
        name="pick_blocks",
    )(ids, prior, cache_pool, hit_holder, hit_block, query_nope, query_rope)

    qm = shift(queries, "ctx", 1, 4)
    qp = shift(queries, "ctx", -1, 4)
    late_queries, qp = lax.optimization_barrier((queries, qp))
    q2 = shift(late_queries, "ctx", 2, 4)
    a0 = lax.all_to_all(picked, "pool", split_axis=0, concat_axis=0, tiled=True)

    ready = partial(prepare, ids, hit_holder, prior, counts)
    state = ready((pin(queries),), key_absorb, new_latent, 0)
    state, marks, table = state[:4], state[4], state[5]
    state = ready((qp,), key_absorb, new_latent, 1, state)
    near, a0 = lax.optimization_barrier((state[0], a0))
    am = shift(a0[:4], "head", 2, 8)
    ap = shift(a0[4:], "head", -2, 8)
    b0 = swap_core(a0)
    state = ready((qm, q2), key_absorb, new_latent, 2, (near, *state[1:]))
    far, ap = lax.optimization_barrier((state[0], ap))
    far, am = lax.optimization_barrier((far, am))
    bm = swap_core(am)
    bp = swap_core(ap)
    b0, bm, bp, late_weight = lax.optimization_barrier((b0, bm, bp, out_weight))
    other_weight = swap_core(late_weight)
    partial_out = attend(
        ids,
        (far, *state[1:], marks, table),
        (a0, am, ap, b0, bm, bp),
        value_absorb,
    )
    got = lax.all_to_all(partial_out, "ctx", split_axis=0, concat_axis=0, tiled=True)

    heads = pl.pallas_call(
        merge_kernel,
        out_shape=jax.ShapeDtypeStruct((TOK, 512), BF),
        compiler_params=pltpu.CompilerParams(vmem_limit_bytes=8 * 2**20),
        name="merge",
    )(got)
    other_heads = swap_core(heads)
    vmem = pl.BlockSpec(memory_space=pltpu.VMEM)
    shares = pl.pallas_call(
        project_kernel,
        grid_spec=pltpu.PrefetchScalarGridSpec(
            num_scalar_prefetch=1,
            in_specs=[vmem] * 4,
            out_specs=vmem,
        ),
        out_shape=jax.ShapeDtypeStruct((4, TOK, 896), BF),
        compiler_params=pltpu.CompilerParams(vmem_limit_bytes=20 * 2**20),
        name="project",
    )(ids, heads, other_heads, out_weight, other_weight)
    shares = lax.all_to_all(
        shares, "head", split_axis=0, concat_axis=0, tiled=True,
        axis_index_groups=[[0, 2, 4, 6], [1, 3, 5, 7]],
    )
    return jnp.sum(shares.astype(F32), axis=0).astype(BF)


def solution(mesh):
    return jax.shard_map(
        local,
        mesh=mesh,
        in_specs=(
            P(("pool", "ctx"), "head"),
            P(("pool", "ctx"), "head"),
            P(("pool", "ctx"), None),
            P(("pool", "ctx"), None),
            P(),
            P(),
            P(),
            P(),
            P("head", None, None),
            P("head", None, None),
            P("head", None),
        ),
        out_specs=P(("pool", "ctx"), "head"),
        check_vma=False,
    )
```
